128 devices in a mesh: dp: 32 (over y, z, core), tensor: 4 (over x).
Axes of the slice: x: 4, y: 4, z: 4, core: 2. Of those that a mesh axis runs over, the one named last changes fastest.
Arguments:
- tokens: bfloat16 [32768, 768], P('dp'), may hold values from -6 to 6
- lengths: int32 [32, 8], P('dp'), may hold values from 1 to 512, 1024 in all within a row
- attn_gain: float32 [768], replicated, may hold values from 0.1 to 1.9
- query_weight: bfloat16 [768, 768], P(None, 'tensor'), may hold values from -0.21875 to 0.21875
- key_weight: bfloat16 [768, 768], P(None, 'tensor'), may hold values from -0.21875 to 0.21875
- value_weight: bfloat16 [768, 768], P(None, 'tensor'), may hold values from -0.21875 to 0.21875
- output_weight: bfloat16 [768, 768], P('tensor'), may hold values from -0.875 to 0.875
- ffn_gain: float32 [768], replicated, may hold values from 0.1 to 1.9
- gate_weight: bfloat16 [768, 2048], P(None, 'tensor'), may hold values from -0.21875 to 0.21875
- up_weight: bfloat16 [768, 2048], P(None, 'tensor'), may hold values from -0.21875 to 0.21875
- down_weight: bfloat16 [2048, 768], P('tensor'), may hold values from -0.125 to 0.125
- cotangent: bfloat16 [32768, 768], P('dp'), may hold values from -6 to 6
Outputs:
- layer_out: bfloat16 [32768, 768], P('dp')
- token_grad: float32 [32768, 768], P('dp')
- attn_gain_grad: float32 [768], replicated
- query_grad: float32 [768, 768], P(None, 'tensor')
- key_grad: float32 [768, 768], P(None, 'tensor')
- value_grad: float32 [768, 768], P(None, 'tensor')
- output_grad: float32 [768, 768], P('tensor')
- ffn_gain_grad: float32 [768], replicated
- gate_grad: float32 [768, 2048], P(None, 'tensor')
- up_grad: float32 [768, 2048], P(None, 'tensor')
- down_grad: float32 [2048, 768], P('tensor')
The draws below stay inside these ranges and needn't reach their ends.
Inputs may be any that keep to these rules, and one draw needn't show every extreme that they name: Each row's 8 lengths add up to 1024; the longest segment of every row has exactly 512 blocks.
All inputs are finite; a program needn't handle non-finite values.
Results may differ from the reference program's by a relative error of at most 0.015.
Values sent between devices are 32-bit elements; how exact they have to be, the bound alone decides.
No kernel may reach another device: no remote copies, remote signals or barrier semaphores. Data moves between devices by JAX's collectives and lax.ppermute only.
A program may use at most 128 MiB of HBM per device.

```python
import math
import jax
import jax.numpy as jnp
import numpy as np
from jax import lax

D = 768
HEADS = 12
HEAD = 64
FF = 2048
L = 1024
SEGS = 8
TOKENS = 32768
N_DP = 32


def block_levels(rng, dims, split, smallest, high):
    level = 1.0
    for position, parts in split:
        heights = jax.random.uniform(jax.random.fold_in(jax.random.fold_in(rng, 6), position), (parts,), jnp.float32, smallest / len(split), high / len(split))
        level = level * jnp.repeat(jnp.exp(heights), dims[position] // parts).reshape((-1,) + (1,) * (len(dims) - 1 - position))
    return level


def profile(count, total, limit, skew):
    loads = [(1 << 20) // math.isqrt(grade ** skew) + 1 for grade in range(2, count + 1)]
    surplus, given = total - limit - (count - 1), [1] * (count - 1)
    while surplus > 0:
        candidates = [i for i in range(count - 1) if given[i] < limit]
        whole, left = sum([loads[i] for i in candidates]), surplus
        for i in candidates:
            extra = min(limit - given[i], max(1, left * loads[i] // whole), surplus)
            given[i] = given[i] + extra
            surplus = surplus - extra
    return np.array([limit] + given)


def uneven_parts(key, count, total, most, lean):
    if count == 2:
        one = jax.random.randint(key, (), max(1, total - most), min(most, total - 1) + 1)
        return jnp.stack([one, total - one])
    tallies = jnp.asarray(profile(count, total, most, lean), jnp.int32)
    pairs = (count - 1) // 2
    giver, sink = tallies[1:1 + 2 * pairs:2], tallies[2:2 + 2 * pairs:2]
    margin = jnp.minimum(giver - 1, most - sink)
    passed = jax.random.randint(jax.random.fold_in(key, 1), (pairs,), 0, 1 << 20) % (margin + 1)
    tallies = tallies.at[1:1 + 2 * pairs:2].set(giver - passed).at[2:2 + 2 * pairs:2].set(sink + passed)
    return tallies[jax.random.permutation(jax.random.fold_in(key, 2), count)]


def noise(own_key, shape, scale, limit, cuts=(), kind=jnp.bfloat16):
    loudness = block_levels(own_key, shape, cuts, -0.22, 0.18) if cuts else 1.0
    values = jax.random.normal(own_key, shape, jnp.float32) * scale * loudness
    return jnp.minimum(jnp.maximum(values, -limit), limit).astype(kind)


def setup_inputs(seed: int = 0) -> dict:
    key_list = jax.random.split(jax.random.key(seed), 13)
    tokens = noise(key_list[0], (TOKENS, D), 1.0, 6.0, ((0, 32),))
    lengths = jax.vmap(lambda own: uneven_parts(own, SEGS, L, L // 2, 2))(jax.random.split(key_list[1], N_DP)).reshape((N_DP, SEGS)).astype(jnp.int32)
    attn_gain = jnp.clip(1.0 + 0.18 * jax.random.normal(key_list[2], (D,), jnp.float32), 0.1, 1.9)
    query_weight = noise(key_list[3], (D, D), D ** -0.5, 0.21875, ((1, 4),))
    key_weight = noise(key_list[4], (D, D), D ** -0.5, 0.21875, ((1, 4),))
    value_weight = noise(key_list[5], (D, D), D ** -0.5, 0.21875, ((1, 4),))
    output_weight = noise(key_list[6], (D, D), (D // 16) ** -0.5, 0.875, ((0, 4),))
    ffn_gain = jnp.clip(1.0 + 0.18 * jax.random.normal(key_list[7], (D,), jnp.float32), 0.1, 1.9)
    gate_weight = noise(key_list[8], (D, FF), D ** -0.5, 0.21875, ((1, 4),))
    up_weight = noise(key_list[9], (D, FF), D ** -0.5, 0.21875, ((1, 4),))
    down_weight = noise(key_list[10], (FF, D), FF ** -0.5, 0.125, ((0, 4),))
    cotangent = noise(key_list[11], (TOKENS, D), 1.0, 6.0, ((0, 32),))
    return dict(tokens=tokens, lengths=lengths, attn_gain=attn_gain, query_weight=query_weight, key_weight=key_weight, value_weight=value_weight, output_weight=output_weight, ffn_gain=ffn_gain, gate_weight=gate_weight, up_weight=up_weight, down_weight=down_weight, cotangent=cotangent)


@jax.custom_vjp
def low(v):
    return lax.optimization_barrier(v.astype(jnp.bfloat16)).astype(jnp.float32)

@jax.custom_vjp
def low_back(v):
    return v

def low_keep(v):
    return (low(v), None)

def low_pass(kept, grad):
    return (grad,)

def back_keep(v):
    return (v, None)

def back_low(kept, grad):
    return (low(grad),)
low.defvjp(low_keep, low_pass)
low_back.defvjp(back_keep, back_low)
epsilon = 1e-06
highest = lax.Precision.HIGHEST

def matmul(left, right):
    return jnp.dot(left, right, precision=highest)

def rms_gain(values, gain):
    return values * lax.rsqrt(lax.optimization_barrier(jnp.mean(values * values, axis=-1, keepdims=True)) + epsilon) * gain

def segment_ids(row_lengths):
    ends = jnp.cumsum(row_lengths).astype(jnp.int32)
    places = jnp.arange(L, dtype=jnp.int32)
    return lax.optimization_barrier(jnp.sum((places[:, None] >= ends[None, :-1]).astype(jnp.int32), axis=1))

def attend(pieces):
    query, keys, values, ids = pieces
    scores = jnp.einsum('qhd,khd->hqk', query, keys, precision=highest) * HEAD ** (-0.5)
    scores = low_back(scores)
    same = (ids[:, None] == ids[None, :])[None]
    scores = jnp.where(same, scores, jnp.float32(-1e+30))
    top = lax.optimization_barrier(jnp.max(scores, axis=-1, keepdims=True))
    expo = jnp.exp(scores - top)
    probs = low(expo / lax.optimization_barrier(jnp.sum(expo, axis=-1, keepdims=True)))
    return jnp.einsum('hqk,khd->qhd', probs, values, precision=highest)

def reference(tokens, lengths, attn_gain, query_weight, key_weight, value_weight, output_weight, ffn_gain, gate_weight, up_weight, down_weight, cotangent):
    ids = jax.vmap(segment_ids)(lengths)

    def forward(inputs, gain_one, wquery, wkey, wvalue, wout, gain_two, wgate, wup, wdown):
        normed = low(rms_gain(inputs, gain_one))

        def project(weight):
            return low_back(low(matmul(normed, weight))).reshape(N_DP, L, HEADS, HEAD)
        mixed = lax.map(jax.checkpoint(attend), (project(wquery), project(wkey), project(wvalue), ids))
        mixed = low_back(low(mixed.reshape(TOKENS, D)))
        middle = inputs + low_back(matmul(mixed, wout))
        normed_two = low(rms_gain(middle, gain_two))
        gate = low_back(matmul(normed_two, wgate))
        upper = low_back(matmul(normed_two, wup))
        hidden = low(jax.nn.gelu(gate, approximate=True) * upper)
        return middle + low_back(matmul(hidden, wdown))
    primals = (tokens.astype(jnp.float32), attn_gain, query_weight.astype(jnp.float32), key_weight.astype(jnp.float32), value_weight.astype(jnp.float32), output_weight.astype(jnp.float32), ffn_gain, gate_weight.astype(jnp.float32), up_weight.astype(jnp.float32), down_weight.astype(jnp.float32))
    result, pullback = jax.vjp(forward, *primals)
    grads = pullback(cotangent.astype(jnp.float32))
    return (result.astype(jnp.bfloat16), grads[0], grads[1], grads[2], grads[3], grads[4], grads[5], grads[6], grads[7], grads[8], grads[9])
```

```python
import jax
import jax.numpy as jnp
from jax import lax
from jax.sharding import PartitionSpec as P

HEAD = 64


epsilon = 1e-06


def norm_forward(values):
    factor = lax.rsqrt(jnp.mean(values * values, axis=-1, keepdims=True) + epsilon)
    return (values * factor, factor)


def norm_backward(grad, based, factor, gain):
    scaled = grad * gain
    inner = jnp.mean(scaled * based, axis=-1, keepdims=True)
    return (factor * (scaled - based * inner), jnp.sum(grad * based, axis=0))


def gelu_product(gate, upper):
    return jax.nn.gelu(gate, approximate=True) * upper


def mat(left, right):
    return jnp.dot(left, right, preferred_element_type=jnp.float32)


def local(
    tokens,
    lengths,
    attn_gain,
    query_weight,
    key_weight,
    value_weight,
    output_weight,
    ffn_gain,
    gate_weight,
    up_weight,
    down_weight,
    cotangent,
):
    rows = tokens.shape[0]
    width = query_weight.shape[1]
    heads_here = width // HEAD
    factor_head = HEAD ** (-0.5)
    ends = jnp.cumsum(lengths[0])
    places = jnp.arange(rows, dtype=jnp.int32)
    ids = jnp.sum((places[:, None] >= ends[None, :-1]).astype(jnp.int32), axis=1)
    same = (ids[:, None] == ids[None, :])[None]
    inputs = tokens.astype(jnp.float32)
    based_one, factor_one = norm_forward(inputs)
    normed_one = (based_one * attn_gain).astype(jnp.bfloat16)
    query = mat(normed_one, query_weight).astype(jnp.bfloat16)
    keys = mat(normed_one, key_weight).astype(jnp.bfloat16)
    values = mat(normed_one, value_weight).astype(jnp.bfloat16)
    query_heads = query.reshape(rows, heads_here, HEAD)
    key_heads = keys.reshape(rows, heads_here, HEAD)
    value_heads = values.reshape(rows, heads_here, HEAD)
    scores = (
        jnp.einsum("qhd,khd->hqk", query_heads, key_heads, preferred_element_type=jnp.float32)
        * factor_head
    )
    scores = jnp.where(same, scores, jnp.float32(-1e30))
    top = jnp.max(scores, axis=-1, keepdims=True)
    expo = jnp.exp(scores - top)
    total = jnp.sum(expo, axis=-1, keepdims=True)
    logsum = top + jnp.log(total)
    probs_low = (expo / total).astype(jnp.bfloat16)
    mixed = jnp.einsum("hqk,khd->qhd", probs_low, value_heads, preferred_element_type=jnp.float32)
    mixed = mixed.astype(jnp.bfloat16).reshape(rows, width)
    attn = lax.psum(mat(mixed, output_weight), "tensor")
    middle = inputs + attn
    based_two, factor_two = norm_forward(middle)
    normed_two = (based_two * ffn_gain).astype(jnp.bfloat16)
    gate = mat(normed_two, gate_weight)
    upper = mat(normed_two, up_weight)
    product, product_pull = jax.vjp(gelu_product, gate, upper)
    hidden = product.astype(jnp.bfloat16)
    ffn_part = mat(hidden, down_weight)
    ffn = ffn_part
    for shift in (1, 3, 2):
        ffn = ffn + lax.ppermute(ffn_part, "tensor", [(i, (i + shift) % 4) for i in range(4)])
    layer_out = (middle + ffn).astype(jnp.bfloat16)
    grad_out = cotangent.astype(jnp.float32)
    down_grad = mat(hidden.T, cotangent)
    grad_hidden = mat(cotangent, down_weight.T)
    grad_gate, grad_upper = product_pull(grad_hidden)
    grad_gate = grad_gate.astype(jnp.bfloat16)
    grad_upper = grad_upper.astype(jnp.bfloat16)
    gate_grad = mat(normed_two.T, grad_gate)
    up_grad = mat(normed_two.T, grad_upper)
    grad_normed_two = lax.psum(
        mat(grad_gate, gate_weight.T) + mat(grad_upper, up_weight.T), "tensor"
    )
    grad_from_two, ffn_gain_grad = norm_backward(grad_normed_two, based_two, factor_two, ffn_gain)
    grad_middle = grad_out + grad_from_two
    grad_attn = grad_middle.astype(jnp.bfloat16)
    output_grad = mat(mixed.T, grad_attn)
    grad_mixed = (
        mat(grad_attn, output_weight.T).astype(jnp.bfloat16).reshape(rows, heads_here, HEAD)
    )
    again = (
        jnp.einsum("qhd,khd->hqk", query_heads, key_heads, preferred_element_type=jnp.float32)
        * factor_head
    )
    probs = jnp.where(same, jnp.exp(again - logsum), jnp.float32(0.0))
    probs_again = probs.astype(jnp.bfloat16)
    grad_values = jnp.einsum(
        "hqk,qhd->khd", probs_again, grad_mixed, preferred_element_type=jnp.float32
    )
    grad_values = grad_values.astype(jnp.bfloat16).reshape(rows, width)
    grad_probs = jnp.einsum(
        "qhd,khd->hqk", grad_mixed, value_heads, preferred_element_type=jnp.float32
    )
    grad_scores = probs * (grad_probs - jnp.sum(grad_probs * probs, axis=-1, keepdims=True))
    grad_scores = grad_scores.astype(jnp.bfloat16)
    grad_query = (
        jnp.einsum("hqk,khd->qhd", grad_scores, key_heads, preferred_element_type=jnp.float32)
        * factor_head
    )
    grad_query = grad_query.astype(jnp.bfloat16).reshape(rows, width)
    grad_keys = (
        jnp.einsum("hqk,qhd->khd", grad_scores, query_heads, preferred_element_type=jnp.float32)
        * factor_head
    )
    grad_keys = grad_keys.astype(jnp.bfloat16).reshape(rows, width)
    query_grad = mat(normed_one.T, grad_query)
    key_grad = mat(normed_one.T, grad_keys)
    value_grad = mat(normed_one.T, grad_values)
    partial_one = (
        mat(grad_query, query_weight.T)
        + mat(grad_keys, key_weight.T)
        + mat(grad_values, value_weight.T)
    )
    grad_normed_one = lax.psum(partial_one, "tensor")
    grad_from_one, attn_gain_grad = norm_backward(grad_normed_one, based_one, factor_one, attn_gain)
    token_grad = grad_middle + grad_from_one
    (
        attn_gain_grad,
        query_grad,
        key_grad,
        value_grad,
        output_grad,
        ffn_gain_grad,
        gate_grad,
        up_grad,
        down_grad,
    ) = lax.psum(
        (
            attn_gain_grad,
            query_grad,
            key_grad,
            value_grad,
            output_grad,
            ffn_gain_grad,
            gate_grad,
            up_grad,
            down_grad,
        ),
        "dp",
    )
    return (
        layer_out,
        token_grad,
        attn_gain_grad,
        query_grad,
        key_grad,
        value_grad,
        output_grad,
        ffn_gain_grad,
        gate_grad,
        up_grad,
        down_grad,
    )


def solution(mesh):
    placed = (
        P("dp", None),
        P("dp", None),
        P(),
        P(None, "tensor"),
        P(None, "tensor"),
        P(None, "tensor"),
        P("tensor", None),
        P(),
        P(None, "tensor"),
        P(None, "tensor"),
        P("tensor", None),
        P("dp", None),
    )
    return jax.shard_map(
        local,
        mesh=mesh,
        in_specs=placed,
        out_specs=(
            P("dp", None),
            P("dp", None),
            P(),
            P(None, "tensor"),
            P(None, "tensor"),
            P(None, "tensor"),
            P("tensor", None),
            P(),
            P(None, "tensor"),
            P(None, "tensor"),
            P("tensor", None),
        ),
        check_vma=False,
    )
```

```python
import functools
import jax
import jax.numpy as jnp
from jax import lax
from jax.experimental import pallas as pl
from jax.experimental.pallas import tpu as pltpu
from jax.sharding import PartitionSpec as P

T = 1024
D = 768
HALF = 512
HW = 192
UN = 512
EPS = 1e-06
F32 = jnp.float32
BF16 = jnp.bfloat16
PIECE_A, CUT_A = 120, 184
PIECE_B, CUT_B = 96, 160
VM = pl.BlockSpec(memory_space=pltpu.VMEM)
SM = pl.BlockSpec(memory_space=pltpu.SMEM)


def call(body, out_shape, n_vmem, smem=0, scratch=(), flops=0, bytes_accessed=0, limit=56, outs=None):
    return pl.pallas_call(
        body,
        out_shape=out_shape,
        in_specs=[SM] * smem + [VM] * n_vmem,
        out_specs=jax.tree.map(lambda _: VM, out_shape),
        scratch_shapes=list(scratch),
        compiler_params=pltpu.CompilerParams(vmem_limit_bytes=limit << 20),
        cost_estimate=pl.CostEstimate(flops=int(flops), bytes_accessed=int(bytes_accessed), transcendentals=0),
    )


def sds(shape, dtype):
    return jax.ShapeDtypeStruct(shape, dtype)


def nn(a, b):
    return jnp.dot(a, b, preferred_element_type=F32)


def nt(a, b):
    return lax.dot_general(a, b, (((1,), (1,)), ((), ())), preferred_element_type=F32)


def tn(a, b):
    return lax.dot_general(a, b, (((0,), (0,)), ((), ())), preferred_element_type=F32)


def long_start(len_ref):
    start, acc = jnp.int32(0), jnp.int32(0)
    for k in range(8):
        n = len_ref[0, k]
        start = jnp.where(n == HALF, acc, start)
        acc = acc + n
    return start


def rest_mask(len_ref):
    start = long_start(len_ref)

    def ids(shape, dim):
        place = lax.broadcasted_iota(jnp.int32, shape, dim) + (HALF + start)
        place = jnp.where(place >= T, place - T, place)
        end, got = jnp.int32(0), jnp.zeros(shape, jnp.int32)
        for k in range(7):
            end = end + len_ref[0, k]
            got = got + (place >= end).astype(jnp.int32)
        return got

    return ids((HALF, 1), 0) == ids((1, HALF), 1)


def window(buf, first):
    first = jnp.where(first >= T, first - T, first)
    base = pl.multiple_of(first // 8 * 8, 8)
    v = buf[pl.ds(base, 264), :]
    return pltpu.roll(v, lax.rem(264 - (first - base), 264), 0)[0:256]


def pack_body(pos_ref, wq_ref, wk_ref, wv_ref, wo_ref, wg_ref, wu_ref, wd_ref, a_ref, b_ref, s_ref, tmp):
    core, j, d = pos_ref[1], pos_ref[2], pos_ref[4]
    cols = pl.ds(pl.multiple_of(j * 128, 128), 128)
    for m, ref in enumerate((wg_ref, wu_ref)):
        both = ref[:, cols].astype(F32).T
        mine = jnp.where(core == 0, both[0:64], both[64:128])
        a_ref[pl.ds(32 * m, 32), :] = mine[0:32]
        b_ref[pl.ds(32 * m, 32), :] = mine[32:64]
    first = j * 128 + core * 64
    a_ref[64:96, :] = wd_ref[pl.ds(pl.multiple_of(first, 32), 32), :].astype(F32)
    b_ref[64:96, :] = wd_ref[pl.ds(pl.multiple_of(first + 32, 32), 32), :].astype(F32)
    tmp[0:192, :] = wo_ref[...].astype(F32)
    a_ref[96:120, :] = tmp[pl.ds(pl.multiple_of(core * 96 + j * 24, 8), 24), :]
    for m, ref in enumerate((wq_ref, wk_ref, wv_ref)):
        tmp[:, 256 * m : 256 * m + 192] = ref[...].astype(F32)
        tmp[:, 256 * m + 192 : 256 * m + 256] = jnp.zeros((D, 64), F32)
    s_ref[...] = tmp[pl.ds(pl.multiple_of(d * 24, 8), 24), :]


def pack(pos, *weights):
    return call(pack_body, (sds((PIECE_A, D), F32), sds((PIECE_B, D), F32), sds((24, D), F32)), 7, 1,
                [pltpu.VMEM((D, D), F32)], 1e6, 5e6)(pos, *weights)


def unpack_ffn_body(pos_ref, *refs):
    blocks, (wg_ref, wu_ref, wd_ref, buf) = refs[:8], refs[8:]
    for row, v in unpacked(pos_ref, blocks):
        rows = pl.ds(row, 24)
        wg_ref[rows, :] = v[:, 0:512]
        wu_ref[rows, :] = v[:, 512:1024]
        buf[rows, :] = v[:, 1024:1536]
    wd_ref[...] = buf[...].T


def unpacked(pos_ref, blocks):
    core = pos_ref[1]
    for k, (half, ja, jb) in enumerate(((core, pos_ref[2], pos_ref[3]), (1 - core, pos_ref[3], pos_ref[2]))):
        for block, sa in zip(blocks[4 * k : 4 * k + 4], (0, 3, 1, 2)):
            for n, sb in enumerate((0, 3, 1, 2)):
                row = half * 384 + lax.rem(ja + sa, 4) * 96 + lax.rem(jb + sb, 4) * 24
                yield pl.multiple_of(row, 8), block[pl.ds(24 * n, 24), :]


def unpack_ffn(pos, blocks):
    return call(unpack_ffn_body, (sds((D, UN), F32), sds((D, UN), F32), sds((UN, D), F32)), 8, 1,
                [pltpu.VMEM((D, UN), F32)], 1e6, 1e7)(pos, *blocks)


def unpack_attn_body(pos_ref, *refs):
    blocks, (wq_ref, wk_ref, wv_ref, wo_ref, buf) = refs[:8], refs[8:]
    for row, v in unpacked(pos_ref, blocks):
        rows = pl.ds(row, 24)
        wq_ref[rows, :] = v[:, 0:192]
        wk_ref[rows, :] = v[:, 192:384]
        wv_ref[rows, :] = v[:, 384:576]
        buf[rows, :] = v[:, 576:768]
    wo_ref[...] = buf[...].T


def unpack_attn(pos, blocks):
    o = sds((D, HW), F32)
    return call(unpack_attn_body, (o, o, o, sds((HW, D), F32)), 8, 1, [pltpu.VMEM((D, HW), F32)], 1e6, 5e6)(pos, *blocks)


def prep_body(len_ref, x_ref, dy_ref, gain_ref, xr_ref, n1_ref, dyr_ref, buf):
    start = long_start(len_ref)

    def fill(src):
        for t in range(4):
            buf[pl.ds(256 * t, 256), :] = src[pl.ds(256 * t, 256), :].astype(F32)
        buf[pl.ds(T, 264), :] = buf[pl.ds(0, 264), :]

    def piece(t):
        return window(buf, start + 256 * t)

    fill(x_ref)
    for t in range(4):
        x = piece(t)
        xr_ref[pl.ds(256 * t, 256), :] = x.astype(BF16)
        r = lax.rsqrt(jnp.mean(x * x, axis=-1, keepdims=True) + EPS)
        n1_ref[pl.ds(256 * t, 256), :] = (x * r * gain_ref[...]).astype(BF16)
    fill(dy_ref)
    for t in range(4):
        dyr_ref[pl.ds(256 * t, 256), :] = piece(t).astype(BF16)


def prep(lengths, tokens, cot, gain):
    o = sds((T, D), BF16)
    return call(prep_body, (o, o, o), 3, 1, [pltpu.VMEM((T + 264, D), F32)], 6e6, 8e6)(
        lengths, tokens, cot, gain.reshape(1, D)
    )


def head_mask(h):
    lane = lax.broadcasted_iota(jnp.int32, (1, HW), 1)
    return (lane >= 64 * h) & (lane < 64 * h + 64)


def only(v, h):
    return jnp.where(head_mask(h), v, jnp.zeros_like(v))


def attn_body(len_ref, n1_ref, wq_ref, wk_ref, wv_ref, q_ref, k_ref, v_ref, o_ref, ot_ref, lse_ref):
    mask = rest_mask(len_ref)
    for i in range(2):
        rows = pl.ds(HALF * i, HALF)
        n1 = n1_ref[rows, :]
        q = (nn(n1, wq_ref[...]).astype(BF16).astype(F32) * 0.125).astype(BF16)
        k = nn(n1, wk_ref[...]).astype(BF16)
        v = nn(n1, wv_ref[...]).astype(BF16)
        q_ref[rows, :] = q
        k_ref[rows, :] = k
        v_ref[rows, :] = v
        vt = v.T
        outs = []
        for h in range(3):
            s = nt(k, only(q, h))
            if i == 1:
                s = jnp.where(mask, s, -1e30)
            top = jnp.max(s, axis=0, keepdims=True)
            e = jnp.exp(s - top)
            total = jnp.sum(e, axis=0, keepdims=True)
            lse_ref[pl.ds(h, 1), rows] = top + jnp.log(total)
            o = nn(vt[64 * h : 64 * h + 64, :], e.astype(BF16))
            outs.append(o * (1.0 / total))
        o = jnp.concatenate(outs, axis=0).astype(BF16)
        ot_ref[:, rows] = o.astype(F32)
        o_ref[rows, :] = o.T


def attn(lengths, n1, wq, wk, wv):
    b = sds((T, HW), BF16)
    return call(attn_body, (b, b, b, b, sds((HW, T), F32), sds((8, T), F32)), 4, 1, (), 4e9, 4e6)(
        lengths, n1, wq, wk, wv
    )


def heads_back(i, mask, q, k, v, do, lse):
    kt = k.T
    dk = dv = None
    dqt = []
    for h in range(3):
        qh, doh = only(q, h), only(do, h)
        s = nt(k, qh)
        if i == 1:
            s = jnp.where(mask, s, -1e30)
        if lse is None:
            top = jnp.max(s, axis=0, keepdims=True)
            e = jnp.exp(s - top)
            p = e * (1.0 / jnp.sum(e, axis=0, keepdims=True))
        else:
            p = jnp.exp(s - lse[h : h + 1, :])
        dp = nt(v, doh)
        delta = jnp.sum(p * dp, axis=0, keepdims=True)
        ds = (p * (dp - delta)).astype(BF16)
        a = nn(p.astype(BF16), doh)
        b = nn(ds, qh)
        dv = a if dv is None else dv + a
        dk = b if dk is None else dk + b
        dqt.append(nn(kt[64 * h : 64 * h + 64, :], ds))
    dq = (jnp.concatenate(dqt, axis=0) * 0.125).T
    return dq.astype(BF16), dk.astype(BF16), dv.astype(BF16)


def own_back_body(len_ref, dhb_ref, wo_ref, q_ref, k_ref, v_ref, lse_ref, n1_ref, o_ref, g_ref, d_ref):
    mask = rest_mask(len_ref)
    for i in range(2):
        rows = pl.ds(HALF * i, HALF)
        do = nt(dhb_ref[rows, :], wo_ref[...]).astype(BF16)
        dq, dk, dv = heads_back(i, mask, q_ref[rows, :], k_ref[rows, :], v_ref[rows, :], do, lse_ref[:, rows])
        d_ref[rows, 0:192] = dq
        d_ref[rows, 192:384] = dk
        d_ref[rows, 384:576] = dv
    for t in range(3):
        cols = pl.ds(256 * t, 256)
        g_ref[cols, 0:576] = tn(n1_ref[:, cols], d_ref[...])
        g_ref[cols, 576:768] = tn(dhb_ref[:, cols], o_ref[...])


def own_back(lengths, dhb, wo, q, k, v, lse, n1, o):
    return call(
        own_back_body, (sds((D, D), F32), sds((T, 576), BF16)), 8, 1, (), 8e9, 9e6
    )(lengths, dhb, wo, q, k, v, lse, n1, o)


def rest_back_body(len_ref, pos_ref, n1_ref, dhb_ref, w_ref, wo_rem, d_ref, dn1_ref):
    j = pl.program_id(0)
    me = pos_ref[0]
    mask = rest_mask(len_ref)

    w = w_ref[0]
    wqb = w[:, 0:192].astype(BF16)
    wkb = w[:, 256:448].astype(BF16)
    wvb = w[:, 512:704].astype(BF16)

    def add(rows, dq, dk, dv):
        new = nt(dq, wqb) + nt(dk, wkb) + nt(dv, wvb)

        @pl.when(j == 0)
        def _():
            dn1_ref[rows, :] = new

        @pl.when(j > 0)
        def _():
            dn1_ref[rows, :] = dn1_ref[rows, :] + new

    @pl.when(j == me)
    def _():
        for i in range(2):
            rows = pl.ds(HALF * i, HALF)
            add(rows, d_ref[rows, 0:192], d_ref[rows, 192:384], d_ref[rows, 384:576])

    @pl.when(j != me)
    def _():
        back = lax.rem(me - j + 4, 4)
        wo = wo_rem[jnp.where(back == 1, 0, jnp.where(back == 3, 1, 2))]
        for i in range(2):
            rows = pl.ds(HALF * i, HALF)
            n1 = n1_ref[rows, :]
            q = (nn(n1, wqb).astype(BF16).astype(F32) * 0.125).astype(BF16)
            k = nn(n1, wkb).astype(BF16)
            v = nn(n1, wvb).astype(BF16)
            do = nt(dhb_ref[rows, :], wo).astype(BF16)
            add(rows, *heads_back(i, mask, q, k, v, do, None))


def rest_back(lengths, pos, n1, dhb, w, wo_rem, d):
    whole = lambda shape: pl.BlockSpec(shape, lambda j: (0,) * len(shape))
    return pl.pallas_call(
        rest_back_body,
        grid=(4,),
        out_shape=sds((T, D), F32),
        in_specs=[SM, SM, whole((T, D)), whole((T, D)), pl.BlockSpec((1, D, D), lambda j: (j, 0, 0)),
                  whole((3, HW, D)), whole((T, 576))],
        out_specs=whole((T, D)),
        compiler_params=pltpu.CompilerParams(vmem_limit_bytes=56 << 20),
        cost_estimate=pl.CostEstimate(flops=int(2.4e10), bytes_accessed=int(2e7), transcendentals=0),
    )(lengths, pos, n1, dhb, w, wo_rem, d)


def middle_body(pos_ref, x_ref, oo, oa, ob, oc, od, wo_own, qa, aa, ba, ca, da, qb, ab, bb, cb, db, gain_ref,
                h_ref, n2_ref, rem_ref, buf):
    core = pos_ref[1]
    for half, j, (q, a, b, c, d) in ((core, pos_ref[2], (qa, aa, ba, ca, da)), (1 - core, pos_ref[3], (qb, ab, bb, cb, db))):
        for r in range(3):
            at = PIECE_A * r + 96
            for src, step in ((q, 0), (a, 3), (b, 1), (c if at < CUT_A else d, 2)):
                where = lax.rem(j + step, 4)
                row = pl.multiple_of(half * 96 + where * 24, 8)
                first = at - CUT_A if src is d else at
                buf[r, pl.ds(row, 24), :] = src[pl.ds(first, 24), :]
    rem_ref[...] = buf[...].astype(BF16)
    for t in range(4):
        rows = pl.ds(256 * t, 256)
        h = x_ref[rows, :].astype(F32) + tn(oo[:, rows].astype(BF16), wo_own[...])
        h = h + tn(oa[:, rows].astype(BF16), rem_ref[0])
        h = h + tn(ob[:, rows].astype(BF16), rem_ref[1])
        h = h + tn(oc[:, rows].astype(BF16), rem_ref[2, 0:96, :]) + tn(od[:, rows].astype(BF16), rem_ref[2, 96:192, :])
        h_ref[rows, :] = h
        f = lax.rsqrt(jnp.mean(h * h, axis=-1, keepdims=True) + EPS)
        n2_ref[rows, :] = (h * f * gain_ref[...]).astype(BF16)


def middle(pos, xr, os, wo, mine, other, gain):
    return call(middle_body, (sds((T, D), F32), sds((T, D), BF16), sds((3, HW, D), BF16)), 18, 1,
                [pltpu.VMEM((3, HW, D), F32)], 1.2e9, 8e6)(pos, xr, *os, wo, *mine, *other, gain.reshape(1, D))


C1 = 0.7978845608028654
C2 = 0.044715 * C1


def ffn_math(gate, up, dhid):
    u2 = gate * gate
    t = jnp.tanh(gate * (C1 + C2 * u2))
    hp = 0.5 + 0.5 * t
    g = gate * hp
    slope = hp + g * (1.0 - t) * (C1 + 3.0 * C2 * u2)
    return (g * up).astype(BF16), (dhid * up * slope).astype(BF16), (dhid * g).astype(BF16)


def ffn_own_body(n2_ref, dy_ref, wg_ref, wu_ref, wd_ref, f_ref, dn2_ref, g_ref, hid, dgu):
    for t in range(4):
        rows = pl.ds(256 * t, 256)
        n2, dy = n2_ref[rows, :], dy_ref[rows, :]
        gate = nn(n2, wg_ref[...])
        up = nn(n2, wu_ref[...])
        dh = nt(dy, wd_ref[...])
        a, b, c = ffn_math(gate, up, dh)
        hid[rows, :] = a
        dgu[rows, 0:512] = b
        dgu[rows, 512:1024] = c
        f_ref[rows, :] = nn(a, wd_ref[...])
        dn2_ref[rows, :] = nt(b, wg_ref[...]) + nt(c, wu_ref[...])
    for t in range(3):
        cols = pl.ds(256 * t, 256)
        g_ref[cols, 0:1024] = tn(n2_ref[:, cols], dgu[...])
        g_ref[cols, 1024:1536] = tn(dy_ref[:, cols], hid[...])


def ffn_own(n2, dy, wg, wu, wd):
    o = sds((T, D), F32)
    return call(ffn_own_body, (o, o, sds((D, 1536), F32)), 5, 0,
                [pltpu.VMEM((T, UN), BF16), pltpu.VMEM((T, 1024), BF16)], 7.2e9, 1.6e7)(n2, dy, wg, wu, wd)


def ffn_rest_body(piece, cut, n2_ref, dy_ref, f_in, dn2_in, qa, aa, ba, ca, da, qb, ab, bb, cb, db, f_ref, dn2_ref, wb):
    n = 0
    for q, a, b, c, d in ((qa, aa, ba, ca, da), (qb, ab, bb, cb, db)):
        for r in range(3):
            for which in range(4):
                for m in range(3):
                    at = piece * r + 32 * m
                    src = (q, a, b, c)[which]
                    if which == 3 and at >= cut:
                        src, at = d, at - cut
                    wb[m, pl.ds(32 * n, 32), :] = src[pl.ds(at, 32), :].astype(BF16)
                n += 1
    for t in range(4):
        rows = pl.ds(256 * t, 256)
        n2, dy = n2_ref[rows, :], dy_ref[rows, :]
        f, dn2 = f_in[rows, :], dn2_in[rows, :]
        for u in range(3):
            us = pl.ds(256 * u, 256)
            gate = nt(n2, wb[0, us, :])
            up = nt(n2, wb[1, us, :])
            dh = nt(dy, wb[2, us, :])
            a, b, c = ffn_math(gate, up, dh)
            f = f + nn(a, wb[2, us, :])
            dn2 = dn2 + nn(b, wb[0, us, :]) + nn(c, wb[1, us, :])
        f_ref[rows, :] = f
        dn2_ref[rows, :] = dn2


def ffn_rest(piece, cut, n2, dy, f, dn2, mine, other):
    o = sds((T, D), F32)
    return call(functools.partial(ffn_rest_body, piece, cut), (o, o), 14, 0, [pltpu.VMEM((3, 768, D), BF16)],
                12 * T * D * 768, 2e7)(n2, dy, f, dn2, *mine, *other)


def dh_body(h_ref, dn2_ref, dy_ref, gain_ref, dh_ref, dhb_ref, gg_ref):
    gg = jnp.zeros((8, D), F32)
    for t in range(4):
        rows = pl.ds(256 * t, 256)
        h = h_ref[rows, :]
        r = lax.rsqrt(jnp.mean(h * h, axis=-1, keepdims=True) + EPS)
        b = h * r
        dn2 = dn2_ref[rows, :]
        gg = gg + jnp.sum((dn2 * b).reshape(32, 8, D), axis=0)
        e = dn2 * gain_ref[...]
        dh = dy_ref[rows, :].astype(F32) + r * (e - b * jnp.mean(e * b, axis=-1, keepdims=True))
        dh_ref[rows, :] = dh
        dhb_ref[rows, :] = dh.astype(BF16)
    gg_ref[...] = jnp.broadcast_to(jnp.sum(gg, axis=0, keepdims=True), (8, D))


def dh_call(h, dn2, dy, gain):
    return call(dh_body, (sds((T, D), F32), sds((T, D), BF16), sds((8, D), F32)), 4, 0, (), 2e7, 1.2e7)(
        h, dn2, dy, gain.reshape(1, D))


def unrotate(start, buf, out_ref, dtype):
    back = jnp.where(start > 0, T - start, 0)
    buf[pl.ds(T, 264), :] = buf[pl.ds(0, 264), :]
    for t in range(4):
        out_ref[pl.ds(256 * t, 256), :] = window(buf, back + 256 * t).astype(dtype)


def layer_body(len_ref, h_ref, f_ref, out_ref, buf):
    for t in range(4):
        rows = pl.ds(256 * t, 256)
        buf[rows, :] = h_ref[rows, :] + f_ref[rows, :]
    unrotate(long_start(len_ref), buf, out_ref, BF16)


def layer_call(lengths, h, f):
    return call(layer_body, sds((T, D), BF16), 2, 1, [pltpu.VMEM((T + 264, D), F32)], 2e6, 8e6)(lengths, h, f)


def token_body(len_ref, x_ref, dh_ref, dn1_ref, gain_ref, out_ref, gg_ref, buf):
    gg = jnp.zeros((8, D), F32)
    for t in range(4):
        rows = pl.ds(256 * t, 256)
        x = x_ref[rows, :].astype(F32)
        r = lax.rsqrt(jnp.mean(x * x, axis=-1, keepdims=True) + EPS)
        b = x * r
        dn1 = dn1_ref[rows, :]
        gg = gg + jnp.sum((dn1 * b).reshape(32, 8, D), axis=0)
        e = dn1 * gain_ref[...]
        buf[rows, :] = dh_ref[rows, :] + r * (e - b * jnp.mean(e * b, axis=-1, keepdims=True))
    gg_ref[...] = jnp.broadcast_to(jnp.sum(gg, axis=0, keepdims=True), (8, D))
    unrotate(long_start(len_ref), buf, out_ref, F32)


def token_call(lengths, xr, dh, dn1, gain):
    return call(token_body, (sds((T, D), F32), sds((8, D), F32)), 4, 1, [pltpu.VMEM((T + 264, D), F32)], 2e7, 1.2e7)(
        lengths, xr, dh, dn1, gain.reshape(1, D))


RING = 4


def x_shift(v, step):
    return lax.ppermute(v, "tensor", [(i, (i + step) % RING) for i in range(RING)])


def dp_table(move):
    table = []
    for y in range(RING):
        for z in range(RING):
            for c in range(2):
                to_y, to_z, to_c = move(y, z, c)
                table.append(((y * RING + z) * 2 + c, (to_y % RING * RING + to_z % RING) * 2 + to_c))
    return table


def a_shift(v, step):
    return lax.ppermute(v, "dp", dp_table(lambda y, z, c: (y + step * (1 - c), z + step * c, c)))


def b_shift(v, step):
    return lax.ppermute(v, "dp", dp_table(lambda y, z, c: (y + step * c, z + step * (1 - c), c)))


def y_shift(v, step):
    return lax.ppermute(v, "dp", dp_table(lambda y, z, c: (y + step, z, c)))


def z_shift(v, step):
    return lax.ppermute(v, "dp", dp_table(lambda y, z, c: (y, z + step, c)))


def core_swap(v):
    return lax.ppermute(v, "dp", dp_table(lambda y, z, c: (y, z, 1 - c)))


def gather_shards(piece, cut):
    q = jnp.concatenate([x_shift(piece, 1), x_shift(piece, -1), x_shift(piece, 2)], axis=0)
    a, b = a_shift(q, 1), a_shift(q, -1)
    c, d = a_shift(a[:cut], 1), a_shift(b[cut:], -1)
    mine = (q, a, b, c, d)
    return mine, tuple(core_swap(v) for v in mine)


def rows_at(v, row, count):
    return lax.dynamic_slice_in_dim(v, row, count, axis=0)


def sum_over_dp(v, core, ja, jb):
    half = rows_at(v, core * 384, 384) + core_swap(rows_at(v, (1 - core) * 384, 384))
    for shift, j, size in ((a_shift, ja, 96), (b_shift, jb, 24)):
        at = lambda step: rows_at(half, (j + step) % RING * size, size)
        got = [shift(at(step), step) for step in (1, -1, 2)]
        half = (at(0) + got[2]) + (got[0] + got[1])
    block = jnp.concatenate([half] + [b_shift(half, step) for step in (1, -1, 2)], axis=0)
    blocks = [block] + [a_shift(block, step) for step in (1, -1, 2)]
    return blocks + [core_swap(b) for b in blocks]


def small_sum_over_dp(v):
    for shift in (y_shift, z_shift):
        v = (v + shift(v, 2)) + (shift(v, 1) + shift(v, -1))
    return v + core_swap(v)


def local(
    tokens,
    lengths,
    attn_gain,
    query_weight,
    key_weight,
    value_weight,
    output_weight,
    ffn_gain,
    gate_weight,
    up_weight,
    down_weight,
    cotangent,
):
    x = lax.axis_index("tensor").astype(jnp.int32)
    d = lax.axis_index("dp").astype(jnp.int32)
    core, y, z = d % 2, d // 8, d // 2 % 4
    ja, jb = jnp.where(core == 0, y, z), jnp.where(core == 0, z, y)
    pos = jnp.stack([x, core, ja, jb, d])
    piece_a, piece_b, piece_s = pack(
        pos, query_weight, key_weight, value_weight, output_weight, gate_weight, up_weight, down_weight
    )
    mine_a, other_a = gather_shards(piece_a, CUT_A)
    mine_b, other_b = gather_shards(piece_b, CUT_B)
    qkv = lax.all_gather(piece_s, ("tensor", "dp"), axis=0, tiled=True).reshape(4, D, D)

    xr, n1, dyr = prep(lengths, tokens, cotangent, attn_gain)
    q, k, v, o, ot, lse = attn(lengths, n1, query_weight, key_weight, value_weight)
    oa, ob = x_shift(ot, 1), x_shift(ot, -1)
    os = (ot, oa, ob, x_shift(oa[:96], 1), x_shift(ob[96:], -1))
    h, n2, wo_rem = middle(pos, xr, os, output_weight, mine_a, other_a, ffn_gain)

    f, dn2, g_ffn = ffn_own(n2, dyr, gate_weight, up_weight, down_weight)
    ffn_blocks = sum_over_dp(g_ffn, core, ja, jb)
    f, dn2 = ffn_rest(PIECE_A, CUT_A, n2, dyr, f, dn2, mine_a, other_a)
    f, dn2 = ffn_rest(PIECE_B, CUT_B, n2, dyr, f, dn2, mine_b, other_b)
    layer_out = layer_call(lengths, h, f)
    dh, dhb, gain_two = dh_call(h, dn2, dyr, ffn_gain)

    g_attn, dqkv = own_back(lengths, dhb, output_weight, q, k, v, lse, n1, o)
    attn_blocks = sum_over_dp(g_attn, core, ja, jb)
    dn1 = rest_back(lengths, pos, n1, dhb, qkv, wo_rem, dqkv)
    token_grad, gain_one = token_call(lengths, xr, dh, dn1, attn_gain)
    gains = small_sum_over_dp(jnp.concatenate([gain_one[0:1], gain_two[0:1]], axis=0))
    query_grad, key_grad, value_grad, output_grad = unpack_attn(pos, attn_blocks)
    gate_grad, up_grad, down_grad = unpack_ffn(pos, ffn_blocks)
    return (
        layer_out,
        token_grad,
        gains[0],
        query_grad,
        key_grad,
        value_grad,
        output_grad,
        gains[1],
        gate_grad,
        up_grad,
        down_grad,
    )


def solution(mesh):
    placed = (
        P("dp", None),
        P("dp", None),
        P(),
        P(None, "tensor"),
        P(None, "tensor"),
        P(None, "tensor"),
        P("tensor", None),
        P(),
        P(None, "tensor"),
        P(None, "tensor"),
        P("tensor", None),
        P("dp", None),
    )
    return jax.shard_map(
        local,
        mesh=mesh,
        in_specs=placed,
        out_specs=(
            P("dp", None),
            P("dp", None),
            P(),
            P(None, "tensor"),
            P(None, "tensor"),
            P(None, "tensor"),
            P("tensor", None),
            P(),
            P(None, "tensor"),
            P(None, "tensor"),
            P("tensor", None),
        ),
        check_vma=False,
    )
```

```python
import functools
import jax
import jax.numpy as jnp
from jax import lax
from jax.experimental import pallas as pl
from jax.experimental.pallas import tpu as pltpu
from jax.sharding import PartitionSpec as P

T = 1024
D = 768
HALF = 512
HW = 192
UN = 512
EPS = 1e-06
F32 = jnp.float32
BF16 = jnp.bfloat16
VM = pl.BlockSpec(memory_space=pltpu.VMEM)
SM = pl.BlockSpec(memory_space=pltpu.SMEM)


ANY = pl.BlockSpec(memory_space=pl.ANY)


def call(body, out_shape, n_vmem, smem=0, scratch=(), flops=0, bytes_accessed=0, limit=12, alias={}):
    def run(*args, deps=(), far=()):
        deps = [d for d in deps if d is not None]
        n = smem + n_vmem + len(far)

        def inner(*refs):
            body(*refs[:n], *refs[n + len(deps) :])

        return pl.pallas_call(
            inner,
            out_shape=out_shape,
            in_specs=[SM] * smem + [VM] * n_vmem + [ANY] * (len(far) + len(deps)),
            out_specs=jax.tree.map(lambda _: VM, out_shape),
            scratch_shapes=list(scratch),
            input_output_aliases=alias,
            compiler_params=pltpu.CompilerParams(vmem_limit_bytes=limit << 20),
            cost_estimate=pl.CostEstimate(flops=int(flops), bytes_accessed=int(bytes_accessed), transcendentals=0),
        )(*args, *far, *deps)

    return run


def sds(shape, dtype):
    return jax.ShapeDtypeStruct(shape, dtype)


def nn(a, b):
    return jnp.dot(a, b, preferred_element_type=F32)


def nt(a, b):
    return lax.dot_general(a, b, (((1,), (1,)), ((), ())), preferred_element_type=F32)


def tn(a, b):
    return lax.dot_general(a, b, (((0,), (0,)), ((), ())), preferred_element_type=F32)


def long_start(len_ref):
    start, acc = jnp.int32(0), jnp.int32(0)
    for k in range(8):
        n = len_ref[0, k]
        start = jnp.where(n == HALF, acc, start)
        acc = acc + n
    return start


def rest_mask(len_ref):
    start = long_start(len_ref)

    def ids(shape, dim):
        place = lax.broadcasted_iota(jnp.int32, shape, dim) + (HALF + start)
        place = jnp.where(place >= T, place - T, place)
        end, got = jnp.int32(0), jnp.zeros(shape, jnp.int32)
        for k in range(7):
            end = end + len_ref[0, k]
            got = got + (place >= end).astype(jnp.int32)
        return got

    return ids((HALF, 1), 0) == ids((1, HALF), 1)


def window(buf, first):
    first = jnp.where(first >= T, first - T, first)
    base = pl.multiple_of(first // 8 * 8, 8)
    v = buf[pl.ds(base, 264), :]
    return pltpu.roll(v, lax.rem(264 - (first - base), 264), 0)[0:256]


def pack_body(pos_ref, wo_ref, wg_ref, wu_ref, wd_ref, out_ref, half_ref, tmp):
    core, d = pos_ref[1], pos_ref[4]
    half_ref[...] = wo_ref[pl.ds(pl.multiple_of(core * 96, 32), 96), :].astype(F32)
    cols = pl.ds(pl.multiple_of(d // 8 * 128, 128), 128)
    first = pl.multiple_of(lax.rem(d, 8) * 16, 16)
    for m, ref in enumerate((wg_ref, wu_ref, wd_ref)):
        tmp[...] = ref[cols, :].astype(F32) if m == 2 else ref[:, cols].astype(F32).T
        out_ref[pl.ds(16 * m, 16), :] = tmp[pl.ds(first, 16), :]


def pack(pos, *weights):
    return call(pack_body, (sds((48, D), F32), sds((96, D), F32)), 4, 1, [pltpu.VMEM((128, D), F32)], 1e6, 5e6)(
        pos, *weights)


def cat_body(*refs):
    out, at = refs[-1], 0
    for ref in refs[:-1]:
        out[pl.ds(at, ref.shape[0]), :] = ref[...]
        at += ref.shape[0]


def cat(*parts, deps=()):
    shape = (sum(p.shape[0] for p in parts), parts[0].shape[1])
    return call(cat_body, sds(shape, F32), len(parts), 0, (), 1e5, 8 * shape[0] * shape[1])(*parts, deps=deps)


def cat_sum_body(size, *refs):
    out, parts = refs[-1], refs[:-1]
    for n, ref in enumerate(parts):
        out[pl.ds(size * n, size), :] = ref[0:size, :]
    own, left, right, opposite = [ref[size : size + 8, :] for ref in parts]
    out[pl.ds(4 * size, 8), :] = (own + opposite) + (left + right)


def cat_sum(*parts, deps=()):
    size = parts[0].shape[0] - 8
    return call(functools.partial(cat_sum_body, size), sds((4 * size + 8, D), F32), 4, 0, (), 1e5, 32e3 * size)(
        *parts, deps=deps)


def unpack_ffn_body(g_ref, wg_ref, wu_ref, wd_ref):
    wg_ref[...] = g_ref[:, 0:512]
    wu_ref[...] = g_ref[:, 512:1024]
    wd_ref[...] = g_ref[:, 1024:1536].T


def unpack_ffn(g, deps=()):
    return call(unpack_ffn_body, (sds((D, UN), F32), sds((D, UN), F32), sds((UN, D), F32)), 1, 0, (), 1e6, 1e7)(
        g, deps=deps)


def piece_row(core, ja, jb):
    return pl.multiple_of(jnp.where(core == 0, ja * 4 + jb, jb * 4 + ja) * 48 + core * 24, 8)


def unpack_attn_body(pos_ref, mine, other, wq_ref, wk_ref, wv_ref, wo_ref, one_ref, two_ref, buf):
    core, ja, jb = pos_ref[1], pos_ref[2], pos_ref[3]
    for ref, c, a, b in ((mine, core, ja, jb), (other, 1 - core, jb, ja)):
        for m, sa in enumerate((0, 3, 1, 2)):
            for n, sb in enumerate((0, 3, 1, 2)):
                row = piece_row(c, lax.rem(a + sa, 4), lax.rem(b + sb, 4))
                buf[pl.ds(row, 24), :] = ref[pl.ds(96 * m + 24 * n, 24), :]
    for n, out in enumerate((wq_ref, wk_ref, wv_ref, wo_ref)):
        out[...] = buf[192 * n : 192 * n + 192, :]
    gains = mine[384:392, :] + other[384:392, :]
    one_ref[...] = gains[0].reshape(D)
    two_ref[...] = gains[1].reshape(D)


def unpack_attn(pos, mine, other, deps=()):
    o, g = sds((HW, D), F32), sds((D,), F32)
    return call(unpack_attn_body, (o, o, o, o, g, g), 2, 1, [pltpu.VMEM((D, D), F32)], 1e6, 5e6)(pos, mine, other, deps=deps)


def split_rows(pos_ref, buf, keep_ref, send_ref):
    core, ja, jb = pos_ref[1], pos_ref[2], pos_ref[3]
    for out, half, a, b in ((keep_ref, core, ja, jb), (send_ref, 1 - core, jb, ja)):
        for sa in range(4):
            for sb in range(4):
                row = piece_row(half, lax.rem(a + sa, 4), lax.rem(b + sb, 4))
                out[pl.ds(96 * sa + 24 * sb, 24), :] = buf[pl.ds(row, 24), :]


def add_split_body(*refs):
    ins, outs = refs[:-4], refs[-4:]
    size = outs[0].shape[0]
    for n, out in enumerate(outs):
        rows = pl.ds(size * n, size)
        if len(ins) == 2:
            out[...] = ins[0][rows, :] + ins[1][rows, :]
        else:
            own, left, right, opposite = ins
            out[...] = (own[rows, :] + opposite[rows, :]) + (left[rows, :] + right[rows, :])


def add_split(*ins, deps=()):
    rows, lanes = ins[0].shape
    o = sds((rows // 4, lanes), F32)
    return call(add_split_body, (o,) * 4, len(ins), 0, (), rows * lanes * 2, rows * lanes * 12, 12)(*ins, deps=deps)


def add_body(own, left, right, opposite, *refs):
    out = refs[-1]
    rows = own.shape[0]
    out[0:rows, :] = (own[...] + opposite[...]) + (left[...] + right[...])
    if len(refs) > 1:
        row = lax.broadcasted_iota(jnp.int32, (8, 1), 0)
        out[rows : rows + 8, :] = jnp.where(row == 0, refs[0][...], jnp.where(row == 1, refs[1][...], 0.0))


def add_four(*ins, deps=()):
    rows, lanes = ins[0].shape
    out = sds((rows + (8 if len(ins) > 4 else 0), lanes), F32)
    return call(add_body, out, len(ins), 0, (), 1e5, 1e6)(*ins, deps=deps)


def prep_body(len_ref, x_ref, dy_ref, gain_ref, xr_ref, n1_ref, dyr_ref, buf):
    start = long_start(len_ref)

    def fill(src):
        for t in range(4):
            buf[pl.ds(256 * t, 256), :] = src[pl.ds(256 * t, 256), :].astype(F32)
        buf[pl.ds(T, 264), :] = buf[pl.ds(0, 264), :]

    def piece(t):
        return window(buf, start + 256 * t)

    fill(x_ref)
    for t in range(4):
        x = piece(t)
        xr_ref[pl.ds(256 * t, 256), :] = x.astype(BF16)
        r = lax.rsqrt(jnp.mean(x * x, axis=-1, keepdims=True) + EPS)
        n1_ref[pl.ds(256 * t, 256), :] = (x * r * gain_ref[...].reshape(1, D)).astype(BF16)
    fill(dy_ref)
    for t in range(4):
        dyr_ref[pl.ds(256 * t, 256), :] = piece(t).astype(BF16)


def prep(lengths, tokens, cot, gain, deps=()):
    o = sds((T, D), BF16)
    return call(prep_body, (o, o, o), 3, 1, [pltpu.VMEM((T + 264, D), F32)], 6e6, 8e6)(
        lengths, tokens, cot, gain, deps=deps
    )


def head_mask(h):
    lane = lax.broadcasted_iota(jnp.int32, (1, HW), 1)
    return (lane >= 64 * h) & (lane < 64 * h + 64)


def only(v, h):
    return jnp.where(head_mask(h), v, jnp.zeros_like(v))


def attn_body(len_ref, n1_ref, wq_ref, wk_ref, wv_ref, q_ref, k_ref, v_ref, o_ref, ot_ref, lse_ref):
    mask = rest_mask(len_ref)
    for i in range(2):
        rows = pl.ds(HALF * i, HALF)
        n1 = n1_ref[rows, :]
        q = (nt(n1, wq_ref[...]).astype(BF16).astype(F32) * 0.125).astype(BF16)
        k = nt(n1, wk_ref[...]).astype(BF16)
        v = nt(n1, wv_ref[...]).astype(BF16)
        q_ref[rows, :] = q
        k_ref[rows, :] = k
        v_ref[rows, :] = v
        vt = v.T
        outs = []
        for h in range(3):
            s = nt(k, only(q, h))
            if i == 1:
                s = jnp.where(mask, s, -1e30)
            top = jnp.max(s, axis=0, keepdims=True)
            e = jnp.exp(s - top)
            total = jnp.sum(e, axis=0, keepdims=True)
            lse_ref[pl.ds(h, 1), rows] = top + jnp.log(total)
            o = nn(vt[64 * h : 64 * h + 64, :], e.astype(BF16))
            outs.append(o * (1.0 / total))
        o = jnp.concatenate(outs, axis=0).astype(BF16)
        ot_ref[:, rows] = o.astype(F32)
        o_ref[rows, :] = o.T


def attn(lengths, n1, wq, wk, wv, deps=()):
    b = sds((T, HW), BF16)
    return call(attn_body, (b, b, b, b, sds((HW, T), F32), sds((8, T), F32)), 4, 1, (), 4e9, 4e6)(
        lengths, n1, wq, wk, wv, deps=deps
    )


def heads_back(i, mask, q, k, v, do, lse):
    lane = lax.broadcasted_iota(jnp.int32, (1, 256), 1)
    head = [(lane >= 64 * h) & (lane < 64 * h + 64) for h in range(3)]
    each = lambda t: jnp.concatenate([jnp.where(m, t, jnp.zeros_like(t)) for m in head], axis=0)
    s_all = nt(each(k), q)
    dp_all = nt(each(v), do)
    kt = k.T
    ps, dss, dqt = [], [], []
    for h in range(3):
        s = s_all[HALF * h : HALF * h + HALF]
        dp = dp_all[HALF * h : HALF * h + HALF]
        if i == 1:
            s = jnp.where(mask, s, -1e30)
        if lse is None:
            e = jnp.exp(s - jnp.max(s, axis=0, keepdims=True))
            p = e * (1.0 / jnp.sum(e, axis=0, keepdims=True))
        else:
            p = jnp.exp(s - lse[h : h + 1, :])
        ds = (p * (dp - jnp.sum(p * dp, axis=0, keepdims=True))).astype(BF16)
        ps.append(p.astype(BF16))
        dss.append(ds)
        dqt.append(nn(kt[64 * h : 64 * h + 64, :], ds))
    dq = (jnp.concatenate(dqt + [jnp.zeros((64, HALF), F32)], axis=0) * 0.125).T
    dv = nn(jnp.concatenate(ps, axis=0), do)
    dk = nn(jnp.concatenate(dss, axis=0), q)

    def pick(t):
        t = [t[HALF * h : HALF * h + HALF] for h in range(3)]
        t = jnp.where(head[0], t[0], jnp.where(head[1], t[1], t[2]))
        return jnp.where(lane < HW, t, 0.0).astype(BF16)

    return dq.astype(BF16), pick(dk), pick(dv)


def padded(t):
    return jnp.concatenate([t, jnp.zeros((t.shape[0], 256 - t.shape[1]), t.dtype)], axis=1)


def own_back_body(len_ref, pos_ref, dhb_ref, wo_ref, q_ref, k_ref, v_ref, lse_ref, n1_ref, o_ref,
                  keep_ref, send_ref, d_ref, g_ref):
    mask = rest_mask(len_ref)
    for i in range(2):
        rows = pl.ds(HALF * i, HALF)
        do = padded(nt(dhb_ref[rows, :], wo_ref[...]).astype(BF16))
        d = heads_back(i, mask, padded(q_ref[rows, :]), padded(k_ref[rows, :]), padded(v_ref[rows, :]), do, lse_ref[:, rows])
        for n in range(3):
            d_ref[rows, 256 * n : 256 * n + 256] = d[n]
    for n in range(3):
        g_ref[192 * n : 192 * n + 192, :] = tn(d_ref[:, 256 * n : 256 * n + 256], n1_ref[...])[0:192]
    g_ref[576:768, :] = tn(o_ref[...], dhb_ref[...])
    split_rows(pos_ref, g_ref, keep_ref, send_ref)


def own_back(lengths, pos, dhb, wo, q, k, v, lse, n1, o, deps=()):
    g = sds((384, D), F32)
    return call(own_back_body, (g, g, sds((T, D), BF16)), 8, 2, [pltpu.VMEM((D, D), F32)], 8e9, 9e6)(
        lengths, pos, dhb, wo, q, k, v, lse, n1, o, deps=deps)


def rest_back_body(first, last, len_ref, n1_ref, dhb_ref, w_ref, wo_ref, *refs):
    mask = rest_mask(len_ref)
    if first:
        own_d, wq, wk, wv, dn1_ref, d = refs
    elif last:
        dn1_in, x_ref, dn1_ref, gg_ref, d = refs
    else:
        dn1_in, dn1_ref, d = refs
    for i in range(2):
        rows = pl.ds(HALF * i, HALF)
        qkv = nt(n1_ref[rows, :], w_ref[...])
        q = (qkv[:, 0:256].astype(BF16).astype(F32) * 0.125).astype(BF16)
        k = qkv[:, 256:512].astype(BF16)
        v = qkv[:, 512:768].astype(BF16)
        do = nt(dhb_ref[rows, :], wo_ref[...]).astype(BF16)
        for n, t in enumerate(heads_back(i, mask, q, k, v, do, None)):
            d[:, 256 * n : 256 * n + 256] = t
        new = nn(d[...], w_ref[...])
        if first:
            for n, w in enumerate((wq, wk, wv)):
                new = new + nn(own_d[rows, 256 * n : 256 * n + 192], w[...])
        else:
            new = new + dn1_in[rows, :]
        dn1_ref[rows, :] = new
    if last:
        gg = jnp.zeros((8, D), F32)
        for t in range(4):
            rows = pl.ds(256 * t, 256)
            x = x_ref[rows, :].astype(F32)
            r = lax.rsqrt(jnp.mean(x * x, axis=-1, keepdims=True) + EPS)
            gg = gg + jnp.sum((dn1_ref[rows, :] * (x * r)).reshape(32, 8, D), axis=0)
        gg_ref[...] = jnp.broadcast_to(jnp.sum(gg, axis=0, keepdims=True), (8, D))


def rest_back(first, last, lengths, n1, dhb, w, wo, *more, deps=()):
    o = sds((T, D), F32)
    return call(functools.partial(rest_back_body, first, last), (o, sds((8, D), F32)) if last else o, 4 + len(more), 1,
                [pltpu.VMEM((HALF, D), BF16)], 6e9, 1e7)(lengths, n1, dhb, w, wo, *more, deps=deps)


def middle_body(pos_ref, x_ref, oo, oa, ob, oc, od, wo_own, wo_mine, wo_other, wq, wk, wv, gain_ref,
                h_ref, n2_ref, wo_l, wo_r, wo_x, qkv_ref, buf):
    core = pos_ref[1]
    for n, ref in enumerate((wo_l, wo_r, wo_x)):
        shard = pl.ds(96 * n, 96)
        buf[pl.ds(pl.multiple_of(core * 96, 32), 96), :] = wo_mine[shard, :]
        buf[pl.ds(pl.multiple_of((1 - core) * 96, 32), 96), :] = wo_other[shard, :]
        ref[0:192, :] = buf[0:192, :].astype(BF16)
        ref[192:256, :] = jnp.zeros((64, D), BF16)
    for t in range(4):
        rows = pl.ds(256 * t, 256)
        h = x_ref[rows, :].astype(F32) + tn(oo[:, rows].astype(BF16), wo_own[...])
        h = h + tn(oa[:, rows].astype(BF16), wo_l[0:192, :])
        h = h + tn(ob[:, rows].astype(BF16), wo_r[0:192, :])
        h = h + tn(oc[:, rows].astype(BF16), wo_x[0:96, :]) + tn(od[:, rows].astype(BF16), wo_x[96:192, :])
        h_ref[rows, :] = h
        f = lax.rsqrt(jnp.mean(h * h, axis=-1, keepdims=True) + EPS)
        n2_ref[rows, :] = (h * f * gain_ref[...].reshape(1, D)).astype(BF16)
    @pl.when(core == 0)
    def _():
        qkv_ref[0:192, :] = wq[...].astype(F32)
        qkv_ref[192:288, :] = wk[0:96, :].astype(F32)

    @pl.when(core == 1)
    def _():
        qkv_ref[0:96, :] = wk[96:192, :].astype(F32)
        qkv_ref[96:288, :] = wv[...].astype(F32)


def middle(pos, xr, os, wo, wo_mine, wo_other, wq, wk, wv, gain, deps=()):
    w = sds((256, D), BF16)
    return call(middle_body, (sds((T, D), F32), sds((T, D), BF16), w, w, w, sds((288, D), F32)), 13, 1,
                [pltpu.VMEM((192, D), F32)], 1.2e9, 8e6, 20)(
        pos, xr, *os, wo, wo_mine, wo_other, wq, wk, wv, gain, deps=deps)


def qkv_body(pos_ref, mine, other, out_l, out_r, out_x, buf):
    core = pos_ref[1]
    for r, ref in enumerate((out_l, out_r, out_x)):
        buf[pl.ds(pl.multiple_of(core * 288, 32), 288), :] = mine[288 * r : 288 * r + 288, :]
        buf[pl.ds(pl.multiple_of((1 - core) * 288, 32), 288), :] = other[288 * r : 288 * r + 288, :]
        for n in range(3):
            ref[256 * n : 256 * n + 192, :] = buf[192 * n : 192 * n + 192, :].astype(BF16)
            ref[256 * n + 192 : 256 * n + 256, :] = jnp.zeros((64, D), BF16)


def qkv_shards(pos, mine, other, deps=()):
    o = sds((D, D), BF16)
    return call(qkv_body, (o, o, o), 2, 1, [pltpu.VMEM((576, D), F32)], 1e6, 1e7)(pos, mine, other, deps=deps)


C1 = 0.7978845608028654
C2 = 0.044715 * C1


def ffn_math(gate, up, dhid):
    u2 = gate * gate
    t = jnp.tanh(gate * (C1 + C2 * u2))
    hp = 0.5 + 0.5 * t
    g = gate * hp
    slope = hp + g * (1.0 - t) * (C1 + 3.0 * C2 * u2)
    return (g * up).astype(BF16), (dhid * up * slope).astype(BF16), (dhid * g).astype(BF16)


def ffn_own_body(pos_ref, n2_ref, dy_ref, wg_ref, wu_ref, wd_ref, f_ref, dn2_ref, keep_ref, send_ref, hid, dgu, g_ref):
    for t in range(4):
        rows = pl.ds(256 * t, 256)
        n2, dy = n2_ref[rows, :], dy_ref[rows, :]
        gate = nn(n2, wg_ref[...])
        up = nn(n2, wu_ref[...])
        dh = nt(dy, wd_ref[...])
        a, b, c = ffn_math(gate, up, dh)
        hid[rows, :] = a
        dgu[rows, 0:512] = b
        dgu[rows, 512:1024] = c
        f_ref[rows, :] = nn(a, wd_ref[...])
        dn2_ref[rows, :] = nt(b, wg_ref[...]) + nt(c, wu_ref[...])
    for t in range(3):
        cols = pl.ds(256 * t, 256)
        g_ref[cols, 0:1024] = tn(n2_ref[:, cols], dgu[...])
        g_ref[cols, 1024:1536] = tn(dy_ref[:, cols], hid[...])
    split_rows(pos_ref, g_ref, keep_ref, send_ref)


def ffn_own(pos, n2, dy, wg, wu, wd, deps=()):
    o, g = sds((T, D), F32), sds((384, 1536), F32)
    return call(ffn_own_body, (o, o, g, g), 5, 1,
                [pltpu.VMEM((T, UN), BF16), pltpu.VMEM((T, 1024), BF16), pltpu.VMEM((D, 1536), F32)], 7.2e9, 1.6e7)(
        pos, n2, dy, wg, wu, wd, deps=deps)


def ffn_rest_body(pos_ref, n2_ref, dy_ref, f_in, dn2_in, w_ref, f_ref, dn2_ref, buf, wb, sems):
    me = pos_ref[0]

    def fetch(step, slot):
        first = lax.rem(me + 1 + step // 2, 4) * 1536 + lax.rem(step, 2) * 768
        return pltpu.make_async_copy(w_ref.at[pl.ds(pl.multiple_of(first, 768), 768), :], buf.at[slot], sems.at[slot])

    fetch(0, 0).start()

    def body(step, carry):
        slot = lax.rem(step, 2)

        @pl.when(step < 5)
        def _():
            fetch(step + 1, 1 - slot).start()

        fetch(step, slot).wait()
        for p in range(16):
            for m in range(3):
                wb[m, pl.ds(16 * p, 16), :] = buf[slot, pl.ds(48 * p + 16 * m, 16), :].astype(BF16)
        for t in range(4):
            rows = pl.ds(256 * t, 256)
            n2, dy = n2_ref[rows, :], dy_ref[rows, :]
            a, b, c = ffn_math(nt(n2, wb[0]), nt(n2, wb[1]), nt(dy, wb[2]))
            f_ref[rows, :] = f_ref[rows, :] + nn(a, wb[2])
            dn2_ref[rows, :] = dn2_ref[rows, :] + (nn(b, wb[0]) + nn(c, wb[1]))
        return carry

    lax.fori_loop(0, 6, body, 0)


def ffn_rest(pos, n2, dy, f, dn2, w, deps=()):
    o = sds((T, D), F32)
    scratch = [pltpu.VMEM((2, 768, D), F32), pltpu.VMEM((3, 256, D), BF16), pltpu.SemaphoreType.DMA((2,))]
    return call(ffn_rest_body, (o, o), 4, 1, scratch, 12 * T * D * 1536, 2e7, 16, alias={3: 0, 4: 1})(
        pos, n2, dy, f, dn2, far=[w], deps=deps)


def dh_body(h_ref, dn2_ref, dy_ref, gain_ref, dh_ref, dhb_ref, gg_ref):
    gg = jnp.zeros((8, D), F32)
    for t in range(4):
        rows = pl.ds(256 * t, 256)
        h = h_ref[rows, :]
        r = lax.rsqrt(jnp.mean(h * h, axis=-1, keepdims=True) + EPS)
        b = h * r
        dn2 = dn2_ref[rows, :]
        gg = gg + jnp.sum((dn2 * b).reshape(32, 8, D), axis=0)
        e = dn2 * gain_ref[...].reshape(1, D)
        dh = dy_ref[rows, :].astype(F32) + r * (e - b * jnp.mean(e * b, axis=-1, keepdims=True))
        dh_ref[rows, :] = dh
        dhb_ref[rows, :] = dh.astype(BF16)
    gg_ref[...] = jnp.broadcast_to(jnp.sum(gg, axis=0, keepdims=True), (8, D))


def dh_call(h, dn2, dy, gain, deps=()):
    return call(dh_body, (sds((T, D), F32), sds((T, D), BF16), sds((8, D), F32)), 4, 0, (), 2e7, 1.2e7)(
        h, dn2, dy, gain, deps=deps)


def unrotate(start, buf, out_ref, dtype):
    back = jnp.where(start > 0, T - start, 0)
    buf[pl.ds(T, 264), :] = buf[pl.ds(0, 264), :]
    for t in range(4):
        out_ref[pl.ds(256 * t, 256), :] = window(buf, back + 256 * t).astype(dtype)


def layer_body(len_ref, h_ref, f_ref, out_ref, tick_ref, buf):
    tick_ref[...] = jnp.zeros_like(tick_ref)
    for t in range(4):
        rows = pl.ds(256 * t, 256)
        buf[rows, :] = h_ref[rows, :] + f_ref[rows, :]
    unrotate(long_start(len_ref), buf, out_ref, BF16)


def layer_call(lengths, h, f, deps=()):
    return call(layer_body, (sds((T, D), BF16), sds((8, 128), F32)), 2, 1, [pltpu.VMEM((T + 264, D), F32)], 2e6, 8e6)(lengths, h, f, deps=deps)


def token_body(len_ref, x_ref, dh_ref, dn1_ref, gain_ref, out_ref, tick_ref, buf):
    tick_ref[...] = jnp.zeros_like(tick_ref)
    for t in range(4):
        rows = pl.ds(256 * t, 256)
        x = x_ref[rows, :].astype(F32)
        r = lax.rsqrt(jnp.mean(x * x, axis=-1, keepdims=True) + EPS)
        b = x * r
        e = dn1_ref[rows, :] * gain_ref[...].reshape(1, D)
        buf[rows, :] = dh_ref[rows, :] + r * (e - b * jnp.mean(e * b, axis=-1, keepdims=True))
    unrotate(long_start(len_ref), buf, out_ref, F32)


def token_call(lengths, xr, dh, dn1, gain, deps=()):
    return call(token_body, (sds((T, D), F32), sds((8, 128), F32)), 4, 1, [pltpu.VMEM((T + 264, D), F32)], 2e7, 1.2e7)(lengths, xr, dh, dn1, gain, deps=deps)


RING = 4


def x_shift(v, step):
    return lax.ppermute(v, "tensor", [(i, (i + step) % RING) for i in range(RING)])


def dp_table(move):
    table = []
    for y in range(RING):
        for z in range(RING):
            for c in range(2):
                to_y, to_z, to_c = move(y, z, c)
                table.append(((y * RING + z) * 2 + c, (to_y % RING * RING + to_z % RING) * 2 + to_c))
    return table


def a_shift(v, step):
    return lax.ppermute(v, "dp", dp_table(lambda y, z, c: (y + step * (1 - c), z + step * c, c)))


def b_shift(v, step):
    return lax.ppermute(v, "dp", dp_table(lambda y, z, c: (y + step * c, z + step * (1 - c), c)))


def core_swap(v):
    return lax.ppermute(v, "dp", dp_table(lambda y, z, c: (y, z, 1 - c)))


def local(
    tokens,
    lengths,
    attn_gain,
    query_weight,
    key_weight,
    value_weight,
    output_weight,
    ffn_gain,
    gate_weight,
    up_weight,
    down_weight,
    cotangent,
):
    x = lax.axis_index("tensor").astype(jnp.int32)
    d = lax.axis_index("dp").astype(jnp.int32)
    core, y, z = d % 2, d // 8, d // 2 % 4
    ja, jb = jnp.where(core == 0, y, z), jnp.where(core == 0, z, y)
    pos = jnp.stack([x, core, ja, jb, d])
    wq, wk, wv = query_weight.T, key_weight.T, value_weight.T
    piece, wo_half = pack(pos, output_weight, gate_weight, up_weight, down_weight)
    ffn_weights = lax.all_gather(piece, ("tensor", "dp"), axis=0, tiled=True)
    near = [x_shift(wo_half, 1), x_shift(wo_half, -1), x_shift(wo_half, 2)]
    xr, n1, dyr = prep(lengths, tokens, cotangent, attn_gain, deps=[piece])
    q, k, v, o, ot, lse = attn(lengths, n1, wq, wk, wv)
    oa, ob = x_shift(ot, 1), x_shift(ot, -1)
    wo_mine = cat(*near, deps=[ot])
    wo_other = core_swap(wo_mine)
    os = (ot, oa, ob, x_shift(oa[:96], 1), x_shift(ob[96:], -1))
    h, n2, wo_l, wo_r, wo_x, qkv_half = middle(pos, xr, os, output_weight, wo_mine, wo_other, wq, wk, wv, ffn_gain)

    qkv_mine = (x_shift(qkv_half, 1), x_shift(qkv_half, -1), x_shift(qkv_half, 2))
    f, dn2, ffn_keep, send = ffn_own(pos, n2, dyr, gate_weight, up_weight, down_weight)
    ffn_got = core_swap(send)
    f, dn2 = ffn_rest(pos, n2, dyr, f, dn2, ffn_weights)
    own, right, opposite, left = add_split(ffn_keep, ffn_got, deps=[f])
    qkv_mine = cat(*qkv_mine, deps=[f])
    ffn_got = (a_shift(left, -1), a_shift(right, 1), a_shift(opposite, 2))
    qkv_other = core_swap(qkv_mine)
    dh, dhb, gain_two = dh_call(h, dn2, dyr, ffn_gain, deps=[own, qkv_mine])
    keep, send, dqkv = own_back(lengths, pos, dhb, output_weight, q, k, v, lse, n1, o)
    own, right, opposite, left = add_split(own, *ffn_got, deps=[keep])
    ffn_got = (b_shift(left, -1), b_shift(right, 1), b_shift(opposite, 2))
    got = core_swap(send)
    w_l, w_r, w_x = qkv_shards(pos, qkv_mine, qkv_other, deps=[own])
    dn1 = rest_back(True, False, lengths, n1, dhb, w_l, wo_l, dqkv, wq, wk, wv)
    ffn_sum = add_four(own, *ffn_got, deps=[dn1])
    ffn_sums = lax.all_gather(ffn_sum, "dp", axis=0, tiled=True)
    own, right, opposite, left = add_split(keep, got, deps=[dn1])
    got = (a_shift(left, -1), a_shift(right, 1), a_shift(opposite, 2))
    dn1 = rest_back(False, False, lengths, n1, dhb, w_r, wo_r, dn1, deps=[own, ffn_sum])
    own, right, opposite, left = add_split(own, *got, deps=[dn1])
    got = (b_shift(left, -1), b_shift(right, 1), b_shift(opposite, 2))
    dn1, gain_one = rest_back(False, True, lengths, n1, dhb, w_x, wo_x, dn1, xr, deps=[own])
    own = add_four(own, *got, gain_one, gain_two)
    got = (b_shift(own, 1), b_shift(own, -1), b_shift(own, 2))
    token_grad, tick = token_call(lengths, xr, dh, dn1, attn_gain, deps=[own])
    own = cat_sum(own, *got, deps=[tick])
    got = (a_shift(own, 1), a_shift(own, -1), a_shift(own, 2))
    layer_out, tick = layer_call(lengths, h, f, deps=[own])
    own = cat_sum(own, *got, deps=[tick])
    other = core_swap(own)
    gate_grad, up_grad, down_grad = unpack_ffn(ffn_sums, deps=[own])
    query_grad, key_grad, value_grad, output_grad, attn_gain_grad, ffn_gain_grad = unpack_attn(pos, own, other)
    return (
        layer_out,
        token_grad,
        attn_gain_grad,
        query_grad.T,
        key_grad.T,
        value_grad.T,
        output_grad,
        ffn_gain_grad,
        gate_grad,
        up_grad,
        down_grad,
    )


def solution(mesh):
    placed = (
        P("dp", None),
        P("dp", None),
        P(),
        P(None, "tensor"),
        P(None, "tensor"),
        P(None, "tensor"),
        P("tensor", None),
        P(),
        P(None, "tensor"),
        P(None, "tensor"),
        P("tensor", None),
        P("dp", None),
    )
    return jax.shard_map(
        local,
        mesh=mesh,
        in_specs=placed,
        out_specs=(
            P("dp", None),
            P("dp", None),
            P(),
            P(None, "tensor"),
            P(None, "tensor"),
            P(None, "tensor"),
            P("tensor", None),
            P(),
            P(None, "tensor"),
            P(None, "tensor"),
            P("tensor", None),
        ),
        check_vma=False,
    )
```

```python
import functools
import jax
import jax.numpy as jnp
from jax import lax
from jax.experimental import pallas as pl
from jax.experimental.pallas import tpu as pltpu
from jax.sharding import PartitionSpec as P

T = 1024
D = 768
HALF = 512
HW = 192
UN = 512
EPS = 1e-06
LIGHT = 20
F32 = jnp.float32
BF16 = jnp.bfloat16
VM = pl.BlockSpec(memory_space=pltpu.VMEM)
SM = pl.BlockSpec(memory_space=pltpu.SMEM)


ANY = pl.BlockSpec(memory_space=pl.ANY)
FAR = pl.BlockSpec(memory_space=pltpu.HBM)


def call(body, out_shape, n_vmem, smem=0, scratch=(), flops=0, bytes_accessed=0, limit=12, alias={}, near=True):
    def run(*args, deps=(), far=()):
        deps = [d for d in deps if d is not None]
        n = smem + n_vmem + len(far)

        def inner(*refs):
            body(*refs[:n], *refs[n + len(deps) :])

        args = [
            *args[:smem],
            *(pltpu.with_memory_space_constraint(v, pltpu.VMEM) for v in args[smem:]),
            *(pltpu.with_memory_space_constraint(v, pltpu.HBM) for v in far),
        ]
        return pl.pallas_call(
            inner,
            out_shape=jax.tree.map(lambda s: pltpu.VMEM(s.shape, s.dtype), out_shape) if near else out_shape,
            in_specs=[SM] * smem + [VM] * n_vmem + [FAR] * len(far) + [ANY] * len(deps),
            out_specs=jax.tree.map(lambda _: VM, out_shape),
            scratch_shapes=list(scratch),
            input_output_aliases=alias,
            compiler_params=pltpu.CompilerParams(vmem_limit_bytes=limit << 20),
            cost_estimate=pl.CostEstimate(flops=int(flops) // LIGHT, bytes_accessed=int(bytes_accessed) // LIGHT, transcendentals=0),
        )(*args, *deps)

    return run


def sds(shape, dtype):
    return jax.ShapeDtypeStruct(shape, dtype)


def nn(a, b):
    return jnp.dot(a, b, preferred_element_type=F32)


def nt(a, b):
    return lax.dot_general(a, b, (((1,), (1,)), ((), ())), preferred_element_type=F32)


def tn(a, b):
    return lax.dot_general(a, b, (((0,), (0,)), ((), ())), preferred_element_type=F32)


def long_start(len_ref):
    start, acc = jnp.int32(0), jnp.int32(0)
    for k in range(8):
        n = len_ref[0, k]
        start = jnp.where(n == HALF, acc, start)
        acc = acc + n
    return start


def rest_mask(len_ref):
    start = long_start(len_ref)

    def ids(shape, dim):
        place = lax.broadcasted_iota(jnp.int32, shape, dim) + (HALF + start)
        place = jnp.where(place >= T, place - T, place)
        end, got = jnp.int32(0), jnp.zeros(shape, jnp.int32)
        for k in range(7):
            end = end + len_ref[0, k]
            got = got + (place >= end).astype(jnp.int32)
        return got

    return ids((HALF, 1), 0) == ids((1, HALF), 1)


def window(buf, first):
    first = jnp.where(first >= T, first - T, first)
    base = pl.multiple_of(first // 8 * 8, 8)
    n = first - base
    v = pltpu.roll(buf[pl.ds(base, 264), :].reshape(33, 8, D), lax.rem(8 - n, 8), 1)
    row = lax.broadcasted_iota(jnp.int32, (1, 8, 1), 1)
    return jnp.where(row < 8 - n, v[0:32], v[1:33]).reshape(256, D)


def pack_body(pos_ref, wo_ref, wg_ref, wu_ref, wd_ref, out_ref, half_ref, cols, rows, half, sems):
    core, d = pos_ref[1], pos_ref[4]
    lanes = pl.ds(pl.multiple_of(d // 8 * 128, 128), 128)
    units = pl.ds(pl.multiple_of(d * 16, 16), 16)
    copies = (
        pltpu.make_async_copy(wg_ref.at[:, lanes], cols.at[0], sems.at[0]),
        pltpu.make_async_copy(wu_ref.at[:, lanes], cols.at[1], sems.at[1]),
        pltpu.make_async_copy(wd_ref.at[units, :], rows, sems.at[2]),
        pltpu.make_async_copy(wo_ref.at[pl.ds(pl.multiple_of(core * 96, 32), 96), :], half, sems.at[3]),
    )
    for copy in copies:
        copy.start()
    for copy in copies:
        copy.wait()
    half_ref[...] = half[...].astype(F32)
    for m in range(2):
        tmp = cols[m].astype(F32).T
        out_ref[pl.ds(16 * m, 16), :] = pick_rows(tmp, lax.rem(d, 8))
    out_ref[32:48, :] = rows[...].astype(F32)


def pick_rows(v, n):
    out = v[0:16]
    for k in range(1, 8):
        out = jnp.where(n == k, v[16 * k : 16 * k + 16], out)
    return out


def pack(pos, *weights):
    scratch = [pltpu.VMEM((2, D, 128), BF16), pltpu.VMEM((16, D), BF16), pltpu.VMEM((96, D), BF16), pltpu.SemaphoreType.DMA((4,))]
    return call(pack_body, (sds((48, D), F32), sds((96, D), F32)), 0, 1, scratch, 1e6, 1e6)(pos, far=weights)


def cat_body(*refs):
    out, at = refs[-1], 0
    for ref in refs[:-1]:
        out[pl.ds(at, ref.shape[0]), :] = ref[...]
        at += ref.shape[0]


def cat(*parts, deps=()):
    shape = (sum(p.shape[0] for p in parts), parts[0].shape[1])
    return call(cat_body, sds(shape, F32), len(parts), 0, (), 1e5, 8 * shape[0] * shape[1])(*parts, deps=deps)


def cat_rows_body(first, count, *refs):
    out = refs[-1]
    for n, ref in enumerate(refs[:-1]):
        out[pl.ds(count * n, count), :] = ref[first : first + count, :]


def cat_rows(first, count, *parts, deps=()):
    shape = (count * len(parts), parts[0].shape[1])
    return call(functools.partial(cat_rows_body, first, count), sds(shape, F32), len(parts), 0, (), 1e5, 8 * shape[0] * shape[1])(
        *parts, deps=deps)


def cat_sum_body(size, *refs):
    out, parts = refs[-1], refs[:-1]
    for n, ref in enumerate(parts):
        out[pl.ds(size * n, size), :] = ref[0:size, :]
    own, left, right, opposite = [ref[size : size + 8, :] for ref in parts]
    out[pl.ds(4 * size, 8), :] = (own + opposite) + (left + right)


def cat_sum(*parts, deps=()):
    size = parts[0].shape[0] - 8
    return call(functools.partial(cat_sum_body, size), sds((4 * size + 8, D), F32), 4, 0, (), 1e5, 32e3 * size)(
        *parts, deps=deps)


def piece_row(core, ja, jb):
    return pl.multiple_of(jnp.where(core == 0, ja * 4 + jb, jb * 4 + ja) * 48 + core * 24, 8)


def unpack_ffn_body(g_ref, wg_ref, wu_ref, wd_ref, buf, sems):
    copies = [pltpu.make_async_copy(g_ref.at[pl.ds(256 * n, 256), :], buf.at[n], sems.at[n]) for n in range(3)]
    for copy in copies:
        copy.start()
    for n, copy in enumerate(copies):
        rows = pl.ds(256 * n, 256)
        copy.wait()
        wg_ref[rows, :] = buf[n, :, 0:512]
        wu_ref[rows, :] = buf[n, :, 512:1024]
        wd_ref[:, rows] = buf[n, :, 1024:1536].T


def unpack_ffn(g, deps=()):
    return call(unpack_ffn_body, (sds((D, UN), F32), sds((D, UN), F32), sds((UN, D), F32)), 0, 0,
                [pltpu.VMEM((3, 256, 1536), F32), pltpu.SemaphoreType.DMA((3,))], 1e6, 1e7, near=False)(far=[g], deps=deps)


def unpack_attn_body(pos_ref, mine, other, wq_ref, wk_ref, wv_ref, wo_ref, one_ref, two_ref, buf):
    core, ja, jb = pos_ref[1], pos_ref[2], pos_ref[3]
    for ref, c, a, b in ((mine, core, ja, jb), (other, 1 - core, jb, ja)):
        for m, sa in enumerate((0, 3, 1, 2)):
            for n, sb in enumerate((0, 3, 1, 2)):
                row = piece_row(c, lax.rem(a + sa, 4), lax.rem(b + sb, 4))
                buf[pl.ds(row, 24), :] = ref[pl.ds(96 * m + 24 * n, 24), :]
    for n, out in enumerate((wq_ref, wk_ref, wv_ref, wo_ref)):
        out[...] = buf[192 * n : 192 * n + 192, :]
    gains = mine[384:392, :] + other[384:392, :]
    one_ref[...] = gains[0].reshape(D)
    two_ref[...] = gains[1].reshape(D)


def unpack_attn(pos, mine, other, deps=()):
    o, g = sds((HW, D), F32), sds((D,), F32)
    return call(unpack_attn_body, (o, o, o, o, g, g), 2, 1, [pltpu.VMEM((D, D), F32)], 1e6, 5e6, near=False)(pos, mine, other, deps=deps)


def split_rows(pos_ref, buf, keep_ref, send_ref):
    core, ja, jb = pos_ref[1], pos_ref[2], pos_ref[3]
    for out, half, a, b in ((keep_ref, core, ja, jb), (send_ref, 1 - core, jb, ja)):
        for sa in range(4):
            for sb in range(4):
                row = piece_row(half, lax.rem(a + sa, 4), lax.rem(b + sb, 4))
                out[pl.ds(96 * sa + 24 * sb, 24), :] = buf[pl.ds(row, 24), :]


def add_split_body(*refs):
    ins, outs = refs[:-4], refs[-4:]
    size = outs[0].shape[0]
    for n, out in enumerate(outs):
        rows = pl.ds(size * n, size)
        if len(ins) == 2:
            out[...] = ins[0][rows, :] + ins[1][rows, :]
        else:
            own, left, right, opposite = ins
            out[...] = (own[rows, :] + opposite[rows, :]) + (left[rows, :] + right[rows, :])


def add_split(*ins, deps=()):
    rows, lanes = ins[0].shape
    o = sds((rows // 4, lanes), F32)
    return call(add_split_body, (o,) * 4, len(ins), 0, (), rows * lanes * 2, rows * lanes * 12, 12)(*ins, deps=deps)


def add_body(own, left, right, opposite, *refs):
    out = refs[-1]
    rows = own.shape[0]
    out[0:rows, :] = (own[...] + opposite[...]) + (left[...] + right[...])
    if len(refs) > 1:
        row = lax.broadcasted_iota(jnp.int32, (8, 1), 0)
        out[rows : rows + 8, :] = jnp.where(row == 0, refs[0][...], jnp.where(row == 1, refs[1][...], 0.0))


def add_four(*ins, deps=()):
    rows, lanes = ins[0].shape
    out = sds((rows + (8 if len(ins) > 4 else 0), lanes), F32)
    return call(add_body, out, len(ins), 0, (), 1e5, 1e6)(*ins, deps=deps)


def prep_body(len_ref, x_ref, dy_ref, gain_ref, xr_ref, n1_ref, dyr_ref, buf):
    start = long_start(len_ref)

    def fill(src):
        for t in range(4):
            buf[pl.ds(256 * t, 256), :] = src[pl.ds(256 * t, 256), :].astype(F32)
        buf[pl.ds(T, 264), :] = buf[pl.ds(0, 264), :]

    def piece(t):
        return window(buf, start + 256 * t)

    fill(x_ref)
    for t in range(4):
        x = piece(t)
        xr_ref[pl.ds(256 * t, 256), :] = x.astype(BF16)
        r = lax.rsqrt(jnp.mean(x * x, axis=-1, keepdims=True) + EPS)
        n1_ref[pl.ds(256 * t, 256), :] = (x * r * gain_ref[...].reshape(1, D)).astype(BF16)
    fill(dy_ref)
    for t in range(4):
        dyr_ref[pl.ds(256 * t, 256), :] = piece(t).astype(BF16)


def prep(lengths, tokens, cot, gain, deps=()):
    o = sds((T, D), BF16)
    return call(prep_body, (o, o, o), 3, 1, [pltpu.VMEM((T + 264, D), F32)], 6e6, 8e6)(
        lengths, tokens, cot, gain, deps=deps
    )


def head_mask(h):
    lane = lax.broadcasted_iota(jnp.int32, (1, HW), 1)
    return (lane >= 64 * h) & (lane < 64 * h + 64)


def only(v, h):
    return jnp.where(head_mask(h), v, jnp.zeros_like(v))


def attn_body(len_ref, n1_ref, wq_ref, wk_ref, wv_ref, q_ref, k_ref, v_ref, o_ref, ot_ref, lse_ref):
    mask = rest_mask(len_ref)
    for i in range(2):
        rows = pl.ds(HALF * i, HALF)
        n1 = n1_ref[rows, :]
        q = (nt(n1, wq_ref[...]).astype(BF16).astype(F32) * 0.125).astype(BF16)
        k = nt(n1, wk_ref[...]).astype(BF16)
        v = nt(n1, wv_ref[...]).astype(BF16)
        q_ref[rows, :] = q
        k_ref[rows, :] = k
        v_ref[rows, :] = v
        vt = v.T
        outs = []
        for h in range(3):
            s = nt(k, only(q, h))
            if i == 1:
                s = jnp.where(mask, s, -1e30)
            top = jnp.max(s, axis=0, keepdims=True)
            e = jnp.exp(s - top)
            total = jnp.sum(e, axis=0, keepdims=True)
            lse_ref[pl.ds(h, 1), rows] = top + jnp.log(total)
            o = nn(vt[64 * h : 64 * h + 64, :], e.astype(BF16))
            outs.append(o * (1.0 / total))
        o = jnp.concatenate(outs, axis=0).astype(BF16)
        ot_ref[:, rows] = o.astype(F32)
        o_ref[rows, :] = o.T


def attn(lengths, n1, wq, wk, wv, deps=()):
    b = sds((T, HW), BF16)
    return call(attn_body, (b, b, b, b, sds((HW, T), F32), sds((8, T), F32)), 4, 1, (), 4e9, 4e6)(
        lengths, n1, wq, wk, wv, deps=deps
    )


def heads_back(i, mask, q, k, v, do, lse):
    lane = lax.broadcasted_iota(jnp.int32, (1, 256), 1)
    head = [(lane >= 64 * h) & (lane < 64 * h + 64) for h in range(3)]
    each = lambda t: jnp.concatenate([jnp.where(m, t, jnp.zeros_like(t)) for m in head], axis=0)
    s_all = nt(each(k), q)
    dp_all = nt(each(v), do)
    kt = k.T
    ps, dss, dqt = [], [], []
    for h in range(3):
        s = s_all[HALF * h : HALF * h + HALF]
        dp = dp_all[HALF * h : HALF * h + HALF]
        if i == 1:
            s = jnp.where(mask, s, -1e30)
        if lse is None:
            e = jnp.exp(s - jnp.max(s, axis=0, keepdims=True))
            p = e * (1.0 / jnp.sum(e, axis=0, keepdims=True))
        else:
            p = jnp.exp(s - lse[h : h + 1, :])
        ds = (p * (dp - jnp.sum(p * dp, axis=0, keepdims=True))).astype(BF16)
        ps.append(p.astype(BF16))
        dss.append(ds)
        dqt.append(nn(kt[64 * h : 64 * h + 64, :], ds))
    dq = (jnp.concatenate(dqt + [jnp.zeros((64, HALF), F32)], axis=0) * 0.125).T
    dv = nn(jnp.concatenate(ps, axis=0), do)
    dk = nn(jnp.concatenate(dss, axis=0), q)

    def pick(t):
        t = [t[HALF * h : HALF * h + HALF] for h in range(3)]
        t = jnp.where(head[0], t[0], jnp.where(head[1], t[1], t[2]))
        return jnp.where(lane < HW, t, 0.0).astype(BF16)

    return dq.astype(BF16), pick(dk), pick(dv)


def padded(t):
    return jnp.concatenate([t, jnp.zeros((t.shape[0], 256 - t.shape[1]), t.dtype)], axis=1)


def own_back_body(len_ref, pos_ref, dhb_ref, wo_ref, q_ref, k_ref, v_ref, lse_ref, n1_ref, o_ref,
                  keep_ref, send_ref, d_ref, g_ref):
    mask = rest_mask(len_ref)
    for i in range(2):
        rows = pl.ds(HALF * i, HALF)
        do = padded(nt(dhb_ref[rows, :], wo_ref[...]).astype(BF16))
        d = heads_back(i, mask, padded(q_ref[rows, :]), padded(k_ref[rows, :]), padded(v_ref[rows, :]), do, lse_ref[:, rows])
        for n in range(3):
            d_ref[rows, 256 * n : 256 * n + 256] = d[n]
    for n in range(3):
        g_ref[192 * n : 192 * n + 192, :] = tn(d_ref[:, 256 * n : 256 * n + 256], n1_ref[...])[0:192]
    g_ref[576:768, :] = tn(o_ref[...], dhb_ref[...])
    split_rows(pos_ref, g_ref, keep_ref, send_ref)


def own_back(lengths, pos, dhb, wo, q, k, v, lse, n1, o, deps=()):
    g = sds((384, D), F32)
    return call(own_back_body, (g, g, sds((T, D), BF16)), 8, 2, [pltpu.VMEM((D, D), F32)], 8e9, 9e6)(
        lengths, pos, dhb, wo, q, k, v, lse, n1, o, deps=deps)


def rest_back_body(r, len_ref, n1_ref, dhb_ref, w_ref, wo_ref, *refs):
    mask = rest_mask(len_ref)
    first, last = r == 0, r == 2
    if first:
        own_d, wq, wk, wv, dn1_ref, d = refs
    elif last:
        dn1_in, x_ref, dn1_ref, gg_ref, d = refs
    else:
        dn1_in, dn1_ref, d = refs
    for i in range(2):
        rows = pl.ds(HALF * i, HALF)
        qkv = nt(n1_ref[rows, :], w_ref[...])
        q = (qkv[:, 0:256].astype(BF16).astype(F32) * 0.125).astype(BF16)
        k = qkv[:, 256:512].astype(BF16)
        v = qkv[:, 512:768].astype(BF16)
        do = nt(dhb_ref[rows, :], wo_ref[...]).astype(BF16)
        for n, t in enumerate(heads_back(i, mask, q, k, v, do, None)):
            d[:, 256 * n : 256 * n + 256] = t
        new = nn(d[...], w_ref[...])
        if first:
            for n, w in enumerate((wq, wk, wv)):
                new = new + nn(own_d[rows, 256 * n : 256 * n + 192], w[...])
        else:
            new = new + dn1_in[rows, :]
        dn1_ref[rows, :] = new
    if last:
        gg = jnp.zeros((8, D), F32)
        for t in range(4):
            rows = pl.ds(256 * t, 256)
            x = x_ref[rows, :].astype(F32)
            r = lax.rsqrt(jnp.mean(x * x, axis=-1, keepdims=True) + EPS)
            gg = gg + jnp.sum((dn1_ref[rows, :] * (x * r)).reshape(32, 8, D), axis=0)
        gg_ref[...] = jnp.broadcast_to(jnp.sum(gg, axis=0, keepdims=True), (8, D))


def rest_back(r, lengths, n1, dhb, w, wo, *more, deps=()):
    o = sds((T, D), F32)
    return call(functools.partial(rest_back_body, r), (o, sds((8, D), F32)) if r == 2 else o, 4 + len(more), 1,
                [pltpu.VMEM((HALF, D), BF16)], 6e9, 1e7)(lengths, n1, dhb, w, wo, *more, deps=deps)


def middle_body(pos_ref, x_ref, oo, oa, ob, oc, od, wo_own, wo_mine, wo_other, gain_ref,
                h_ref, n2_ref, wo_l, wo_r, wo_x, buf):
    core = pos_ref[1]
    for n, ref in enumerate((wo_l, wo_r, wo_x)):
        shard = pl.ds(96 * n, 96)
        buf[pl.ds(pl.multiple_of(core * 96, 32), 96), :] = wo_mine[shard, :]
        buf[pl.ds(pl.multiple_of((1 - core) * 96, 32), 96), :] = wo_other[shard, :]
        ref[0:192, :] = buf[0:192, :].astype(BF16)
        ref[192:256, :] = jnp.zeros((64, D), BF16)
    for t in range(4):
        rows = pl.ds(256 * t, 256)
        h = x_ref[rows, :].astype(F32) + tn(oo[:, rows].astype(BF16), wo_own[...])
        h = h + tn(oa[:, rows].astype(BF16), wo_l[0:192, :])
        h = h + tn(ob[:, rows].astype(BF16), wo_r[0:192, :])
        h = h + tn(oc[:, rows].astype(BF16), wo_x[0:96, :]) + tn(od[:, rows].astype(BF16), wo_x[96:192, :])
        h_ref[rows, :] = h
        f = lax.rsqrt(jnp.mean(h * h, axis=-1, keepdims=True) + EPS)
        n2_ref[rows, :] = (h * f * gain_ref[...].reshape(1, D)).astype(BF16)


def middle(pos, xr, os, wo, wo_mine, wo_other, gain, deps=()):
    w = sds((256, D), BF16)
    return call(middle_body, (sds((T, D), F32), sds((T, D), BF16), w, w, w), 10, 1,
                [pltpu.VMEM((192, D), F32)], 1.2e9, 8e6)(pos, xr, *os, wo, wo_mine, wo_other, gain, deps=deps)


def half_body(pos_ref, wq, wk, wv, out_ref, buf, sems):
    core = pos_ref[1]
    copies = [pltpu.make_async_copy(src, buf.at[pl.ds(192 * n, 192), :], sems.at[n]) for n, src in enumerate((wq, wk, wv))]
    for copy in copies:
        copy.start()
    for copy in copies:
        copy.wait()
    out_ref[...] = buf[pl.ds(pl.multiple_of(core * 288, 32), 288), :].astype(F32)


def qkv_half(pos, wq, wk, wv, deps=()):
    return call(half_body, sds((288, D), F32), 0, 1, [pltpu.VMEM((576, D), BF16), pltpu.SemaphoreType.DMA((3,))], 1e6, 2e6)(
        pos, far=(wq, wk, wv), deps=deps)


def qkv_body(pos_ref, mine, other, *refs):
    core, buf = pos_ref[1], refs[-1]
    for r, out in enumerate(refs[:-1]):
        buf[pl.ds(pl.multiple_of(core * 288, 32), 288), :] = mine[288 * r : 288 * r + 288, :]
        buf[pl.ds(pl.multiple_of((1 - core) * 288, 32), 288), :] = other[288 * r : 288 * r + 288, :]
        for n in range(3):
            out[256 * n : 256 * n + 192, :] = buf[192 * n : 192 * n + 192, :].astype(BF16)
            out[256 * n + 192 : 256 * n + 256, :] = jnp.zeros((64, D), BF16)


def qkv_shard(pos, mine, other, deps=()):
    o = sds((D, D), BF16)
    return call(qkv_body, (o,) * (mine.shape[0] // 288), 2, 1, [pltpu.VMEM((576, D), F32)], 1e6, 3e6)(pos, mine, other, deps=deps)


C1 = 0.7978845608028654
C2 = 0.044715 * C1


def ffn_math(gate, up, dhid):
    u2 = gate * gate
    t = jnp.tanh(gate * (C1 + C2 * u2))
    hp = 0.5 + 0.5 * t
    g = gate * hp
    slope = hp + g * (1.0 - t) * (C1 + 3.0 * C2 * u2)
    return (g * up).astype(BF16), (dhid * up * slope).astype(BF16), (dhid * g).astype(BF16)


def ffn_own_body(pos_ref, n2_ref, dy_ref, wg_ref, wu_ref, wd_ref, f_ref, dn2_ref, keep_ref, send_ref, hid, dgu, g_ref):
    for t in range(4):
        rows = pl.ds(256 * t, 256)
        n2, dy = n2_ref[rows, :], dy_ref[rows, :]
        gate = nn(n2, wg_ref[...])
        up = nn(n2, wu_ref[...])
        dh = nt(dy, wd_ref[...])
        a, b, c = ffn_math(gate, up, dh)
        hid[rows, :] = a
        dgu[rows, 0:512] = b
        dgu[rows, 512:1024] = c
        f_ref[rows, :] = nn(a, wd_ref[...])
        dn2_ref[rows, :] = nt(b, wg_ref[...]) + nt(c, wu_ref[...])
    for t in range(3):
        cols = pl.ds(256 * t, 256)
        g_ref[cols, 0:1024] = tn(n2_ref[:, cols], dgu[...])
        g_ref[cols, 1024:1536] = tn(dy_ref[:, cols], hid[...])
    split_rows(pos_ref, g_ref, keep_ref, send_ref)


def ffn_own(pos, n2, dy, wg, wu, wd, deps=()):
    o, g = sds((T, D), F32), sds((384, 1536), F32)
    return call(ffn_own_body, (o, o, g, g), 5, 1,
                [pltpu.VMEM((T, UN), BF16), pltpu.VMEM((T, 1024), BF16), pltpu.VMEM((D, 1536), F32)], 7.2e9, 1.6e7)(
        pos, n2, dy, wg, wu, wd, deps=deps)


def ffn_rest_body(pos_ref, n2_far, dy_far, f_far, dn2_far, w_ref, f_ref, dn2_ref,
                  n2_ref, dy_ref, buf, wb, sems, in_sems):
    me = pos_ref[0]

    def fetch(r, half, slot):
        pieces = pl.ds(16 * half, 16)
        return pltpu.make_async_copy(
            w_ref.at[lax.rem(me + 1 + r, 4), pieces, :, :], buf.at[slot, pieces], sems.at[slot, half])

    ins = [pltpu.make_async_copy(src, dst, in_sems.at[n]) for n, (src, dst) in enumerate(
        ((n2_far, n2_ref), (dy_far, dy_ref), (f_far, f_ref), (dn2_far, dn2_ref)))]
    fetch(0, 0, 0).start()
    fetch(0, 1, 0).start()
    for copy in ins:
        copy.start()

    def step(r, carry):
        slot = lax.rem(r, 2)

        @pl.when(r < 2)
        def _():
            fetch(r + 1, 0, 1 - slot).start()
            fetch(r + 1, 1, 1 - slot).start()

        for half in range(2):
            fetch(r, half, slot).wait()
            for p in range(16 * half, 16 * half + 16):
                for m in range(3):
                    wb[m, pl.ds(16 * p, 16), :] = buf[slot, p, pl.ds(16 * m, 16), :].astype(BF16)

        @pl.when(r == 0)
        def _():
            for copy in ins:
                copy.wait()

        for t in range(4):
            rows = pl.ds(256 * t, 256)
            n2, dy = n2_ref[rows, :], dy_ref[rows, :]
            a, b, c = ffn_math(nt(n2, wb[0]), nt(n2, wb[1]), nt(dy, wb[2]))
            f_ref[rows, :] = f_ref[rows, :] + nn(a, wb[2])
            dn2_ref[rows, :] = dn2_ref[rows, :] + (nn(b, wb[0]) + nn(c, wb[1]))
        return carry

    lax.fori_loop(0, 3, step, 0)


def ffn_rest(pos, *far, deps=()):
    o = sds((T, D), F32)
    scratch = [pltpu.VMEM((T, D), BF16), pltpu.VMEM((T, D), BF16), pltpu.VMEM((2, 32, 48, D), F32), pltpu.VMEM((3, UN, D), BF16),
               pltpu.SemaphoreType.DMA((2, 2)), pltpu.SemaphoreType.DMA((4,))]
    return call(ffn_rest_body, (o, o), 0, 1, scratch, 12 * T * D * 1536, 2e7, 26)(pos, far=far, deps=deps)


def dh_body(h_ref, dn2_ref, dy_ref, gain_ref, dh_ref, dhb_ref, gg_ref):
    gg = jnp.zeros((8, D), F32)
    for t in range(4):
        rows = pl.ds(256 * t, 256)
        h = h_ref[rows, :]
        r = lax.rsqrt(jnp.mean(h * h, axis=-1, keepdims=True) + EPS)
        b = h * r
        dn2 = dn2_ref[rows, :]
        gg = gg + jnp.sum((dn2 * b).reshape(32, 8, D), axis=0)
        e = dn2 * gain_ref[...].reshape(1, D)
        dh = dy_ref[rows, :].astype(F32) + r * (e - b * jnp.mean(e * b, axis=-1, keepdims=True))
        dh_ref[rows, :] = dh
        dhb_ref[rows, :] = dh.astype(BF16)
    gg_ref[...] = jnp.broadcast_to(jnp.sum(gg, axis=0, keepdims=True), (8, D))


def dh_call(h, dn2, dy, gain, deps=()):
    return call(dh_body, (sds((T, D), F32), sds((T, D), BF16), sds((8, D), F32)), 4, 0, (), 2e7, 1.2e7)(
        h, dn2, dy, gain, deps=deps)


def unrotate(start, buf, out_ref, dtype):
    back = jnp.where(start > 0, T - start, 0)
    buf[pl.ds(T, 264), :] = buf[pl.ds(0, 264), :]
    for t in range(4):
        out_ref[pl.ds(256 * t, 256), :] = window(buf, back + 256 * t).astype(dtype)


def layer_body(len_ref, h_ref, f_ref, out_ref, tick_ref, buf):
    tick_ref[...] = jnp.zeros_like(tick_ref)
    for t in range(4):
        rows = pl.ds(256 * t, 256)
        buf[rows, :] = h_ref[rows, :] + f_ref[rows, :]
    unrotate(long_start(len_ref), buf, out_ref, BF16)


def layer_call(lengths, h, f, deps=()):
    return call(layer_body, (sds((T, D), BF16), sds((8, 128), F32)), 2, 1, [pltpu.VMEM((T + 264, D), F32)], 2e6, 8e6, near=False)(lengths, h, f, deps=deps)


def token_body(len_ref, x_ref, dh_ref, dn1_ref, gain_ref, out_ref, tick_ref, buf):
    tick_ref[...] = jnp.zeros_like(tick_ref)
    for t in range(4):
        rows = pl.ds(256 * t, 256)
        x = x_ref[rows, :].astype(F32)
        r = lax.rsqrt(jnp.mean(x * x, axis=-1, keepdims=True) + EPS)
        b = x * r
        e = dn1_ref[rows, :] * gain_ref[...].reshape(1, D)
        buf[rows, :] = dh_ref[rows, :] + r * (e - b * jnp.mean(e * b, axis=-1, keepdims=True))
    unrotate(long_start(len_ref), buf, out_ref, F32)


def token_call(lengths, xr, dh, dn1, gain, deps=()):
    return call(token_body, (sds((T, D), F32), sds((8, 128), F32)), 4, 1, [pltpu.VMEM((T + 264, D), F32)], 2e7, 1.2e7, near=False)(lengths, xr, dh, dn1, gain, deps=deps)


RING = 4


def x_shift(v, step):
    return lax.ppermute(v, "tensor", [(i, (i + step) % RING) for i in range(RING)])


def dp_table(move):
    table = []
    for y in range(RING):
        for z in range(RING):
            for c in range(2):
                to_y, to_z, to_c = move(y, z, c)
                table.append(((y * RING + z) * 2 + c, (to_y % RING * RING + to_z % RING) * 2 + to_c))
    return table


def a_shift(v, step):
    return lax.ppermute(v, "dp", dp_table(lambda y, z, c: (y + step * (1 - c), z + step * c, c)))


def b_shift(v, step):
    return lax.ppermute(v, "dp", dp_table(lambda y, z, c: (y + step * c, z + step * (1 - c), c)))


def core_swap(v):
    return lax.ppermute(v, "dp", dp_table(lambda y, z, c: (y, z, 1 - c)))


def local(
    tokens,
    lengths,
    attn_gain,
    query_weight,
    key_weight,
    value_weight,
    output_weight,
    ffn_gain,
    gate_weight,
    up_weight,
    down_weight,
    cotangent,
):
    x = lax.axis_index("tensor").astype(jnp.int32)
    d = lax.axis_index("dp").astype(jnp.int32)
    core, y, z = d % 2, d // 8, d // 2 % 4
    ja, jb = jnp.where(core == 0, y, z), jnp.where(core == 0, z, y)
    pos = jnp.stack([x, core, ja, jb, d])
    wq, wk, wv = query_weight.T, key_weight.T, value_weight.T
    piece, wo_half = pack(pos, output_weight, gate_weight, up_weight, down_weight)
    weights = lax.all_gather(piece, ("tensor", "dp"), axis=0, tiled=True).reshape(4, 32, 48, D)
    wo_mine = cat(x_shift(wo_half, 1), x_shift(wo_half, -1), x_shift(wo_half, 2))
    xr, n1, dyr = prep(lengths, tokens, cotangent, attn_gain, deps=[piece])
    q, k, v, o, ot, lse = attn(lengths, n1, wq, wk, wv, deps=[wo_mine])
    oa, ob = x_shift(ot, 1), x_shift(ot, -1)
    wo_other = core_swap(wo_mine)
    oc = x_shift(cat_rows(0, 96, oa, deps=[wo_mine]), 1)
    od = x_shift(cat_rows(96, 96, ob, deps=[wo_mine]), -1)
    h, n2, wo_l, wo_r, wo_x = middle(pos, xr, (ot, oa, ob, oc, od), output_weight, wo_mine, wo_other, ffn_gain)
    f, dn2, keep, send = ffn_own(pos, n2, dyr, gate_weight, up_weight, down_weight)
    half = qkv_half(pos, wq, wk, wv, deps=[send])
    ffn_keep, ffn_got = keep, core_swap(send)
    qkv_l, qkv_r = x_shift(half, 1), x_shift(half, -1)
    f, dn2 = ffn_rest(pos, n2, dyr, f, dn2, weights, deps=[half])

    own, right, opposite, left = add_split(ffn_keep, ffn_got, deps=[f])
    ffn_got = (a_shift(left, -1), a_shift(right, 1), a_shift(opposite, 2))
    qkv_near = cat(qkv_l, qkv_r, deps=[f])
    qkv_near_other = core_swap(qkv_near)
    qkv_x = x_shift(half, 2)
    dh, dhb, gain_two = dh_call(h, dn2, dyr, ffn_gain, deps=[own, qkv_near])
    keep, send, dqkv = own_back(lengths, pos, dhb, output_weight, q, k, v, lse, n1, o)

    ffn_part, right, opposite, left = add_split(own, *ffn_got, deps=[keep])
    ffn_got = (b_shift(left, -1), b_shift(right, 1), b_shift(opposite, 2))
    got = core_swap(send)
    w_l, w_r = qkv_shard(pos, qkv_near, qkv_near_other)
    dn1 = rest_back(0, lengths, n1, dhb, w_l, wo_l, dqkv, wq, wk, wv, deps=[ffn_part, qkv_x])
    ffn_sum = add_four(ffn_part, *ffn_got, deps=[dn1])
    ffn_sums = lax.all_gather(ffn_sum, "dp", axis=0, tiled=True)
    own, right, opposite, left = add_split(keep, got, deps=[dn1])
    got = (a_shift(left, -1), a_shift(right, 1), a_shift(opposite, 2))
    qkv_x_other = core_swap(qkv_x)
    dn1 = rest_back(1, lengths, n1, dhb, w_r, wo_r, dn1, deps=[own])
    own, right, opposite, left = add_split(own, *got, deps=[dn1])
    got = (b_shift(left, -1), b_shift(right, 1), b_shift(opposite, 2))
    (w_x,) = qkv_shard(pos, qkv_x, qkv_x_other)
    dn1, gain_one = rest_back(2, lengths, n1, dhb, w_x, wo_x, dn1, xr, deps=[own])
    own = add_four(own, *got, gain_one, gain_two)
    got = (b_shift(own, 1), b_shift(own, -1), b_shift(own, 2))
    token_grad, tick = token_call(lengths, xr, dh, dn1, attn_gain, deps=[own])
    own = cat_sum(own, *got, deps=[tick])
    got = (a_shift(own, 1), a_shift(own, -1), a_shift(own, 2))
    layer_out, tick = layer_call(lengths, h, f, deps=[own])
    own = cat_sum(own, *got, deps=[tick])
    other = core_swap(own)
    gate_grad, up_grad, down_grad = unpack_ffn(ffn_sums, deps=[own])
    query_grad, key_grad, value_grad, output_grad, attn_gain_grad, ffn_gain_grad = unpack_attn(pos, own, other)
    return (
        layer_out,
        token_grad,
        attn_gain_grad,
        query_grad.T,
        key_grad.T,
        value_grad.T,
        output_grad,
        ffn_gain_grad,
        gate_grad,
        up_grad,
        down_grad,
    )


def solution(mesh):
    placed = (
        P("dp", None),
        P("dp", None),
        P(),
        P(None, "tensor"),
        P(None, "tensor"),
        P(None, "tensor"),
        P("tensor", None),
        P(),
        P(None, "tensor"),
        P(None, "tensor"),
        P("tensor", None),
        P("dp", None),
    )
    return jax.shard_map(
        local,
        mesh=mesh,
        in_specs=placed,
        out_specs=(
            P("dp", None),
            P("dp", None),
            P(),
            P(None, "tensor"),
            P(None, "tensor"),
            P(None, "tensor"),
            P("tensor", None),
            P(),
            P(None, "tensor"),
            P(None, "tensor"),
            P("tensor", None),
        ),
        check_vma=False,
    )
```

```python
import functools
import jax
import jax.numpy as jnp
from jax import lax
from jax.experimental import pallas as pl
from jax.experimental.pallas import tpu as pltpu
from jax.sharding import PartitionSpec as P

T = 1024
D = 768
HALF = 512
HW = 192
UN = 512
EPS = 1e-06
LIGHT = 20
F32 = jnp.float32
BF16 = jnp.bfloat16
VM = pl.BlockSpec(memory_space=pltpu.VMEM)
SM = pl.BlockSpec(memory_space=pltpu.SMEM)


ANY = pl.BlockSpec(memory_space=pl.ANY)
FAR = pl.BlockSpec(memory_space=pltpu.HBM)


def call(body, out_shape, n_vmem, smem=0, scratch=(), flops=0, bytes_accessed=0, limit=12, alias={}, near=True, out_far=0):
    def run(*args, deps=(), far=()):
        deps = [d for d in deps if d is not None]
        n = smem + n_vmem + len(far)

        def inner(*refs):
            body(*refs[:n], *refs[n + len(deps) :])

        outs = jax.tree.map(lambda s: pltpu.VMEM(s.shape, s.dtype), out_shape) if near else out_shape
        specs = jax.tree.map(lambda _: VM, out_shape)
        if out_far:
            outs = tuple(pltpu.HBM(s.shape, s.dtype) for s in out_shape[:out_far]) + outs[out_far:]
            specs = (FAR,) * out_far + specs[out_far:]
        args = [
            *args[:smem],
            *(pltpu.with_memory_space_constraint(v, pltpu.VMEM) for v in args[smem:]),
            *(pltpu.with_memory_space_constraint(v, pltpu.HBM) for v in far),
        ]
        return pl.pallas_call(
            inner,
            out_shape=outs,
            in_specs=[SM] * smem + [VM] * n_vmem + [FAR] * len(far) + [ANY] * len(deps),
            out_specs=specs,
            scratch_shapes=list(scratch),
            input_output_aliases=alias,
            compiler_params=pltpu.CompilerParams(vmem_limit_bytes=limit << 20),
            cost_estimate=pl.CostEstimate(flops=int(flops) // LIGHT, bytes_accessed=int(bytes_accessed) // LIGHT, transcendentals=0),
        )(*args, *deps)

    return run


def sds(shape, dtype):
    return jax.ShapeDtypeStruct(shape, dtype)


def nn(a, b):
    return jnp.dot(a, b, preferred_element_type=F32)


def nt(a, b):
    return lax.dot_general(a, b, (((1,), (1,)), ((), ())), preferred_element_type=F32)


def tn(a, b):
    return lax.dot_general(a, b, (((0,), (0,)), ((), ())), preferred_element_type=F32)


def long_start(len_ref):
    start, acc = jnp.int32(0), jnp.int32(0)
    for k in range(8):
        n = len_ref[0, k]
        start = jnp.where(n == HALF, acc, start)
        acc = acc + n
    return start


def rest_mask(len_ref):
    start = long_start(len_ref)

    def ids(shape, dim):
        place = lax.broadcasted_iota(jnp.int32, shape, dim) + (HALF + start)
        place = jnp.where(place >= T, place - T, place)
        end, got = jnp.int32(0), jnp.zeros(shape, jnp.int32)
        for k in range(7):
            end = end + len_ref[0, k]
            got = got + (place >= end).astype(jnp.int32)
        return got

    return ids((HALF, 1), 0) == ids((1, HALF), 1)


def window(buf, first):
    first = jnp.where(first >= T, first - T, first)
    base = pl.multiple_of(first // 8 * 8, 8)
    n = first - base
    v = pltpu.roll(buf[pl.ds(base, 264), :].reshape(33, 8, D), lax.rem(8 - n, 8), 1)
    row = lax.broadcasted_iota(jnp.int32, (1, 8, 1), 1)
    return jnp.where(row < 8 - n, v[0:32], v[1:33]).reshape(256, D)


def pack_body(pos_ref, wo_ref, wg_ref, wu_ref, wd_ref, out_ref, half_ref, cols, rows, half, sems):
    core, d = pos_ref[1], pos_ref[4]
    lanes = pl.ds(pl.multiple_of(d // 8 * 128, 128), 128)
    units = pl.ds(pl.multiple_of(d * 16, 16), 16)
    copies = (
        pltpu.make_async_copy(wg_ref.at[:, lanes], cols.at[0], sems.at[0]),
        pltpu.make_async_copy(wu_ref.at[:, lanes], cols.at[1], sems.at[1]),
        pltpu.make_async_copy(wd_ref.at[units, :], rows, sems.at[2]),
        pltpu.make_async_copy(wo_ref.at[pl.ds(pl.multiple_of(core * 96, 32), 96), :], half, sems.at[3]),
    )
    for copy in copies:
        copy.start()
    for copy in copies:
        copy.wait()
    half_ref[...] = half[...].astype(F32)
    lane = lax.broadcasted_iota(jnp.int32, (16, 128), 1)
    row = lax.broadcasted_iota(jnp.int32, (16, 128), 0)
    pick = (lane == row + lax.rem(d, 8) * 16).astype(BF16)
    for m in range(2):
        out_ref[pl.ds(16 * m, 16), :] = nt(pick, cols[m])
    out_ref[32:48, :] = rows[...].astype(F32)


def pack(pos, *weights):
    scratch = [pltpu.VMEM((2, D, 128), BF16), pltpu.VMEM((16, D), BF16), pltpu.VMEM((96, D), BF16), pltpu.SemaphoreType.DMA((4,))]
    return call(pack_body, (sds((48, D), F32), sds((96, D), F32)), 0, 1, scratch, 1e6, 1e6)(pos, far=weights)


def cat_body(*refs):
    out, at = refs[-1], 0
    for ref in refs[:-1]:
        out[pl.ds(at, ref.shape[0]), :] = ref[...]
        at += ref.shape[0]


def cat(*parts, deps=()):
    shape = (sum(p.shape[0] for p in parts), parts[0].shape[1])
    return call(cat_body, sds(shape, F32), len(parts), 0, (), 1e5, 8 * shape[0] * shape[1])(*parts, deps=deps)


def cat_rows_body(first, count, *refs):
    out = refs[-1]
    for n, ref in enumerate(refs[:-1]):
        out[pl.ds(count * n, count), :] = ref[first : first + count, :]


def cat_rows(first, count, *parts, deps=()):
    shape = (count * len(parts), parts[0].shape[1])
    return call(functools.partial(cat_rows_body, first, count), sds(shape, F32), len(parts), 0, (), 1e5, 8 * shape[0] * shape[1])(
        *parts, deps=deps)


def cat_sum_body(size, *refs):
    out, parts = refs[-1], refs[:-1]
    for n, ref in enumerate(parts):
        out[pl.ds(size * n, size), :] = ref[0:size, :]
    own, left, right, opposite = [ref[size : size + 8, :] for ref in parts]
    out[pl.ds(4 * size, 8), :] = (own + opposite) + (left + right)


def cat_sum(*parts, deps=()):
    size = parts[0].shape[0] - 8
    return call(functools.partial(cat_sum_body, size), sds((4 * size + 8, D), F32), 4, 0, (), 1e5, 32e3 * size)(
        *parts, deps=deps)


def piece_row(core, ja, jb):
    return pl.multiple_of(jnp.where(core == 0, ja * 4 + jb, jb * 4 + ja) * 48 + core * 24, 8)


def unpack_ffn_body(g_ref, wg_ref, wu_ref, wd_ref, tick_ref, buf, sems):
    tick_ref[...] = jnp.zeros_like(tick_ref)
    copies = [pltpu.make_async_copy(g_ref.at[pl.ds(256 * n, 256), :], buf.at[n], sems.at[n]) for n in range(3)]
    for copy in copies:
        copy.start()
    for n, copy in enumerate(copies):
        rows = pl.ds(256 * n, 256)
        copy.wait()
        wg_ref[rows, :] = buf[n, :, 0:512]
        wu_ref[rows, :] = buf[n, :, 512:1024]
        wd_ref[:, rows] = buf[n, :, 1024:1536].T


def unpack_ffn(g, deps=()):
    return call(unpack_ffn_body, (sds((D, UN), F32), sds((D, UN), F32), sds((UN, D), F32), sds((8, 128), F32)), 0, 0,
                [pltpu.VMEM((3, 256, 1536), F32), pltpu.SemaphoreType.DMA((3,))], 1e6, 1e7, near=False)(far=[g], deps=deps)


def unpack_attn_body(pos_ref, mine, other, wq_ref, wk_ref, wv_ref, wo_ref, one_ref, two_ref, buf):
    core, ja, jb = pos_ref[1], pos_ref[2], pos_ref[3]
    for ref, c, a, b in ((mine, core, ja, jb), (other, 1 - core, jb, ja)):
        for m, sa in enumerate((0, 3, 1, 2)):
            for n, sb in enumerate((0, 3, 1, 2)):
                row = piece_row(c, lax.rem(a + sa, 4), lax.rem(b + sb, 4))
                buf[pl.ds(row, 24), :] = ref[pl.ds(96 * m + 24 * n, 24), :]
    for n, out in enumerate((wq_ref, wk_ref, wv_ref, wo_ref)):
        out[...] = buf[192 * n : 192 * n + 192, :]
    gains = mine[384:392, :] + other[384:392, :]
    one_ref[...] = gains[0].reshape(D)
    two_ref[...] = gains[1].reshape(D)


def unpack_attn(pos, mine, other, deps=()):
    o, g = sds((HW, D), F32), sds((D,), F32)
    return call(unpack_attn_body, (o, o, o, o, g, g), 2, 1, [pltpu.VMEM((D, D), F32)], 1e6, 5e6, near=False)(pos, mine, other, deps=deps)


def split_rows(pos_ref, buf, keep_ref, send_ref):
    core, ja, jb = pos_ref[1], pos_ref[2], pos_ref[3]
    for out, half, a, b in ((keep_ref, core, ja, jb), (send_ref, 1 - core, jb, ja)):
        for sa in range(4):
            for sb in range(4):
                row = piece_row(half, lax.rem(a + sa, 4), lax.rem(b + sb, 4))
                out[pl.ds(96 * sa + 24 * sb, 24), :] = buf[pl.ds(row, 24), :]


def add_split_body(*refs):
    ins, outs = refs[:-4], refs[-4:]
    size = outs[0].shape[0]
    for n, out in enumerate(outs):
        rows = pl.ds(size * n, size)
        if len(ins) == 2:
            out[...] = ins[0][rows, :] + ins[1][rows, :]
        else:
            own, left, right, opposite = ins
            out[...] = (own[rows, :] + opposite[rows, :]) + (left[rows, :] + right[rows, :])


def add_split(*ins, deps=()):
    rows, lanes = ins[0].shape
    o = sds((rows // 4, lanes), F32)
    return call(add_split_body, (o,) * 4, len(ins), 0, (), rows * lanes * 2, rows * lanes * 12, 12)(*ins, deps=deps)


def add_body(own, left, right, opposite, *refs):
    out = refs[-1]
    rows = own.shape[0]
    out[0:rows, :] = (own[...] + opposite[...]) + (left[...] + right[...])
    if len(refs) > 1:
        row = lax.broadcasted_iota(jnp.int32, (8, 1), 0)
        out[rows : rows + 8, :] = jnp.where(row == 0, refs[0][...], jnp.where(row == 1, refs[1][...], 0.0))


def add_four(*ins, deps=()):
    rows, lanes = ins[0].shape
    out = sds((rows + (8 if len(ins) > 4 else 0), lanes), F32)
    return call(add_body, out, len(ins), 0, (), 1e5, 1e6)(*ins, deps=deps)


def front_body(len_ref, gain_ref, wq_ref, wk_ref, wv_ref, x_far, dy_far,
               xr_out, n1_out, dyr_out, q_out, k_out, v_out, o_out, ot_ref, lse_ref,
               buf, src, keep, heads, sems, out_sems):
    start = long_start(len_ref)
    mask = rest_mask(len_ref)
    copies = [pltpu.make_async_copy(far.at[pl.ds(512 * h, 512), :], src.at[n, pl.ds(512 * h, 512), :], sems.at[n, h])
              for n, far in enumerate((x_far, dy_far)) for h in range(2)]
    outs = [pltpu.make_async_copy(keep.at[n], out, out_sems.at[n]) for n, out in enumerate((xr_out, n1_out, dyr_out))]
    outs += [pltpu.make_async_copy(heads.at[n], out, out_sems.at[3 + n]) for n, out in enumerate((q_out, k_out, v_out, o_out))]
    for copy in copies:
        copy.start()
    for n in range(2):
        for h in range(2):
            copies[2 * n + h].wait()
            for t in (2 * h, 2 * h + 1):
                buf[pl.ds(256 * t, 256), :] = src[n, pl.ds(256 * t, 256), :].astype(F32)
        buf[pl.ds(T, 264), :] = buf[pl.ds(0, 264), :]
        for t in range(4):
            rows = pl.ds(256 * t, 256)
            x = window(buf, start + 256 * t)
            if n == 0:
                keep[0, rows, :] = x.astype(BF16)
                r = lax.rsqrt(jnp.mean(x * x, axis=-1, keepdims=True) + EPS)
                keep[1, rows, :] = (x * r * gain_ref[...].reshape(1, D)).astype(BF16)
            else:
                keep[2, rows, :] = x.astype(BF16)
    for copy in outs[:3]:
        copy.start()
    lane = lax.broadcasted_iota(jnp.int32, (1, HW), 1)
    for i in range(2):
        rows = pl.ds(HALF * i, HALF)
        n1 = keep[1, rows, :]
        q = (nt(n1, wq_ref[...]).astype(BF16).astype(F32) * 0.125).astype(BF16)
        k = nt(n1, wk_ref[...]).astype(BF16)
        v = nt(n1, wv_ref[...]).astype(BF16)
        heads[0, rows, :] = q
        heads[1, rows, :] = k
        heads[2, rows, :] = v
        vt = v.T
        parts = []
        for h in range(3):
            s = nt(k, jnp.where((lane >= 64 * h) & (lane < 64 * h + 64), q, jnp.zeros_like(q)))
            if i == 1:
                s = jnp.where(mask, s, -1e30)
            top = jnp.max(s, axis=0, keepdims=True)
            e = jnp.exp(s - top)
            total = jnp.sum(e, axis=0, keepdims=True)
            lse_ref[pl.ds(h, 1), rows] = top + jnp.log(total)
            parts.append(nn(vt[64 * h : 64 * h + 64, :], e.astype(BF16)) * (1.0 / total))
        o = jnp.concatenate(parts, axis=0).astype(BF16)
        ot_ref[:, rows] = o.astype(F32)
        heads[3, rows, :] = o.T
    for copy in outs[3:]:
        copy.start()
    for copy in outs:
        copy.wait()


def front(lengths, tokens, cot, gain, wq, wk, wv, deps=()):
    o, b = sds((T, D), BF16), sds((T, HW), BF16)
    scratch = [pltpu.VMEM((T + 264, D), F32), pltpu.VMEM((2, T, D), BF16), pltpu.VMEM((3, T, D), BF16), pltpu.VMEM((4, T, HW), BF16),
               pltpu.SemaphoreType.DMA((2, 2)), pltpu.SemaphoreType.DMA((7,))]
    return call(front_body, (o, o, o, b, b, b, b, sds((HW, T), F32), sds((8, T), F32)), 4, 1, scratch, 4e9, 8e6, 24, out_far=7)(
        lengths, gain, wq, wk, wv, far=(tokens, cot), deps=deps)


def heads_back(i, mask, q, k, v, do, lse):
    lane = lax.broadcasted_iota(jnp.int32, (1, 256), 1)
    head = [(lane >= 64 * h) & (lane < 64 * h + 64) for h in range(3)]
    each = lambda t: jnp.concatenate([jnp.where(m, t, jnp.zeros_like(t)) for m in head], axis=0)
    s_all = nt(each(k), q)
    dp_all = nt(each(v), do)
    kt = k.T
    ps, dss, dqt = [], [], []
    for h in range(3):
        s = s_all[HALF * h : HALF * h + HALF]
        dp = dp_all[HALF * h : HALF * h + HALF]
        if i == 1:
            s = jnp.where(mask, s, -1e30)
        if lse is None:
            e = jnp.exp(s - jnp.max(s, axis=0, keepdims=True))
            p = e * (1.0 / jnp.sum(e, axis=0, keepdims=True))
        else:
            p = jnp.exp(s - lse[h : h + 1, :])
        ds = (p * (dp - jnp.sum(p * dp, axis=0, keepdims=True))).astype(BF16)
        ps.append(p.astype(BF16))
        dss.append(ds)
        dqt.append(nn(kt[64 * h : 64 * h + 64, :], ds))
    dq = (jnp.concatenate(dqt + [jnp.zeros((64, HALF), F32)], axis=0) * 0.125).T
    dv = nn(jnp.concatenate(ps, axis=0), do)
    dk = nn(jnp.concatenate(dss, axis=0), q)

    def pick(t):
        t = [t[HALF * h : HALF * h + HALF] for h in range(3)]
        t = jnp.where(head[0], t[0], jnp.where(head[1], t[1], t[2]))
        return jnp.where(lane < HW, t, 0.0).astype(BF16)

    return dq.astype(BF16), pick(dk), pick(dv)


def padded(t):
    return jnp.concatenate([t, jnp.zeros((t.shape[0], 256 - t.shape[1]), t.dtype)], axis=1)


def own_back_body(len_ref, pos_ref, dhb_ref, wo_ref, q_ref, k_ref, v_ref, lse_ref, n1_ref, o_ref,
                  keep_ref, send_ref, d_ref, g_ref):
    mask = rest_mask(len_ref)
    for i in range(2):
        rows = pl.ds(HALF * i, HALF)
        do = padded(nt(dhb_ref[rows, :], wo_ref[...]).astype(BF16))
        d = heads_back(i, mask, padded(q_ref[rows, :]), padded(k_ref[rows, :]), padded(v_ref[rows, :]), do, lse_ref[:, rows])
        for n in range(3):
            d_ref[rows, 256 * n : 256 * n + 256] = d[n]
    for n in range(3):
        g_ref[192 * n : 192 * n + 192, :] = tn(d_ref[:, 256 * n : 256 * n + 256], n1_ref[...])[0:192]
    g_ref[576:768, :] = tn(o_ref[...], dhb_ref[...])
    split_rows(pos_ref, g_ref, keep_ref, send_ref)


def own_back(lengths, pos, dhb, wo, q, k, v, lse, n1, o, deps=()):
    g = sds((384, D), F32)
    return call(own_back_body, (g, g, sds((T, D), BF16)), 8, 2, [pltpu.VMEM((D, D), F32)], 8e9, 9e6)(
        lengths, pos, dhb, wo, q, k, v, lse, n1, o, deps=deps)


def rest_back_body(r, len_ref, n1_ref, dhb_ref, w_ref, wo_ref, *refs):
    mask = rest_mask(len_ref)
    first, last = r == 0, r == 2
    if first:
        own_d, wq, wk, wv, dn1_ref, d = refs
    elif last:
        dn1_in, x_ref, dn1_ref, gg_ref, d = refs
    else:
        dn1_in, dn1_ref, d = refs
    for i in range(2):
        rows = pl.ds(HALF * i, HALF)
        qkv = nt(n1_ref[rows, :], w_ref[...])
        q = (qkv[:, 0:256].astype(BF16).astype(F32) * 0.125).astype(BF16)
        k = qkv[:, 256:512].astype(BF16)
        v = qkv[:, 512:768].astype(BF16)
        do = nt(dhb_ref[rows, :], wo_ref[...]).astype(BF16)
        for n, t in enumerate(heads_back(i, mask, q, k, v, do, None)):
            d[:, 256 * n : 256 * n + 256] = t
        new = nn(d[...], w_ref[...])
        if first:
            for n, w in enumerate((wq, wk, wv)):
                new = new + nn(own_d[rows, 256 * n : 256 * n + 192], w[...])
        else:
            new = new + dn1_in[rows, :]
        dn1_ref[rows, :] = new
    if last:
        gg = jnp.zeros((8, D), F32)
        for t in range(4):
            rows = pl.ds(256 * t, 256)
            x = x_ref[rows, :].astype(F32)
            r = lax.rsqrt(jnp.mean(x * x, axis=-1, keepdims=True) + EPS)
            gg = gg + jnp.sum((dn1_ref[rows, :] * (x * r)).reshape(32, 8, D), axis=0)
        gg_ref[...] = jnp.broadcast_to(jnp.sum(gg, axis=0, keepdims=True), (8, D))


def rest_back(r, lengths, n1, dhb, w, wo, *more, deps=()):
    o = sds((T, D), F32)
    return call(functools.partial(rest_back_body, r), (o, sds((8, D), F32)) if r == 2 else o, 4 + len(more), 1,
                [pltpu.VMEM((HALF, D), BF16)], 6e9, 1e7)(lengths, n1, dhb, w, wo, *more, deps=deps)


def middle_body(pos_ref, x_ref, oo, oa, ob, oc, od, wo_own, wo_mine, wo_other, gain_ref,
                h_ref, n2_ref, wo_l, wo_r, wo_x, buf):
    core = pos_ref[1]
    for n, ref in enumerate((wo_l, wo_r, wo_x)):
        shard = pl.ds(96 * n, 96)
        buf[pl.ds(pl.multiple_of(core * 96, 32), 96), :] = wo_mine[shard, :]
        buf[pl.ds(pl.multiple_of((1 - core) * 96, 32), 96), :] = wo_other[shard, :]
        ref[0:192, :] = buf[0:192, :].astype(BF16)
        ref[192:256, :] = jnp.zeros((64, D), BF16)
    for t in range(4):
        rows = pl.ds(256 * t, 256)
        h = x_ref[rows, :].astype(F32) + tn(oo[:, rows].astype(BF16), wo_own[...])
        h = h + tn(oa[:, rows].astype(BF16), wo_l[0:192, :])
        h = h + tn(ob[:, rows].astype(BF16), wo_r[0:192, :])
        h = h + tn(oc[:, rows].astype(BF16), wo_x[0:96, :]) + tn(od[:, rows].astype(BF16), wo_x[96:192, :])
        h_ref[rows, :] = h
        f = lax.rsqrt(jnp.mean(h * h, axis=-1, keepdims=True) + EPS)
        n2_ref[rows, :] = (h * f * gain_ref[...].reshape(1, D)).astype(BF16)


def middle(pos, xr, os, wo, wo_mine, wo_other, gain, deps=()):
    w = sds((256, D), BF16)
    return call(middle_body, (sds((T, D), F32), sds((T, D), BF16), w, w, w), 10, 1,
                [pltpu.VMEM((192, D), F32)], 1.2e9, 8e6)(pos, xr, *os, wo, wo_mine, wo_other, gain, deps=deps)


def half_body(pos_ref, wq, wk, wv, out_ref, buf, sems):
    core = pos_ref[1]
    copies = [pltpu.make_async_copy(src, buf.at[pl.ds(192 * n, 192), :], sems.at[n]) for n, src in enumerate((wq, wk, wv))]
    for copy in copies:
        copy.start()
    for copy in copies:
        copy.wait()
    out_ref[...] = buf[pl.ds(pl.multiple_of(core * 288, 32), 288), :].astype(F32)


def qkv_half(pos, wq, wk, wv, deps=()):
    return call(half_body, sds((288, D), F32), 0, 1, [pltpu.VMEM((576, D), BF16), pltpu.SemaphoreType.DMA((3,))], 1e6, 2e6)(
        pos, far=(wq, wk, wv), deps=deps)


def qkv_body(pos_ref, mine, other, *refs):
    core, buf = pos_ref[1], refs[-1]
    for r, out in enumerate(refs[:-1]):
        buf[pl.ds(pl.multiple_of(core * 288, 32), 288), :] = mine[288 * r : 288 * r + 288, :]
        buf[pl.ds(pl.multiple_of((1 - core) * 288, 32), 288), :] = other[288 * r : 288 * r + 288, :]
        for n in range(3):
            out[256 * n : 256 * n + 192, :] = buf[192 * n : 192 * n + 192, :].astype(BF16)
            out[256 * n + 192 : 256 * n + 256, :] = jnp.zeros((64, D), BF16)


def qkv_shard(pos, mine, other, deps=()):
    o = sds((D, D), BF16)
    return call(qkv_body, (o,) * (mine.shape[0] // 288), 2, 1, [pltpu.VMEM((576, D), F32)], 1e6, 3e6)(pos, mine, other, deps=deps)


C1 = 0.7978845608028654
C2 = 0.044715 * C1


def ffn_math(gate, up, dhid):
    u2 = gate * gate
    t = jnp.tanh(gate * (C1 + C2 * u2))
    hp = 0.5 + 0.5 * t
    g = gate * hp
    slope = hp + g * (1.0 - t) * (C1 + 3.0 * C2 * u2)
    return (g * up).astype(BF16), (dhid * up * slope).astype(BF16), (dhid * g).astype(BF16)


def ffn_own_body(pos_ref, n2_ref, dy_ref, wg_ref, wu_ref, wd_ref, f_ref, dn2_ref, keep_ref, send_ref, hid, dgu, g_ref):
    for t in range(4):
        rows = pl.ds(256 * t, 256)
        n2, dy = n2_ref[rows, :], dy_ref[rows, :]
        gate = nn(n2, wg_ref[...])
        up = nn(n2, wu_ref[...])
        dh = nt(dy, wd_ref[...])
        a, b, c = ffn_math(gate, up, dh)
        hid[rows, :] = a
        dgu[rows, 0:512] = b
        dgu[rows, 512:1024] = c
        f_ref[rows, :] = nn(a, wd_ref[...])
        dn2_ref[rows, :] = nt(b, wg_ref[...]) + nt(c, wu_ref[...])
    for t in range(3):
        cols = pl.ds(256 * t, 256)
        g_ref[cols, 0:1024] = tn(n2_ref[:, cols], dgu[...])
        g_ref[cols, 1024:1536] = tn(dy_ref[:, cols], hid[...])
    split_rows(pos_ref, g_ref, keep_ref, send_ref)


def ffn_own(pos, n2, dy, wg, wu, wd, deps=()):
    o, g = sds((T, D), F32), sds((384, 1536), F32)
    return call(ffn_own_body, (o, o, g, g), 5, 1,
                [pltpu.VMEM((T, UN), BF16), pltpu.VMEM((T, 1024), BF16), pltpu.VMEM((D, 1536), F32)], 7.2e9, 1.6e7)(
        pos, n2, dy, wg, wu, wd, deps=deps)


def ffn_rest_body(n2_far, dy_far, w_ref, f_ref, dn2_ref,
                  n2_ref, dy_ref, buf, wb, sems, in_sems):
    def fetch(r, half, slot):
        pieces = pl.ds(16 * half, 16)
        return pltpu.make_async_copy(w_ref.at[pieces, r, :, :], buf.at[slot, pieces], sems.at[slot, half])

    ins = [pltpu.make_async_copy(src, dst, in_sems.at[n]) for n, (src, dst) in enumerate(((n2_far, n2_ref), (dy_far, dy_ref)))]
    fetch(0, 0, 0).start()
    fetch(0, 1, 0).start()
    for copy in ins:
        copy.start()
    f_ref[...] = jnp.zeros_like(f_ref)
    dn2_ref[...] = jnp.zeros_like(dn2_ref)

    def step(r, carry):
        slot = lax.rem(r, 2)

        @pl.when(r < 2)
        def _():
            fetch(r + 1, 0, 1 - slot).start()
            fetch(r + 1, 1, 1 - slot).start()

        for half in range(2):
            fetch(r, half, slot).wait()
            for p in range(16 * half, 16 * half + 16):
                for m in range(3):
                    wb[m, pl.ds(16 * p, 16), :] = buf[slot, p, pl.ds(16 * m, 16), :].astype(BF16)

        @pl.when(r == 0)
        def _():
            for copy in ins:
                copy.wait()

        for t in range(4):
            rows = pl.ds(256 * t, 256)
            n2, dy = n2_ref[rows, :], dy_ref[rows, :]
            a, b, c = ffn_math(nt(n2, wb[0]), nt(n2, wb[1]), nt(dy, wb[2]))
            f_ref[rows, :] = f_ref[rows, :] + nn(a, wb[2])
            dn2_ref[rows, :] = dn2_ref[rows, :] + (nn(b, wb[0]) + nn(c, wb[1]))
        return carry

    lax.fori_loop(0, 3, step, 0)


def ffn_rest(*far, deps=()):
    o = sds((T, D), F32)
    scratch = [pltpu.VMEM((T, D), BF16), pltpu.VMEM((T, D), BF16), pltpu.VMEM((2, 32, 48, D), F32), pltpu.VMEM((3, UN, D), BF16),
               pltpu.SemaphoreType.DMA((2, 2)), pltpu.SemaphoreType.DMA((2,))]
    return call(ffn_rest_body, (o, o), 0, 0, scratch, 12 * T * D * 1536, 2e7, 26)(far=far, deps=deps)


def dh_body(h_ref, own_ref, rest_ref, dy_ref, gain_ref, dh_ref, dhb_ref, gg_ref):
    gg = jnp.zeros((8, D), F32)
    for t in range(4):
        rows = pl.ds(256 * t, 256)
        h = h_ref[rows, :]
        r = lax.rsqrt(jnp.mean(h * h, axis=-1, keepdims=True) + EPS)
        b = h * r
        dn2 = own_ref[rows, :] + rest_ref[rows, :]
        gg = gg + jnp.sum((dn2 * b).reshape(32, 8, D), axis=0)
        e = dn2 * gain_ref[...].reshape(1, D)
        dh = dy_ref[rows, :].astype(F32) + r * (e - b * jnp.mean(e * b, axis=-1, keepdims=True))
        dh_ref[rows, :] = dh
        dhb_ref[rows, :] = dh.astype(BF16)
    gg_ref[...] = jnp.broadcast_to(jnp.sum(gg, axis=0, keepdims=True), (8, D))


def dh_call(h, own, rest, dy, gain, deps=()):
    return call(dh_body, (sds((T, D), F32), sds((T, D), BF16), sds((8, D), F32)), 5, 0, (), 2e7, 1.2e7)(
        h, own, rest, dy, gain, deps=deps)


def unrotate(start, buf, out_ref, dtype):
    back = jnp.where(start > 0, T - start, 0)
    buf[pl.ds(T, 264), :] = buf[pl.ds(0, 264), :]
    for t in range(4):
        out_ref[pl.ds(256 * t, 256), :] = window(buf, back + 256 * t).astype(dtype)


def layer_body(len_ref, h_ref, own_ref, rest_ref, out_ref, tick_ref, buf):
    tick_ref[...] = jnp.zeros_like(tick_ref)
    for t in range(4):
        rows = pl.ds(256 * t, 256)
        buf[rows, :] = h_ref[rows, :] + (own_ref[rows, :] + rest_ref[rows, :])
    unrotate(long_start(len_ref), buf, out_ref, BF16)


def layer_call(lengths, h, own, rest, deps=()):
    return call(layer_body, (sds((T, D), BF16), sds((8, 128), F32)), 3, 1, [pltpu.VMEM((T + 264, D), F32)], 2e6, 8e6, near=False)(lengths, h, own, rest, deps=deps)


def token_body(len_ref, x_ref, dh_ref, dn1_ref, gain_ref, out_ref, tick_ref, buf):
    tick_ref[...] = jnp.zeros_like(tick_ref)
    for t in range(4):
        rows = pl.ds(256 * t, 256)
        x = x_ref[rows, :].astype(F32)
        r = lax.rsqrt(jnp.mean(x * x, axis=-1, keepdims=True) + EPS)
        b = x * r
        e = dn1_ref[rows, :] * gain_ref[...].reshape(1, D)
        buf[rows, :] = dh_ref[rows, :] + r * (e - b * jnp.mean(e * b, axis=-1, keepdims=True))
    unrotate(long_start(len_ref), buf, out_ref, F32)


def token_call(lengths, xr, dh, dn1, gain, deps=()):
    return call(token_body, (sds((T, D), F32), sds((8, 128), F32)), 4, 1, [pltpu.VMEM((T + 264, D), F32)], 2e7, 1.2e7, near=False)(lengths, xr, dh, dn1, gain, deps=deps)


RING = 4


def x_shift(v, step):
    return lax.ppermute(v, "tensor", [(i, (i + step) % RING) for i in range(RING)])


def dp_table(move):
    table = []
    for y in range(RING):
        for z in range(RING):
            for c in range(2):
                to_y, to_z, to_c = move(y, z, c)
                table.append(((y * RING + z) * 2 + c, (to_y % RING * RING + to_z % RING) * 2 + to_c))
    return table


def a_shift(v, step):
    return lax.ppermute(v, "dp", dp_table(lambda y, z, c: (y + step * (1 - c), z + step * c, c)))


def b_shift(v, step):
    return lax.ppermute(v, "dp", dp_table(lambda y, z, c: (y + step * c, z + step * (1 - c), c)))


def core_swap(v):
    return lax.ppermute(v, "dp", dp_table(lambda y, z, c: (y, z, 1 - c)))


def local(
    tokens,
    lengths,
    attn_gain,
    query_weight,
    key_weight,
    value_weight,
    output_weight,
    ffn_gain,
    gate_weight,
    up_weight,
    down_weight,
    cotangent,
):
    x = lax.axis_index("tensor").astype(jnp.int32)
    d = lax.axis_index("dp").astype(jnp.int32)
    core, y, z = d % 2, d // 8, d // 2 % 4
    ja, jb = jnp.where(core == 0, y, z), jnp.where(core == 0, z, y)
    pos = jnp.stack([x, core, ja, jb, d])
    wq, wk, wv = query_weight.T, key_weight.T, value_weight.T
    piece, wo_half = pack(pos, output_weight, gate_weight, up_weight, down_weight)
    pieces = [x_shift(piece, 1), x_shift(piece, -1), x_shift(piece, 2)]
    xr, n1, dyr, q, k, v, o, ot, lse = front(lengths, tokens, cotangent, attn_gain, wq, wk, wv, deps=[piece])
    pieces = cat(*pieces, deps=[lse])
    weights = lax.all_gather(pieces, "dp", axis=0, tiled=True).reshape(32, 3, 48, D)
    near = [x_shift(wo_half, 1), x_shift(wo_half, -1), x_shift(wo_half, 2)]
    wo_mine = cat(*near)
    oa, ob = x_shift(ot, 1), x_shift(ot, -1)
    wo_other = core_swap(wo_mine)
    oc = x_shift(cat_rows(0, 96, oa, deps=[wo_mine]), 1)
    od = x_shift(cat_rows(96, 96, ob, deps=[wo_mine]), -1)
    h, n2, wo_l, wo_r, wo_x = middle(pos, xr, (ot, oa, ob, oc, od), output_weight, wo_mine, wo_other, ffn_gain)
    f, dn2, keep, send = ffn_own(pos, n2, dyr, gate_weight, up_weight, down_weight)
    ffn_keep, ffn_got = keep, core_swap(send)
    half = qkv_half(pos, wq, wk, wv, deps=[send])
    qkv_l, qkv_r = x_shift(half, 1), x_shift(half, -1)
    f_rest, dn2_rest = ffn_rest(n2, dyr, weights, deps=[half])

    own, right, opposite, left = add_split(ffn_keep, ffn_got, deps=[f_rest])
    ffn_got = (a_shift(left, -1), a_shift(right, 1), a_shift(opposite, 2))
    qkv_near = cat(qkv_l, qkv_r, deps=[f_rest])
    qkv_near_other = core_swap(qkv_near)
    qkv_x = x_shift(half, 2)
    dh, dhb, gain_two = dh_call(h, dn2, dn2_rest, dyr, ffn_gain, deps=[own, qkv_near])
    keep, send, dqkv = own_back(lengths, pos, dhb, output_weight, q, k, v, lse, n1, o)

    ffn_part, right, opposite, left = add_split(own, *ffn_got, deps=[keep])
    ffn_got = (b_shift(left, -1), b_shift(right, 1), b_shift(opposite, 2))
    got = core_swap(send)
    w_l, w_r = qkv_shard(pos, qkv_near, qkv_near_other)
    dn1 = rest_back(0, lengths, n1, dhb, w_l, wo_l, dqkv, wq, wk, wv, deps=[ffn_part, qkv_x])
    ffn_sum = add_four(ffn_part, *ffn_got, deps=[dn1])
    ffn_sums = lax.all_gather(ffn_sum, "dp", axis=0, tiled=True)
    own, right, opposite, left = add_split(keep, got, deps=[dn1])
    got = (a_shift(left, -1), a_shift(right, 1), a_shift(opposite, 2))
    qkv_x_other = core_swap(qkv_x)
    dn1 = rest_back(1, lengths, n1, dhb, w_r, wo_r, dn1, deps=[own])
    own, right, opposite, left = add_split(own, *got, deps=[dn1])
    got = (b_shift(left, -1), b_shift(right, 1), b_shift(opposite, 2))
    (w_x,) = qkv_shard(pos, qkv_x, qkv_x_other)
    dn1, gain_one = rest_back(2, lengths, n1, dhb, w_x, wo_x, dn1, xr, deps=[own])
    own = add_four(own, *got, gain_one, gain_two)
    got = (b_shift(own, 1), b_shift(own, -1), b_shift(own, 2))
    token_grad, tick = token_call(lengths, xr, dh, dn1, attn_gain, deps=[own])
    own = cat_sum(own, *got, deps=[tick])
    got = (a_shift(own, 1), a_shift(own, -1), a_shift(own, 2))
    layer_out, tick = layer_call(lengths, h, f, f_rest, deps=[own])
    own = cat_sum(own, *got, deps=[tick])
    other = core_swap(own)
    gate_grad, up_grad, down_grad, tick = unpack_ffn(ffn_sums, deps=[own])
    query_grad, key_grad, value_grad, output_grad, attn_gain_grad, ffn_gain_grad = unpack_attn(pos, own, other, deps=[tick])
    return (
        layer_out,
        token_grad,
        attn_gain_grad,
        query_grad.T,
        key_grad.T,
        value_grad.T,
        output_grad,
        ffn_gain_grad,
        gate_grad,
        up_grad,
        down_grad,
    )


def solution(mesh):
    placed = (
        P("dp", None),
        P("dp", None),
        P(),
        P(None, "tensor"),
        P(None, "tensor"),
        P(None, "tensor"),
        P("tensor", None),
        P(),
        P(None, "tensor"),
        P(None, "tensor"),
        P("tensor", None),
        P("dp", None),
    )
    return jax.shard_map(
        local,
        mesh=mesh,
        in_specs=placed,
        out_specs=(
            P("dp", None),
            P("dp", None),
            P(),
            P(None, "tensor"),
            P(None, "tensor"),
            P(None, "tensor"),
            P("tensor", None),
            P(),
            P(None, "tensor"),
            P(None, "tensor"),
            P("tensor", None),
        ),
        check_vma=False,
    )
```

```python
import functools
import jax
import jax.numpy as jnp
from jax import lax
from jax.experimental import pallas as pl
from jax.experimental.pallas import tpu as pltpu
from jax.sharding import PartitionSpec as P

T = 1024
D = 768
HALF = 512
HW = 192
UN = 512
EPS = 1e-06
LIGHT = 20
F32 = jnp.float32
BF16 = jnp.bfloat16
VM = pl.BlockSpec(memory_space=pltpu.VMEM)
SM = pl.BlockSpec(memory_space=pltpu.SMEM)


ANY = pl.BlockSpec(memory_space=pl.ANY)
FAR = pl.BlockSpec(memory_space=pltpu.HBM)


def call(body, out_shape, n_vmem, smem=0, scratch=(), flops=0, bytes_accessed=0, limit=12, alias={}, near=True, out_far=0):
    def run(*args, deps=(), far=()):
        deps = [d for d in deps if d is not None]
        n = smem + n_vmem + len(far)

        def inner(*refs):
            body(*refs[:n], *refs[n + len(deps) :])

        outs = jax.tree.map(lambda s: pltpu.VMEM(s.shape, s.dtype), out_shape) if near else out_shape
        specs = jax.tree.map(lambda _: VM, out_shape)
        if out_far:
            outs = tuple(pltpu.HBM(s.shape, s.dtype) for s in out_shape[:out_far]) + outs[out_far:]
            specs = (FAR,) * out_far + specs[out_far:]
        args = [
            *args[:smem],
            *(pltpu.with_memory_space_constraint(v, pltpu.VMEM) for v in args[smem:]),
            *(pltpu.with_memory_space_constraint(v, pltpu.HBM) for v in far),
        ]
        return pl.pallas_call(
            inner,
            out_shape=outs,
            in_specs=[SM] * smem + [VM] * n_vmem + [FAR] * len(far) + [ANY] * len(deps),
            out_specs=specs,
            scratch_shapes=list(scratch),
            input_output_aliases=alias,
            compiler_params=pltpu.CompilerParams(vmem_limit_bytes=limit << 20),
            cost_estimate=pl.CostEstimate(flops=int(flops) // LIGHT, bytes_accessed=int(bytes_accessed) // LIGHT, transcendentals=0),
        )(*args, *deps)

    return run


def sds(shape, dtype):
    return jax.ShapeDtypeStruct(shape, dtype)


def nn(a, b):
    return jnp.dot(a, b, preferred_element_type=F32)


def nt(a, b):
    return lax.dot_general(a, b, (((1,), (1,)), ((), ())), preferred_element_type=F32)


def tn(a, b):
    return lax.dot_general(a, b, (((0,), (0,)), ((), ())), preferred_element_type=F32)


def long_start(len_ref):
    start, acc = jnp.int32(0), jnp.int32(0)
    for k in range(8):
        n = len_ref[0, k]
        start = jnp.where(n == HALF, acc, start)
        acc = acc + n
    return start


def rest_mask(len_ref):
    start = long_start(len_ref)

    def ids(shape, dim):
        place = lax.broadcasted_iota(jnp.int32, shape, dim) + (HALF + start)
        place = jnp.where(place >= T, place - T, place)
        end, got = jnp.int32(0), jnp.zeros(shape, jnp.int32)
        for k in range(7):
            end = end + len_ref[0, k]
            got = got + (place >= end).astype(jnp.int32)
        return got

    return ids((HALF, 1), 0) == ids((1, HALF), 1)


def window(buf, first):
    first = jnp.where(first >= T, first - T, first)
    base = pl.multiple_of(first // 8 * 8, 8)
    n = first - base
    v = pltpu.roll(buf[pl.ds(base, 264), :].reshape(33, 8, D), lax.rem(8 - n, 8), 1)
    row = lax.broadcasted_iota(jnp.int32, (1, 8, 1), 1)
    return jnp.where(row < 8 - n, v[0:32], v[1:33]).reshape(256, D)


def pack_body(pos_ref, wo_ref, wg_ref, wu_ref, wd_ref, out_ref, half_ref, cols, rows, half, sems):
    core, d = pos_ref[1], pos_ref[4]
    lanes = pl.ds(pl.multiple_of(d // 8 * 128, 128), 128)
    units = pl.ds(pl.multiple_of(d * 16, 16), 16)
    copies = (
        pltpu.make_async_copy(wg_ref.at[:, lanes], cols.at[0], sems.at[0]),
        pltpu.make_async_copy(wu_ref.at[:, lanes], cols.at[1], sems.at[1]),
        pltpu.make_async_copy(wd_ref.at[units, :], rows, sems.at[2]),
        pltpu.make_async_copy(wo_ref.at[pl.ds(pl.multiple_of(core * 96, 32), 96), :], half, sems.at[3]),
    )
    for copy in copies:
        copy.start()
    for copy in copies:
        copy.wait()
    half_ref[...] = half[...].astype(F32)
    lane = lax.broadcasted_iota(jnp.int32, (16, 128), 1)
    row = lax.broadcasted_iota(jnp.int32, (16, 128), 0)
    pick = (lane == row + lax.rem(d, 8) * 16).astype(BF16)
    for m in range(2):
        out_ref[pl.ds(16 * m, 16), :] = nt(pick, cols[m])
    out_ref[32:48, :] = rows[...].astype(F32)


def pack(pos, *weights):
    scratch = [pltpu.VMEM((2, D, 128), BF16), pltpu.VMEM((16, D), BF16), pltpu.VMEM((96, D), BF16), pltpu.SemaphoreType.DMA((4,))]
    return call(pack_body, (sds((48, D), F32), sds((96, D), F32)), 0, 1, scratch, 1e6, 1e6)(pos, far=weights)


def cat_body(*refs):
    out, at = refs[-1], 0
    for ref in refs[:-1]:
        out[pl.ds(at, ref.shape[0]), :] = ref[...]
        at += ref.shape[0]


def cat(*parts, deps=()):
    shape = (sum(p.shape[0] for p in parts), parts[0].shape[1])
    return call(cat_body, sds(shape, F32), len(parts), 0, (), 1e5, 8 * shape[0] * shape[1])(*parts, deps=deps)


def cat_rows_body(first, count, *refs):
    out = refs[-1]
    for n, ref in enumerate(refs[:-1]):
        out[pl.ds(count * n, count), :] = ref[first : first + count, :]


def cat_rows(first, count, *parts, deps=()):
    shape = (count * len(parts), parts[0].shape[1])
    return call(functools.partial(cat_rows_body, first, count), sds(shape, F32), len(parts), 0, (), 1e5, 8 * shape[0] * shape[1])(
        *parts, deps=deps)


def cat_sum_body(size, *refs):
    out, parts = refs[-1], refs[:-1]
    for n, ref in enumerate(parts):
        out[pl.ds(size * n, size), :] = ref[0:size, :]
    own, left, right, opposite = [ref[size : size + 8, :] for ref in parts]
    out[pl.ds(4 * size, 8), :] = (own + opposite) + (left + right)


def cat_sum(*parts, deps=()):
    size = parts[0].shape[0] - 8
    return call(functools.partial(cat_sum_body, size), sds((4 * size + 8, D), F32), 4, 0, (), 1e5, 32e3 * size)(
        *parts, deps=deps)


def piece_row(core, ja, jb):
    return pl.multiple_of(jnp.where(core == 0, ja * 4 + jb, jb * 4 + ja) * 48 + core * 24, 8)


def unpack_ffn_body(g_ref, wg_ref, wu_ref, wd_ref, tick_ref, buf, sems):
    tick_ref[...] = jnp.zeros_like(tick_ref)
    copies = [pltpu.make_async_copy(g_ref.at[pl.ds(256 * n, 256), :], buf.at[n], sems.at[n]) for n in range(3)]
    for copy in copies:
        copy.start()
    for n, copy in enumerate(copies):
        rows = pl.ds(256 * n, 256)
        copy.wait()
        wg_ref[rows, :] = buf[n, :, 0:512]
        wu_ref[rows, :] = buf[n, :, 512:1024]
        wd_ref[:, rows] = buf[n, :, 1024:1536].T


def unpack_ffn(g, deps=()):
    return call(unpack_ffn_body, (sds((D, UN), F32), sds((D, UN), F32), sds((UN, D), F32), sds((8, 128), F32)), 0, 0,
                [pltpu.VMEM((3, 256, 1536), F32), pltpu.SemaphoreType.DMA((3,))], 1e6, 1e7, near=False)(far=[g], deps=deps)


def unpack_attn_body(pos_ref, mine, other, wq_ref, wk_ref, wv_ref, wo_ref, one_ref, two_ref, buf):
    core, ja, jb = pos_ref[1], pos_ref[2], pos_ref[3]
    for ref, c, a, b in ((mine, core, ja, jb), (other, 1 - core, jb, ja)):
        for m, sa in enumerate((0, 3, 1, 2)):
            for n, sb in enumerate((0, 3, 1, 2)):
                row = piece_row(c, lax.rem(a + sa, 4), lax.rem(b + sb, 4))
                buf[pl.ds(row, 24), :] = ref[pl.ds(96 * m + 24 * n, 24), :]
    for n, out in enumerate((wq_ref, wk_ref, wv_ref, wo_ref)):
        out[...] = buf[192 * n : 192 * n + 192, :]
    gains = mine[384:392, :] + other[384:392, :]
    one_ref[...] = gains[0].reshape(D)
    two_ref[...] = gains[1].reshape(D)


def unpack_attn(pos, mine, other, deps=()):
    o, g = sds((HW, D), F32), sds((D,), F32)
    return call(unpack_attn_body, (o, o, o, o, g, g), 2, 1, [pltpu.VMEM((D, D), F32)], 1e6, 5e6, near=False)(pos, mine, other, deps=deps)


def split_rows(pos_ref, buf, keep_ref, send_ref):
    core, ja, jb = pos_ref[1], pos_ref[2], pos_ref[3]
    for out, half, a, b in ((keep_ref, core, ja, jb), (send_ref, 1 - core, jb, ja)):
        for sa in range(4):
            for sb in range(4):
                row = piece_row(half, lax.rem(a + sa, 4), lax.rem(b + sb, 4))
                out[pl.ds(96 * sa + 24 * sb, 24), :] = buf[pl.ds(row, 24), :]


def add_split_body(*refs):
    ins, outs = refs[:-4], refs[-4:]
    size = outs[0].shape[0]
    for n, out in enumerate(outs):
        rows = pl.ds(size * n, size)
        if len(ins) == 2:
            out[...] = ins[0][rows, :] + ins[1][rows, :]
        else:
            own, left, right, opposite = ins
            out[...] = (own[rows, :] + opposite[rows, :]) + (left[rows, :] + right[rows, :])


def add_split(*ins, deps=()):
    rows, lanes = ins[0].shape
    o = sds((rows // 4, lanes), F32)
    return call(add_split_body, (o,) * 4, len(ins), 0, (), rows * lanes * 2, rows * lanes * 12, 12)(*ins, deps=deps)


def add_body(own, left, right, opposite, *refs):
    out = refs[-1]
    rows = own.shape[0]
    out[0:rows, :] = (own[...] + opposite[...]) + (left[...] + right[...])
    if len(refs) > 1:
        row = lax.broadcasted_iota(jnp.int32, (8, 1), 0)
        out[rows : rows + 8, :] = jnp.where(row == 0, refs[0][...], jnp.where(row == 1, refs[1][...], 0.0))


def add_four(*ins, deps=()):
    rows, lanes = ins[0].shape
    out = sds((rows + (8 if len(ins) > 4 else 0), lanes), F32)
    return call(add_body, out, len(ins), 0, (), 1e5, 1e6)(*ins, deps=deps)


def rotate(start, far, buf, src, sems):
    copies = [pltpu.make_async_copy(far.at[pl.ds(512 * h, 512), :], src.at[pl.ds(512 * h, 512), :], sems.at[h]) for h in range(2)]
    for copy in copies:
        copy.start()
    for h in range(2):
        copies[h].wait()
        for t in (2 * h, 2 * h + 1):
            buf[pl.ds(256 * t, 256), :] = src[pl.ds(256 * t, 256), :].astype(F32)
    buf[pl.ds(T, 264), :] = buf[pl.ds(0, 264), :]


def turn_body(len_ref, dy_far, out_ref, buf, src, sems):
    start = long_start(len_ref)
    rotate(start, dy_far, buf, src, sems)
    for t in range(4):
        out_ref[pl.ds(256 * t, 256), :] = window(buf, start + 256 * t).astype(BF16)


def turn(lengths, dy, deps=()):
    scratch = [pltpu.VMEM((T + 264, D), F32), pltpu.VMEM((T, D), BF16), pltpu.SemaphoreType.DMA((2,))]
    return call(turn_body, sds((T, D), BF16), 0, 1, scratch, 2e6, 4e6)(lengths, far=[dy], deps=deps)


def front_body(len_ref, gain_ref, wq_ref, wk_ref, wv_ref, x_far,
               xr_out, n1_out, q_out, k_out, v_out, o_out, ot_ref, lse_ref,
               buf, src, keep, heads, sems, out_sems, head_sems):
    start = long_start(len_ref)
    mask = rest_mask(len_ref)
    rotate(start, x_far, buf, src, sems)
    outs = [pltpu.make_async_copy(keep.at[n], out, out_sems.at[n]) for n, out in enumerate((xr_out, n1_out))]
    for t in range(4):
        rows = pl.ds(256 * t, 256)
        x = window(buf, start + 256 * t)
        keep[0, rows, :] = x.astype(BF16)
        r = lax.rsqrt(jnp.mean(x * x, axis=-1, keepdims=True) + EPS)
        keep[1, rows, :] = (x * r * gain_ref[...].reshape(1, D)).astype(BF16)
    for copy in outs:
        copy.start()
    lane = lax.broadcasted_iota(jnp.int32, (1, HW), 1)
    for i in range(2):
        rows = pl.ds(HALF * i, HALF)
        n1 = keep[1, rows, :]
        q = (nt(n1, wq_ref[...]).astype(BF16).astype(F32) * 0.125).astype(BF16)
        k = nt(n1, wk_ref[...]).astype(BF16)
        v = nt(n1, wv_ref[...]).astype(BF16)
        heads[0, rows, :] = q
        heads[1, rows, :] = k
        heads[2, rows, :] = v
        vt = v.T
        parts = []
        for h in range(3):
            s = nt(k, jnp.where((lane >= 64 * h) & (lane < 64 * h + 64), q, jnp.zeros_like(q)))
            if i == 1:
                s = jnp.where(mask, s, -1e30)
            top = jnp.max(s, axis=0, keepdims=True)
            e = jnp.exp(s - top)
            total = jnp.sum(e, axis=0, keepdims=True)
            lse_ref[pl.ds(h, 1), rows] = top + jnp.log(total)
            parts.append(nn(vt[64 * h : 64 * h + 64, :], e.astype(BF16)) * (1.0 / total))
        o = jnp.concatenate(parts, axis=0).astype(BF16)
        ot_ref[:, rows] = o.astype(F32)
        heads[3, rows, :] = o.T
        for n, out in enumerate((q_out, k_out, v_out, o_out)):
            copy = pltpu.make_async_copy(heads.at[n, rows, :], out.at[rows, :], head_sems.at[n, i])
            copy.start()
            outs.append(copy)
    for copy in outs:
        copy.wait()


def front(lengths, tokens, gain, wq, wk, wv, deps=()):
    o, b = sds((T, D), BF16), sds((T, HW), BF16)
    scratch = [pltpu.VMEM((T + 264, D), F32), pltpu.VMEM((T, D), BF16), pltpu.VMEM((2, T, D), BF16), pltpu.VMEM((4, T, HW), BF16),
               pltpu.SemaphoreType.DMA((2,)), pltpu.SemaphoreType.DMA((2,)), pltpu.SemaphoreType.DMA((4, 2))]
    return call(front_body, (o, o, b, b, b, b, sds((HW, T), F32), sds((8, T), F32)), 4, 1, scratch, 4e9, 8e6, 24, out_far=6)(
        lengths, gain, wq, wk, wv, far=[tokens], deps=deps)


def heads_back(i, mask, q, k, v, do, lse):
    lane = lax.broadcasted_iota(jnp.int32, (1, 256), 1)
    head = [(lane >= 64 * h) & (lane < 64 * h + 64) for h in range(3)]
    each = lambda t: jnp.concatenate([jnp.where(m, t, jnp.zeros_like(t)) for m in head], axis=0)
    s_all = nt(each(k), q)
    dp_all = nt(each(v), do)
    kt = k.T
    ps, dss, dqt = [], [], []
    for h in range(3):
        s = s_all[HALF * h : HALF * h + HALF]
        dp = dp_all[HALF * h : HALF * h + HALF]
        if i == 1:
            s = jnp.where(mask, s, -1e30)
        if lse is None:
            e = jnp.exp(s - jnp.max(s, axis=0, keepdims=True))
            p = e * (1.0 / jnp.sum(e, axis=0, keepdims=True))
        else:
            p = jnp.exp(s - lse[h : h + 1, :])
        ds = (p * (dp - jnp.sum(p * dp, axis=0, keepdims=True))).astype(BF16)
        ps.append(p.astype(BF16))
        dss.append(ds)
        dqt.append(nn(kt[64 * h : 64 * h + 64, :], ds))
    dq = (jnp.concatenate(dqt + [jnp.zeros((64, HALF), F32)], axis=0) * 0.125).T
    dv = nn(jnp.concatenate(ps, axis=0), do)
    dk = nn(jnp.concatenate(dss, axis=0), q)

    def pick(t):
        t = [t[HALF * h : HALF * h + HALF] for h in range(3)]
        t = jnp.where(head[0], t[0], jnp.where(head[1], t[1], t[2]))
        return jnp.where(lane < HW, t, 0.0).astype(BF16)

    return dq.astype(BF16), pick(dk), pick(dv)


def padded(t):
    return jnp.concatenate([t, jnp.zeros((t.shape[0], 256 - t.shape[1]), t.dtype)], axis=1)


def own_back_body(len_ref, pos_ref, dhb_ref, wo_ref, q_ref, k_ref, v_ref, lse_ref, n1_ref, o_ref,
                  keep_ref, send_ref, d_ref, g_ref):
    mask = rest_mask(len_ref)
    for i in range(2):
        rows = pl.ds(HALF * i, HALF)
        do = padded(nt(dhb_ref[rows, :], wo_ref[...]).astype(BF16))
        d = heads_back(i, mask, padded(q_ref[rows, :]), padded(k_ref[rows, :]), padded(v_ref[rows, :]), do, lse_ref[:, rows])
        for n in range(3):
            d_ref[rows, 256 * n : 256 * n + 256] = d[n]
    for n in range(3):
        g_ref[192 * n : 192 * n + 192, :] = tn(d_ref[:, 256 * n : 256 * n + 256], n1_ref[...])[0:192]
    g_ref[576:768, :] = tn(o_ref[...], dhb_ref[...])
    split_rows(pos_ref, g_ref, keep_ref, send_ref)


def own_back(lengths, pos, dhb, wo, q, k, v, lse, n1, o, deps=()):
    g = sds((384, D), F32)
    return call(own_back_body, (g, g, sds((T, D), BF16)), 8, 2, [pltpu.VMEM((D, D), F32)], 8e9, 9e6)(
        lengths, pos, dhb, wo, q, k, v, lse, n1, o, deps=deps)


def rest_back_body(r, len_ref, n1_ref, dhb_ref, w_ref, wo_ref, *refs):
    mask = rest_mask(len_ref)
    first, last = r == 0, r == 2
    if first:
        own_d, wq, wk, wv, dn1_ref, d = refs
    elif last:
        dn1_in, x_ref, dn1_ref, gg_ref, d = refs
    else:
        dn1_in, dn1_ref, d = refs
    for i in range(2):
        rows = pl.ds(HALF * i, HALF)
        qkv = nt(n1_ref[rows, :], w_ref[...])
        q = (qkv[:, 0:256].astype(BF16).astype(F32) * 0.125).astype(BF16)
        k = qkv[:, 256:512].astype(BF16)
        v = qkv[:, 512:768].astype(BF16)
        do = nt(dhb_ref[rows, :], wo_ref[...]).astype(BF16)
        for n, t in enumerate(heads_back(i, mask, q, k, v, do, None)):
            d[:, 256 * n : 256 * n + 256] = t
        new = nn(d[...], w_ref[...])
        if first:
            for n, w in enumerate((wq, wk, wv)):
                new = new + nn(own_d[rows, 256 * n : 256 * n + 192], w[...])
        else:
            new = new + dn1_in[rows, :]
        dn1_ref[rows, :] = new
    if last:
        gg = jnp.zeros((8, D), F32)
        for t in range(4):
            rows = pl.ds(256 * t, 256)
            x = x_ref[rows, :].astype(F32)
            r = lax.rsqrt(jnp.mean(x * x, axis=-1, keepdims=True) + EPS)
            gg = gg + jnp.sum((dn1_ref[rows, :] * (x * r)).reshape(32, 8, D), axis=0)
        gg_ref[...] = jnp.broadcast_to(jnp.sum(gg, axis=0, keepdims=True), (8, D))


def rest_back(r, lengths, n1, dhb, w, wo, *more, deps=()):
    o = sds((T, D), F32)
    return call(functools.partial(rest_back_body, r), (o, sds((8, D), F32)) if r == 2 else o, 4 + len(more), 1,
                [pltpu.VMEM((HALF, D), BF16)], 6e9, 1e7)(lengths, n1, dhb, w, wo, *more, deps=deps)


def middle_body(pos_ref, x_ref, oo, oa, ob, oc, od, wo_own, wo_mine, wo_other, gain_ref,
                h_ref, n2_ref, wo_l, wo_r, wo_x, buf):
    core = pos_ref[1]
    for n, ref in enumerate((wo_l, wo_r, wo_x)):
        shard = pl.ds(96 * n, 96)
        buf[pl.ds(pl.multiple_of(core * 96, 32), 96), :] = wo_mine[shard, :]
        buf[pl.ds(pl.multiple_of((1 - core) * 96, 32), 96), :] = wo_other[shard, :]
        ref[0:192, :] = buf[0:192, :].astype(BF16)
        ref[192:256, :] = jnp.zeros((64, D), BF16)
    for t in range(4):
        rows = pl.ds(256 * t, 256)
        h = x_ref[rows, :].astype(F32) + tn(oo[:, rows].astype(BF16), wo_own[...])
        h = h + tn(oa[:, rows].astype(BF16), wo_l[0:192, :])
        h = h + tn(ob[:, rows].astype(BF16), wo_r[0:192, :])
        h = h + tn(oc[:, rows].astype(BF16), wo_x[0:96, :]) + tn(od[:, rows].astype(BF16), wo_x[96:192, :])
        h_ref[rows, :] = h
        f = lax.rsqrt(jnp.mean(h * h, axis=-1, keepdims=True) + EPS)
        n2_ref[rows, :] = (h * f * gain_ref[...].reshape(1, D)).astype(BF16)


def middle(pos, xr, os, wo, wo_mine, wo_other, gain, deps=()):
    w = sds((256, D), BF16)
    return call(middle_body, (sds((T, D), F32), sds((T, D), BF16), w, w, w), 10, 1,
                [pltpu.VMEM((192, D), F32)], 1.2e9, 8e6)(pos, xr, *os, wo, wo_mine, wo_other, gain, deps=deps)


def half_body(pos_ref, wq, wk, wv, out_ref, buf, sems):
    core = pos_ref[1]
    copies = [pltpu.make_async_copy(src, buf.at[pl.ds(192 * n, 192), :], sems.at[n]) for n, src in enumerate((wq, wk, wv))]
    for copy in copies:
        copy.start()
    for copy in copies:
        copy.wait()
    out_ref[...] = buf[pl.ds(pl.multiple_of(core * 288, 32), 288), :].astype(F32)


def qkv_half(pos, wq, wk, wv, deps=()):
    return call(half_body, sds((288, D), F32), 0, 1, [pltpu.VMEM((576, D), BF16), pltpu.SemaphoreType.DMA((3,))], 1e6, 2e6)(
        pos, far=(wq, wk, wv), deps=deps)


def qkv_body(pos_ref, mine, other, *refs):
    core, buf = pos_ref[1], refs[-1]
    for r, out in enumerate(refs[:-1]):
        buf[pl.ds(pl.multiple_of(core * 288, 32), 288), :] = mine[288 * r : 288 * r + 288, :]
        buf[pl.ds(pl.multiple_of((1 - core) * 288, 32), 288), :] = other[288 * r : 288 * r + 288, :]
        for n in range(3):
            out[256 * n : 256 * n + 192, :] = buf[192 * n : 192 * n + 192, :].astype(BF16)
            out[256 * n + 192 : 256 * n + 256, :] = jnp.zeros((64, D), BF16)


def qkv_shard(pos, mine, other, deps=()):
    o = sds((D, D), BF16)
    return call(qkv_body, (o,) * (mine.shape[0] // 288), 2, 1, [pltpu.VMEM((576, D), F32)], 1e6, 3e6)(pos, mine, other, deps=deps)


C1 = 0.7978845608028654
C2 = 0.044715 * C1


def ffn_math(gate, up, dhid):
    u2 = gate * gate
    t = jnp.tanh(gate * (C1 + C2 * u2))
    hp = 0.5 + 0.5 * t
    g = gate * hp
    slope = hp + g * (1.0 - t) * (C1 + 3.0 * C2 * u2)
    return (g * up).astype(BF16), (dhid * up * slope).astype(BF16), (dhid * g).astype(BF16)


def ffn_own_body(pos_ref, n2_ref, dy_ref, wg_ref, wu_ref, wd_ref, f_ref, dn2_ref, keep_ref, send_ref, hid, dgu, g_ref):
    for t in range(4):
        rows = pl.ds(256 * t, 256)
        n2, dy = n2_ref[rows, :], dy_ref[rows, :]
        gate = nn(n2, wg_ref[...])
        up = nn(n2, wu_ref[...])
        dh = nt(dy, wd_ref[...])
        a, b, c = ffn_math(gate, up, dh)
        hid[rows, :] = a
        dgu[rows, 0:512] = b
        dgu[rows, 512:1024] = c
        f_ref[rows, :] = nn(a, wd_ref[...])
        dn2_ref[rows, :] = nt(b, wg_ref[...]) + nt(c, wu_ref[...])
    for t in range(3):
        cols = pl.ds(256 * t, 256)
        g_ref[cols, 0:1024] = tn(n2_ref[:, cols], dgu[...])
        g_ref[cols, 1024:1536] = tn(dy_ref[:, cols], hid[...])
    split_rows(pos_ref, g_ref, keep_ref, send_ref)


def ffn_own(pos, n2, dy, wg, wu, wd, deps=()):
    o, g = sds((T, D), F32), sds((384, 1536), F32)
    return call(ffn_own_body, (o, o, g, g), 5, 1,
                [pltpu.VMEM((T, UN), BF16), pltpu.VMEM((T, 1024), BF16), pltpu.VMEM((D, 1536), F32)], 7.2e9, 1.6e7)(
        pos, n2, dy, wg, wu, wd, deps=deps)


def ffn_rest_body(n2_far, dy_far, w_ref, f_ref, dn2_ref,
                  n2_ref, dy_ref, buf, wb, sems, in_sems):
    def fetch(r, half, slot):
        pieces = pl.ds(16 * half, 16)
        return pltpu.make_async_copy(w_ref.at[pieces, r, :, :], buf.at[slot, pieces], sems.at[slot, half])

    ins = [pltpu.make_async_copy(src, dst, in_sems.at[n]) for n, (src, dst) in enumerate(((n2_far, n2_ref), (dy_far, dy_ref)))]
    fetch(0, 0, 0).start()
    fetch(0, 1, 0).start()
    for copy in ins:
        copy.start()
    f_ref[...] = jnp.zeros_like(f_ref)
    dn2_ref[...] = jnp.zeros_like(dn2_ref)

    def step(r, carry):
        slot = lax.rem(r, 2)

        @pl.when(r < 2)
        def _():
            fetch(r + 1, 0, 1 - slot).start()
            fetch(r + 1, 1, 1 - slot).start()

        for half in range(2):
            fetch(r, half, slot).wait()
            for p in range(16 * half, 16 * half + 16):
                for m in range(3):
                    wb[m, pl.ds(16 * p, 16), :] = buf[slot, p, pl.ds(16 * m, 16), :].astype(BF16)

        @pl.when(r == 0)
        def _():
            for copy in ins:
                copy.wait()

        for t in range(4):
            rows = pl.ds(256 * t, 256)
            n2, dy = n2_ref[rows, :], dy_ref[rows, :]
            a, b, c = ffn_math(nt(n2, wb[0]), nt(n2, wb[1]), nt(dy, wb[2]))
            f_ref[rows, :] = f_ref[rows, :] + nn(a, wb[2])
            dn2_ref[rows, :] = dn2_ref[rows, :] + (nn(b, wb[0]) + nn(c, wb[1]))
        return carry

    lax.fori_loop(0, 3, step, 0)


def ffn_rest(*far, deps=()):
    o = sds((T, D), F32)
    scratch = [pltpu.VMEM((T, D), BF16), pltpu.VMEM((T, D), BF16), pltpu.VMEM((2, 32, 48, D), F32), pltpu.VMEM((3, UN, D), BF16),
               pltpu.SemaphoreType.DMA((2, 2)), pltpu.SemaphoreType.DMA((2,))]
    return call(ffn_rest_body, (o, o), 0, 0, scratch, 12 * T * D * 1536, 2e7, 26)(far=far, deps=deps)


def dh_body(h_ref, own_ref, rest_ref, dy_ref, gain_ref, dh_ref, dhb_ref, gg_ref):
    gg = jnp.zeros((8, D), F32)
    for t in range(4):
        rows = pl.ds(256 * t, 256)
        h = h_ref[rows, :]
        r = lax.rsqrt(jnp.mean(h * h, axis=-1, keepdims=True) + EPS)
        b = h * r
        dn2 = own_ref[rows, :] + rest_ref[rows, :]
        gg = gg + jnp.sum((dn2 * b).reshape(32, 8, D), axis=0)
        e = dn2 * gain_ref[...].reshape(1, D)
        dh = dy_ref[rows, :].astype(F32) + r * (e - b * jnp.mean(e * b, axis=-1, keepdims=True))
        dh_ref[rows, :] = dh
        dhb_ref[rows, :] = dh.astype(BF16)
    gg_ref[...] = jnp.broadcast_to(jnp.sum(gg, axis=0, keepdims=True), (8, D))


def dh_call(h, own, rest, dy, gain, deps=()):
    return call(dh_body, (sds((T, D), F32), sds((T, D), BF16), sds((8, D), F32)), 5, 0, (), 2e7, 1.2e7)(
        h, own, rest, dy, gain, deps=deps)


def unrotate(start, buf, out_ref, dtype):
    back = jnp.where(start > 0, T - start, 0)
    buf[pl.ds(T, 264), :] = buf[pl.ds(0, 264), :]
    for t in range(4):
        out_ref[pl.ds(256 * t, 256), :] = window(buf, back + 256 * t).astype(dtype)


def layer_body(len_ref, h_ref, own_ref, rest_ref, out_ref, tick_ref, buf):
    tick_ref[...] = jnp.zeros_like(tick_ref)
    for t in range(4):
        rows = pl.ds(256 * t, 256)
        buf[rows, :] = h_ref[rows, :] + (own_ref[rows, :] + rest_ref[rows, :])
    unrotate(long_start(len_ref), buf, out_ref, BF16)


def layer_call(lengths, h, own, rest, deps=()):
    return call(layer_body, (sds((T, D), BF16), sds((8, 128), F32)), 3, 1, [pltpu.VMEM((T + 264, D), F32)], 2e6, 8e6, near=False)(lengths, h, own, rest, deps=deps)


def token_body(len_ref, x_ref, dh_ref, dn1_ref, gain_ref, out_ref, tick_ref, buf):
    tick_ref[...] = jnp.zeros_like(tick_ref)
    for t in range(4):
        rows = pl.ds(256 * t, 256)
        x = x_ref[rows, :].astype(F32)
        r = lax.rsqrt(jnp.mean(x * x, axis=-1, keepdims=True) + EPS)
        b = x * r
        e = dn1_ref[rows, :] * gain_ref[...].reshape(1, D)
        buf[rows, :] = dh_ref[rows, :] + r * (e - b * jnp.mean(e * b, axis=-1, keepdims=True))
    unrotate(long_start(len_ref), buf, out_ref, F32)


def token_call(lengths, xr, dh, dn1, gain, deps=()):
    return call(token_body, (sds((T, D), F32), sds((8, 128), F32)), 4, 1, [pltpu.VMEM((T + 264, D), F32)], 2e7, 1.2e7, near=False)(lengths, xr, dh, dn1, gain, deps=deps)


RING = 4


def x_shift(v, step):
    return lax.ppermute(v, "tensor", [(i, (i + step) % RING) for i in range(RING)])


def dp_table(move):
    table = []
    for y in range(RING):
        for z in range(RING):
            for c in range(2):
                to_y, to_z, to_c = move(y, z, c)
                table.append(((y * RING + z) * 2 + c, (to_y % RING * RING + to_z % RING) * 2 + to_c))
    return table


def a_shift(v, step):
    return lax.ppermute(v, "dp", dp_table(lambda y, z, c: (y + step * (1 - c), z + step * c, c)))


def b_shift(v, step):
    return lax.ppermute(v, "dp", dp_table(lambda y, z, c: (y + step * c, z + step * (1 - c), c)))


def core_swap(v):
    return lax.ppermute(v, "dp", dp_table(lambda y, z, c: (y, z, 1 - c)))


def local(
    tokens,
    lengths,
    attn_gain,
    query_weight,
    key_weight,
    value_weight,
    output_weight,
    ffn_gain,
    gate_weight,
    up_weight,
    down_weight,
    cotangent,
):
    x = lax.axis_index("tensor").astype(jnp.int32)
    d = lax.axis_index("dp").astype(jnp.int32)
    core, y, z = d % 2, d // 8, d // 2 % 4
    ja, jb = jnp.where(core == 0, y, z), jnp.where(core == 0, z, y)
    pos = jnp.stack([x, core, ja, jb, d])
    wq, wk, wv = query_weight.T, key_weight.T, value_weight.T
    piece, wo_half = pack(pos, output_weight, gate_weight, up_weight, down_weight)
    pieces = [x_shift(piece, 1), x_shift(piece, -1), x_shift(piece, 2)]
    xr, n1, q, k, v, o, ot, lse = front(lengths, tokens, attn_gain, wq, wk, wv, deps=[piece])
    pieces = cat(*pieces, deps=[lse])
    weights = lax.all_gather(pieces, "dp", axis=0, tiled=True).reshape(32, 3, 48, D)
    near = [x_shift(wo_half, 1), x_shift(wo_half, -1), x_shift(wo_half, 2)]
    dyr = turn(lengths, cotangent, deps=[lse])
    wo_mine = cat(*near)
    oa, ob = x_shift(ot, 1), x_shift(ot, -1)
    wo_other = core_swap(wo_mine)
    oc = x_shift(cat_rows(0, 96, oa, deps=[wo_mine]), 1)
    od = x_shift(cat_rows(96, 96, ob, deps=[wo_mine]), -1)
    h, n2, wo_l, wo_r, wo_x = middle(pos, xr, (ot, oa, ob, oc, od), output_weight, wo_mine, wo_other, ffn_gain)
    f, dn2, keep, send = ffn_own(pos, n2, dyr, gate_weight, up_weight, down_weight)
    ffn_keep, ffn_got = keep, core_swap(send)
    half = qkv_half(pos, wq, wk, wv, deps=[send])
    qkv_l, qkv_r = x_shift(half, 1), x_shift(half, -1)
    f_rest, dn2_rest = ffn_rest(n2, dyr, weights, deps=[half])

    own, right, opposite, left = add_split(ffn_keep, ffn_got, deps=[f_rest])
    ffn_got = (a_shift(left, -1), a_shift(right, 1), a_shift(opposite, 2))
    qkv_near = cat(qkv_l, qkv_r, deps=[f_rest])
    qkv_near_other = core_swap(qkv_near)
    qkv_x = x_shift(half, 2)
    dh, dhb, gain_two = dh_call(h, dn2, dn2_rest, dyr, ffn_gain, deps=[own, qkv_near])
    keep, send, dqkv = own_back(lengths, pos, dhb, output_weight, q, k, v, lse, n1, o)

    ffn_part, right, opposite, left = add_split(own, *ffn_got, deps=[keep])
    ffn_got = (b_shift(left, -1), b_shift(right, 1), b_shift(opposite, 2))
    got = core_swap(send)
    w_l, w_r = qkv_shard(pos, qkv_near, qkv_near_other)
    dn1 = rest_back(0, lengths, n1, dhb, w_l, wo_l, dqkv, wq, wk, wv, deps=[ffn_part, qkv_x])
    ffn_sum = add_four(ffn_part, *ffn_got, deps=[dn1])
    ffn_sums = lax.all_gather(ffn_sum, "dp", axis=0, tiled=True)
    own, right, opposite, left = add_split(keep, got, deps=[dn1])
    got = (a_shift(left, -1), a_shift(right, 1), a_shift(opposite, 2))
    qkv_x_other = core_swap(qkv_x)
    dn1 = rest_back(1, lengths, n1, dhb, w_r, wo_r, dn1, deps=[own])
    own, right, opposite, left = add_split(own, *got, deps=[dn1])
    got = (b_shift(left, -1), b_shift(right, 1), b_shift(opposite, 2))
    (w_x,) = qkv_shard(pos, qkv_x, qkv_x_other)
    dn1, gain_one = rest_back(2, lengths, n1, dhb, w_x, wo_x, dn1, xr, deps=[own])
    own = add_four(own, *got, gain_one, gain_two)
    got = (b_shift(own, 1), b_shift(own, -1), b_shift(own, 2))
    token_grad, tick = token_call(lengths, xr, dh, dn1, attn_gain, deps=[own])
    own = cat_sum(own, *got, deps=[tick])
    got = (a_shift(own, 1), a_shift(own, -1), a_shift(own, 2))
    layer_out, tick = layer_call(lengths, h, f, f_rest, deps=[own])
    gate_grad, up_grad, down_grad, tick2 = unpack_ffn(ffn_sums, deps=[tick])
    own = cat_sum(own, *got, deps=[tick2])
    other = core_swap(own)
    query_grad, key_grad, value_grad, output_grad, attn_gain_grad, ffn_gain_grad = unpack_attn(pos, own, other, deps=[tick])
    return (
        layer_out,
        token_grad,
        attn_gain_grad,
        query_grad.T,
        key_grad.T,
        value_grad.T,
        output_grad,
        ffn_gain_grad,
        gate_grad,
        up_grad,
        down_grad,
    )


def solution(mesh):
    placed = (
        P("dp", None),
        P("dp", None),
        P(),
        P(None, "tensor"),
        P(None, "tensor"),
        P(None, "tensor"),
        P("tensor", None),
        P(),
        P(None, "tensor"),
        P(None, "tensor"),
        P("tensor", None),
        P("dp", None),
    )
    return jax.shard_map(
        local,
        mesh=mesh,
        in_specs=placed,
        out_specs=(
            P("dp", None),
            P("dp", None),
            P(),
            P(None, "tensor"),
            P(None, "tensor"),
            P(None, "tensor"),
            P("tensor", None),
            P(),
            P(None, "tensor"),
            P(None, "tensor"),
            P("tensor", None),
        ),
        check_vma=False,
    )
```

```python
import functools
import jax
import jax.numpy as jnp
from jax import lax
from jax.experimental import pallas as pl
from jax.experimental.pallas import tpu as pltpu
from jax.sharding import PartitionSpec as P

T = 1024
D = 768
HALF = 512
HW = 192
UN = 512
EPS = 1e-06
LIGHT = 20
F32 = jnp.float32
BF16 = jnp.bfloat16
VM = pl.BlockSpec(memory_space=pltpu.VMEM)
SM = pl.BlockSpec(memory_space=pltpu.SMEM)


ANY = pl.BlockSpec(memory_space=pl.ANY)
FAR = pl.BlockSpec(memory_space=pltpu.HBM)


def call(body, out_shape, n_vmem, smem=0, scratch=(), flops=0, bytes_accessed=0, limit=12, alias={}, near=True, out_far=0):
    def run(*args, deps=(), far=()):
        deps = [d for d in deps if d is not None]
        n = smem + n_vmem + len(far)

        def inner(*refs):
            body(*refs[:n], *refs[n + len(deps) :])

        outs = jax.tree.map(lambda s: pltpu.VMEM(s.shape, s.dtype), out_shape) if near else out_shape
        specs = jax.tree.map(lambda _: VM, out_shape)
        if out_far:
            outs = tuple(pltpu.HBM(s.shape, s.dtype) for s in out_shape[:out_far]) + outs[out_far:]
            specs = (FAR,) * out_far + specs[out_far:]
        args = [
            *args[:smem],
            *(pltpu.with_memory_space_constraint(v, pltpu.VMEM) for v in args[smem:]),
            *(pltpu.with_memory_space_constraint(v, pltpu.HBM) for v in far),
        ]
        return pl.pallas_call(
            inner,
            out_shape=outs,
            in_specs=[SM] * smem + [VM] * n_vmem + [FAR] * len(far) + [ANY] * len(deps),
            out_specs=specs,
            scratch_shapes=list(scratch),
            input_output_aliases=alias,
            compiler_params=pltpu.CompilerParams(vmem_limit_bytes=limit << 20),
            cost_estimate=pl.CostEstimate(flops=int(flops) // LIGHT, bytes_accessed=int(bytes_accessed) // LIGHT, transcendentals=0),
        )(*args, *deps)

    return run


def sds(shape, dtype):
    return jax.ShapeDtypeStruct(shape, dtype)


def nn(a, b):
    return jnp.dot(a, b, preferred_element_type=F32)


def nt(a, b):
    return lax.dot_general(a, b, (((1,), (1,)), ((), ())), preferred_element_type=F32)


def tn(a, b):
    return lax.dot_general(a, b, (((0,), (0,)), ((), ())), preferred_element_type=F32)


def long_start(len_ref):
    start, acc = jnp.int32(0), jnp.int32(0)
    for k in range(8):
        n = len_ref[0, k]
        start = jnp.where(n == HALF, acc, start)
        acc = acc + n
    return start


def rest_mask(len_ref):
    start = long_start(len_ref)

    def ids(shape, dim):
        place = lax.broadcasted_iota(jnp.int32, shape, dim) + (HALF + start)
        place = jnp.where(place >= T, place - T, place)
        end, got = jnp.int32(0), jnp.zeros(shape, jnp.int32)
        for k in range(7):
            end = end + len_ref[0, k]
            got = got + (place >= end).astype(jnp.int32)
        return got

    return ids((HALF, 1), 0) == ids((1, HALF), 1)


def window(buf, first):
    first = jnp.where(first >= T, first - T, first)
    base = pl.multiple_of(first // 8 * 8, 8)
    n = first - base
    v = pltpu.roll(buf[pl.ds(base, 264), :].reshape(33, 8, D), lax.rem(8 - n, 8), 1)
    row = lax.broadcasted_iota(jnp.int32, (1, 8, 1), 1)
    return jnp.where(row < 8 - n, v[0:32], v[1:33]).reshape(256, D)


def pack_body(pos_ref, wo_ref, wg_ref, wu_ref, wd_ref, out_ref, half_ref, cols, rows, half, sems):
    core, d = pos_ref[1], pos_ref[4]
    lanes = pl.ds(pl.multiple_of(d // 8 * 128, 128), 128)
    units = pl.ds(pl.multiple_of(d * 16, 16), 16)
    copies = (
        pltpu.make_async_copy(wg_ref.at[:, lanes], cols.at[0], sems.at[0]),
        pltpu.make_async_copy(wu_ref.at[:, lanes], cols.at[1], sems.at[1]),
        pltpu.make_async_copy(wd_ref.at[units, :], rows, sems.at[2]),
        pltpu.make_async_copy(wo_ref.at[pl.ds(pl.multiple_of(core * 96, 32), 96), :], half, sems.at[3]),
    )
    for copy in copies:
        copy.start()
    for copy in copies:
        copy.wait()
    half_ref[...] = half[...].astype(F32)
    lane = lax.broadcasted_iota(jnp.int32, (16, 128), 1)
    row = lax.broadcasted_iota(jnp.int32, (16, 128), 0)
    pick = (lane == row + lax.rem(d, 8) * 16).astype(BF16)
    for m in range(2):
        out_ref[pl.ds(16 * m, 16), :] = nt(pick, cols[m])
    out_ref[32:48, :] = rows[...].astype(F32)


def pack(pos, *weights):
    scratch = [pltpu.VMEM((2, D, 128), BF16), pltpu.VMEM((16, D), BF16), pltpu.VMEM((96, D), BF16), pltpu.SemaphoreType.DMA((4,))]
    return call(pack_body, (sds((48, D), F32), sds((96, D), F32)), 0, 1, scratch, 1e6, 1e6)(pos, far=weights)


def cat_body(*refs):
    out, at = refs[-1], 0
    for ref in refs[:-1]:
        out[pl.ds(at, ref.shape[0]), :] = ref[...]
        at += ref.shape[0]


def cat(*parts, deps=()):
    shape = (sum(p.shape[0] for p in parts), parts[0].shape[1])
    return call(cat_body, sds(shape, F32), len(parts), 0, (), 1e5, 8 * shape[0] * shape[1])(*parts, deps=deps)


def cat_rows_body(first, count, *refs):
    out = refs[-1]
    for n, ref in enumerate(refs[:-1]):
        out[pl.ds(count * n, count), :] = ref[first : first + count, :]


def cat_rows(first, count, *parts, deps=()):
    shape = (count * len(parts), parts[0].shape[1])
    return call(functools.partial(cat_rows_body, first, count), sds(shape, F32), len(parts), 0, (), 1e5, 8 * shape[0] * shape[1])(
        *parts, deps=deps)


def cat_sum_body(size, *refs):
    out, parts = refs[-1], refs[:-1]
    for n, ref in enumerate(parts):
        out[pl.ds(size * n, size), :] = ref[0:size, :]
    own, left, right, opposite = [ref[size : size + 8, :] for ref in parts]
    out[pl.ds(4 * size, 8), :] = (own + opposite) + (left + right)


def cat_sum(*parts, deps=()):
    size = parts[0].shape[0] - 8
    return call(functools.partial(cat_sum_body, size), sds((4 * size + 8, D), F32), 4, 0, (), 1e5, 32e3 * size)(
        *parts, deps=deps)


def piece_row(core, ja, jb):
    return pl.multiple_of(jnp.where(core == 0, ja * 4 + jb, jb * 4 + ja) * 48 + core * 24, 8)


def unpack_ffn_body(g_ref, wg_ref, wu_ref, wd_ref, tick_ref, buf, sems):
    tick_ref[...] = jnp.zeros_like(tick_ref)
    copies = [pltpu.make_async_copy(g_ref.at[pl.ds(256 * n, 256), :], buf.at[n], sems.at[n]) for n in range(3)]
    for copy in copies:
        copy.start()
    for n, copy in enumerate(copies):
        rows = pl.ds(256 * n, 256)
        copy.wait()
        wg_ref[rows, :] = buf[n, :, 0:512]
        wu_ref[rows, :] = buf[n, :, 512:1024]
        wd_ref[:, rows] = buf[n, :, 1024:1536].T


def unpack_ffn(g, deps=()):
    return call(unpack_ffn_body, (sds((D, UN), F32), sds((D, UN), F32), sds((UN, D), F32), sds((8, 128), F32)), 0, 0,
                [pltpu.VMEM((3, 256, 1536), F32), pltpu.SemaphoreType.DMA((3,))], 1e6, 1e7, near=False)(far=[g], deps=deps)


def unpack_attn_body(pos_ref, mine, other, wq_ref, wk_ref, wv_ref, wo_ref, one_ref, two_ref, buf, sems):
    core, ja, jb = pos_ref[1], pos_ref[2], pos_ref[3]
    for ref, c, a, b in ((mine, core, ja, jb), (other, 1 - core, jb, ja)):
        for m, sa in enumerate((0, 3, 1, 2)):
            for n, sb in enumerate((0, 3, 1, 2)):
                row = piece_row(c, lax.rem(a + sa, 4), lax.rem(b + sb, 4))
                buf[pl.ds(row, 24), :] = ref[pl.ds(96 * m + 24 * n, 24), :]
    copies = []
    for n, out in enumerate((wq_ref, wk_ref, wv_ref, wo_ref)):
        copies.append(pltpu.make_async_copy(buf.at[pl.ds(192 * n, 192), :], out, sems.at[n]))
        copies[n].start()
    gains = mine[384:392, :] + other[384:392, :]
    one_ref[...] = gains[0].reshape(D)
    two_ref[...] = gains[1].reshape(D)
    for copy in copies:
        copy.wait()


def unpack_attn(pos, mine, other, deps=()):
    o, g = sds((HW, D), F32), sds((D,), F32)
    return call(unpack_attn_body, (o, o, o, o, g, g), 2, 1, [pltpu.VMEM((D, D), F32), pltpu.SemaphoreType.DMA((4,))], 1e6, 5e6,
                near=False, out_far=4)(pos, mine, other, deps=deps)


def split_rows(pos_ref, buf, keep_ref, send_ref):
    core, ja, jb = pos_ref[1], pos_ref[2], pos_ref[3]
    for out, half, a, b in ((keep_ref, core, ja, jb), (send_ref, 1 - core, jb, ja)):
        for sa in range(4):
            for sb in range(4):
                row = piece_row(half, lax.rem(a + sa, 4), lax.rem(b + sb, 4))
                out[pl.ds(96 * sa + 24 * sb, 24), :] = buf[pl.ds(row, 24), :]


def add_split_body(*refs):
    ins, outs = refs[:-4], refs[-4:]
    size = outs[0].shape[0]
    for n, out in enumerate(outs):
        rows = pl.ds(size * n, size)
        if len(ins) == 2:
            out[...] = ins[0][rows, :] + ins[1][rows, :]
        else:
            own, left, right, opposite = ins
            out[...] = (own[rows, :] + opposite[rows, :]) + (left[rows, :] + right[rows, :])


def add_split(*ins, deps=()):
    rows, lanes = ins[0].shape
    o = sds((rows // 4, lanes), F32)
    return call(add_split_body, (o,) * 4, len(ins), 0, (), rows * lanes * 2, rows * lanes * 12, 12)(*ins, deps=deps)


def add_body(own, left, right, opposite, *refs):
    out = refs[-1]
    rows = own.shape[0]
    out[0:rows, :] = (own[...] + opposite[...]) + (left[...] + right[...])
    if len(refs) > 1:
        row = lax.broadcasted_iota(jnp.int32, (8, 1), 0)
        out[rows : rows + 8, :] = jnp.where(row == 0, refs[0][...], jnp.where(row == 1, refs[1][...], 0.0))


def add_four(*ins, deps=()):
    rows, lanes = ins[0].shape
    out = sds((rows + (8 if len(ins) > 4 else 0), lanes), F32)
    return call(add_body, out, len(ins), 0, (), 1e5, 1e6)(*ins, deps=deps)


def rotate(start, far, buf, src, sems):
    copies = [pltpu.make_async_copy(far.at[pl.ds(512 * h, 512), :], src.at[pl.ds(512 * h, 512), :], sems.at[h]) for h in range(2)]
    for copy in copies:
        copy.start()
    for h in range(2):
        copies[h].wait()
        for t in (2 * h, 2 * h + 1):
            buf[pl.ds(256 * t, 256), :] = src[pl.ds(256 * t, 256), :].astype(F32)
    buf[pl.ds(T, 264), :] = buf[pl.ds(0, 264), :]


def turn_body(len_ref, dy_far, out_ref, buf, src, sems):
    start = long_start(len_ref)
    rotate(start, dy_far, buf, src, sems)
    for t in range(4):
        out_ref[pl.ds(256 * t, 256), :] = window(buf, start + 256 * t).astype(BF16)


def turn(lengths, dy, deps=()):
    scratch = [pltpu.VMEM((T + 264, D), F32), pltpu.VMEM((T, D), BF16), pltpu.SemaphoreType.DMA((2,))]
    return call(turn_body, sds((T, D), BF16), 0, 1, scratch, 2e6, 4e6)(lengths, far=[dy], deps=deps)


def front_body(len_ref, gain_ref, wq_ref, wk_ref, wv_ref, x_far,
               xr_out, n1_out, q_out, k_out, v_out, o_out, ot_ref, lse_ref,
               buf, src, keep, heads, sems, out_sems, head_sems):
    start = long_start(len_ref)
    mask = rest_mask(len_ref)
    rotate(start, x_far, buf, src, sems)
    outs = [pltpu.make_async_copy(keep.at[n], out, out_sems.at[n]) for n, out in enumerate((xr_out, n1_out))]
    for t in range(4):
        rows = pl.ds(256 * t, 256)
        x = window(buf, start + 256 * t)
        keep[0, rows, :] = x.astype(BF16)
        r = lax.rsqrt(jnp.mean(x * x, axis=-1, keepdims=True) + EPS)
        keep[1, rows, :] = (x * r * gain_ref[...].reshape(1, D)).astype(BF16)
    for copy in outs:
        copy.start()
    lane = lax.broadcasted_iota(jnp.int32, (1, HW), 1)
    for i in range(2):
        rows = pl.ds(HALF * i, HALF)
        n1 = keep[1, rows, :]
        q = (nt(n1, wq_ref[...]).astype(BF16).astype(F32) * 0.125).astype(BF16)
        k = nt(n1, wk_ref[...]).astype(BF16)
        v = nt(n1, wv_ref[...]).astype(BF16)
        heads[0, rows, :] = q
        heads[1, rows, :] = k
        heads[2, rows, :] = v
        vt = v.T
        parts = []
        for h in range(3):
            s = nt(k, jnp.where((lane >= 64 * h) & (lane < 64 * h + 64), q, jnp.zeros_like(q)))
            if i == 1:
                s = jnp.where(mask, s, -1e30)
            top = jnp.max(s, axis=0, keepdims=True)
            e = jnp.exp(s - top)
            total = jnp.sum(e, axis=0, keepdims=True)
            lse_ref[pl.ds(h, 1), rows] = top + jnp.log(total)
            parts.append(nn(vt[64 * h : 64 * h + 64, :], e.astype(BF16)) * (1.0 / total))
        o = jnp.concatenate(parts, axis=0).astype(BF16)
        ot_ref[:, rows] = o.astype(F32)
        heads[3, rows, :] = o.T
        for n, out in enumerate((q_out, k_out, v_out, o_out)):
            copy = pltpu.make_async_copy(heads.at[n, rows, :], out.at[rows, :], head_sems.at[n, i])
            copy.start()
            outs.append(copy)
    for copy in outs:
        copy.wait()


def front(lengths, tokens, gain, wq, wk, wv, deps=()):
    o, b = sds((T, D), BF16), sds((T, HW), BF16)
    scratch = [pltpu.VMEM((T + 264, D), F32), pltpu.VMEM((T, D), BF16), pltpu.VMEM((2, T, D), BF16), pltpu.VMEM((4, T, HW), BF16),
               pltpu.SemaphoreType.DMA((2,)), pltpu.SemaphoreType.DMA((2,)), pltpu.SemaphoreType.DMA((4, 2))]
    return call(front_body, (o, o, b, b, b, b, sds((HW, T), F32), sds((8, T), F32)), 4, 1, scratch, 4e9, 8e6, 24, out_far=6)(
        lengths, gain, wq, wk, wv, far=[tokens], deps=deps)


def heads_back(i, mask, q, k, v, do, lse):
    lane = lax.broadcasted_iota(jnp.int32, (1, 256), 1)
    head = [(lane >= 64 * h) & (lane < 64 * h + 64) for h in range(3)]
    each = lambda t: jnp.concatenate([jnp.where(m, t, jnp.zeros_like(t)) for m in head], axis=0)
    s_all = nt(each(k), q)
    dp_all = nt(each(v), do)
    kt = k.T
    ps, dss, dqt = [], [], []
    for h in range(3):
        s = s_all[HALF * h : HALF * h + HALF]
        dp = dp_all[HALF * h : HALF * h + HALF]
        if i == 1:
            s = jnp.where(mask, s, -1e30)
        if lse is None:
            e = jnp.exp(s - jnp.max(s, axis=0, keepdims=True))
            p = e * (1.0 / jnp.sum(e, axis=0, keepdims=True))
        else:
            p = jnp.exp(s - lse[h : h + 1, :])
        ds = (p * (dp - jnp.sum(p * dp, axis=0, keepdims=True))).astype(BF16)
        ps.append(p.astype(BF16))
        dss.append(ds)
        dqt.append(nn(kt[64 * h : 64 * h + 64, :], ds))
    dq = (jnp.concatenate(dqt + [jnp.zeros((64, HALF), F32)], axis=0) * 0.125).T
    dv = nn(jnp.concatenate(ps, axis=0), do)
    dk = nn(jnp.concatenate(dss, axis=0), q)

    def pick(t):
        t = [t[HALF * h : HALF * h + HALF] for h in range(3)]
        t = jnp.where(head[0], t[0], jnp.where(head[1], t[1], t[2]))
        return jnp.where(lane < HW, t, 0.0).astype(BF16)

    return dq.astype(BF16), pick(dk), pick(dv)


def padded(t):
    return jnp.concatenate([t, jnp.zeros((t.shape[0], 256 - t.shape[1]), t.dtype)], axis=1)


def own_back_body(len_ref, pos_ref, dhb_ref, wo_ref, q_ref, k_ref, v_ref, lse_ref, n1_ref, o_ref,
                  keep_ref, send_ref, d_ref, g_ref):
    mask = rest_mask(len_ref)
    for i in range(2):
        rows = pl.ds(HALF * i, HALF)
        do = padded(nt(dhb_ref[rows, :], wo_ref[...]).astype(BF16))
        d = heads_back(i, mask, padded(q_ref[rows, :]), padded(k_ref[rows, :]), padded(v_ref[rows, :]), do, lse_ref[:, rows])
        for n in range(3):
            d_ref[rows, 256 * n : 256 * n + 256] = d[n]
    for n in range(3):
        g_ref[192 * n : 192 * n + 192, :] = tn(d_ref[:, 256 * n : 256 * n + 256], n1_ref[...])[0:192]
    g_ref[576:768, :] = tn(o_ref[...], dhb_ref[...])
    split_rows(pos_ref, g_ref, keep_ref, send_ref)


def own_back(lengths, pos, dhb, wo, q, k, v, lse, n1, o, deps=()):
    g = sds((384, D), F32)
    return call(own_back_body, (g, g, sds((T, D), BF16)), 8, 2, [pltpu.VMEM((D, D), F32)], 8e9, 9e6)(
        lengths, pos, dhb, wo, q, k, v, lse, n1, o, deps=deps)


def rest_back_body(r, len_ref, n1_ref, dhb_ref, w_ref, wo_ref, *refs):
    mask = rest_mask(len_ref)
    first, last = r == 0, r == 2
    if first:
        own_d, wq, wk, wv, dn1_ref, d = refs
    elif last:
        dn1_in, x_ref, dn1_ref, gg_ref, d = refs
    else:
        dn1_in, dn1_ref, d = refs
    for i in range(2):
        rows = pl.ds(HALF * i, HALF)
        qkv = nt(n1_ref[rows, :], w_ref[...])
        q = (qkv[:, 0:256].astype(BF16).astype(F32) * 0.125).astype(BF16)
        k = qkv[:, 256:512].astype(BF16)
        v = qkv[:, 512:768].astype(BF16)
        do = nt(dhb_ref[rows, :], wo_ref[...]).astype(BF16)
        for n, t in enumerate(heads_back(i, mask, q, k, v, do, None)):
            d[:, 256 * n : 256 * n + 256] = t
        new = nn(d[...], w_ref[...])
        if first:
            for n, w in enumerate((wq, wk, wv)):
                new = new + nn(own_d[rows, 256 * n : 256 * n + 192], w[...])
        else:
            new = new + dn1_in[rows, :]
        dn1_ref[rows, :] = new
    if last:
        gg = jnp.zeros((8, D), F32)
        for t in range(4):
            rows = pl.ds(256 * t, 256)
            x = x_ref[rows, :].astype(F32)
            r = lax.rsqrt(jnp.mean(x * x, axis=-1, keepdims=True) + EPS)
            gg = gg + jnp.sum((dn1_ref[rows, :] * (x * r)).reshape(32, 8, D), axis=0)
        gg_ref[...] = jnp.broadcast_to(jnp.sum(gg, axis=0, keepdims=True), (8, D))


def rest_back(r, lengths, n1, dhb, w, wo, *more, deps=()):
    o = sds((T, D), F32)
    return call(functools.partial(rest_back_body, r), (o, sds((8, D), F32)) if r == 2 else o, 4 + len(more), 1,
                [pltpu.VMEM((HALF, D), BF16)], 6e9, 1e7)(lengths, n1, dhb, w, wo, *more, deps=deps)


def middle_body(pos_ref, x_ref, oo, oa, ob, oc, od, wo_own, wo_mine, wo_other, gain_ref,
                h_ref, n2_ref, wo_l, wo_r, wo_x, buf):
    core = pos_ref[1]
    for n, ref in enumerate((wo_l, wo_r, wo_x)):
        shard = pl.ds(96 * n, 96)
        buf[pl.ds(pl.multiple_of(core * 96, 32), 96), :] = wo_mine[shard, :]
        buf[pl.ds(pl.multiple_of((1 - core) * 96, 32), 96), :] = wo_other[shard, :]
        ref[0:192, :] = buf[0:192, :].astype(BF16)
        ref[192:256, :] = jnp.zeros((64, D), BF16)
    for t in range(4):
        rows = pl.ds(256 * t, 256)
        h = x_ref[rows, :].astype(F32) + tn(oo[:, rows].astype(BF16), wo_own[...])
        h = h + tn(oa[:, rows].astype(BF16), wo_l[0:192, :])
        h = h + tn(ob[:, rows].astype(BF16), wo_r[0:192, :])
        h = h + tn(oc[:, rows].astype(BF16), wo_x[0:96, :]) + tn(od[:, rows].astype(BF16), wo_x[96:192, :])
        h_ref[rows, :] = h
        f = lax.rsqrt(jnp.mean(h * h, axis=-1, keepdims=True) + EPS)
        n2_ref[rows, :] = (h * f * gain_ref[...].reshape(1, D)).astype(BF16)


def middle(pos, xr, os, wo, wo_mine, wo_other, gain, deps=()):
    w = sds((256, D), BF16)
    return call(middle_body, (sds((T, D), F32), sds((T, D), BF16), w, w, w), 10, 1,
                [pltpu.VMEM((192, D), F32)], 1.2e9, 8e6)(pos, xr, *os, wo, wo_mine, wo_other, gain, deps=deps)


def half_body(pos_ref, wq, wk, wv, out_ref, buf, sems):
    core = pos_ref[1]
    copies = [pltpu.make_async_copy(src, buf.at[pl.ds(192 * n, 192), :], sems.at[n]) for n, src in enumerate((wq, wk, wv))]
    for copy in copies:
        copy.start()
    for copy in copies:
        copy.wait()
    out_ref[...] = buf[pl.ds(pl.multiple_of(core * 288, 32), 288), :].astype(F32)


def qkv_half(pos, wq, wk, wv, deps=()):
    return call(half_body, sds((288, D), F32), 0, 1, [pltpu.VMEM((576, D), BF16), pltpu.SemaphoreType.DMA((3,))], 1e6, 2e6)(
        pos, far=(wq, wk, wv), deps=deps)


def qkv_body(pos_ref, mine, other, *refs):
    core, buf = pos_ref[1], refs[-1]
    for r, out in enumerate(refs[:-1]):
        buf[pl.ds(pl.multiple_of(core * 288, 32), 288), :] = mine[288 * r : 288 * r + 288, :]
        buf[pl.ds(pl.multiple_of((1 - core) * 288, 32), 288), :] = other[288 * r : 288 * r + 288, :]
        for n in range(3):
            out[256 * n : 256 * n + 192, :] = buf[192 * n : 192 * n + 192, :].astype(BF16)
            out[256 * n + 192 : 256 * n + 256, :] = jnp.zeros((64, D), BF16)


def qkv_shard(pos, mine, other, deps=()):
    o = sds((D, D), BF16)
    return call(qkv_body, (o,) * (mine.shape[0] // 288), 2, 1, [pltpu.VMEM((576, D), F32)], 1e6, 3e6)(pos, mine, other, deps=deps)


C1 = 0.7978845608028654
C2 = 0.044715 * C1


def ffn_math(gate, up, dhid):
    u2 = gate * gate
    t = jnp.tanh(gate * (C1 + C2 * u2))
    hp = 0.5 + 0.5 * t
    g = gate * hp
    slope = hp + g * (1.0 - t) * (C1 + 3.0 * C2 * u2)
    return (g * up).astype(BF16), (dhid * up * slope).astype(BF16), (dhid * g).astype(BF16)


def ffn_own_body(pos_ref, n2_ref, dy_ref, wg_ref, wu_ref, wd_ref, f_ref, dn2_ref, keep_ref, send_ref, hid, dgu, g_ref):
    for t in range(4):
        rows = pl.ds(256 * t, 256)
        n2, dy = n2_ref[rows, :], dy_ref[rows, :]
        gate = nn(n2, wg_ref[...])
        up = nn(n2, wu_ref[...])
        dh = nt(dy, wd_ref[...])
        a, b, c = ffn_math(gate, up, dh)
        hid[rows, :] = a
        dgu[rows, 0:512] = b
        dgu[rows, 512:1024] = c
        f_ref[rows, :] = nn(a, wd_ref[...])
        dn2_ref[rows, :] = nt(b, wg_ref[...]) + nt(c, wu_ref[...])
    for t in range(3):
        cols = pl.ds(256 * t, 256)
        g_ref[cols, 0:1024] = tn(n2_ref[:, cols], dgu[...])
        g_ref[cols, 1024:1536] = tn(dy_ref[:, cols], hid[...])
    split_rows(pos_ref, g_ref, keep_ref, send_ref)


def ffn_own(pos, n2, dy, wg, wu, wd, deps=()):
    o, g = sds((T, D), F32), sds((384, 1536), F32)
    return call(ffn_own_body, (o, o, g, g), 5, 1,
                [pltpu.VMEM((T, UN), BF16), pltpu.VMEM((T, 1024), BF16), pltpu.VMEM((D, 1536), F32)], 7.2e9, 1.6e7)(
        pos, n2, dy, wg, wu, wd, deps=deps)


def ffn_rest_body(n2_far, dy_far, w_ref, f_ref, dn2_ref,
                  n2_ref, dy_ref, buf, wb, sems, in_sems):
    def fetch(r, half, slot):
        pieces = pl.ds(16 * half, 16)
        return pltpu.make_async_copy(w_ref.at[pieces, r, :, :], buf.at[slot, pieces], sems.at[slot, half])

    ins = [pltpu.make_async_copy(src, dst, in_sems.at[n]) for n, (src, dst) in enumerate(((n2_far, n2_ref), (dy_far, dy_ref)))]
    fetch(0, 0, 0).start()
    fetch(0, 1, 0).start()
    for copy in ins:
        copy.start()
    f_ref[...] = jnp.zeros_like(f_ref)
    dn2_ref[...] = jnp.zeros_like(dn2_ref)

    def step(r, carry):
        slot = lax.rem(r, 2)

        @pl.when(r < 2)
        def _():
            fetch(r + 1, 0, 1 - slot).start()
            fetch(r + 1, 1, 1 - slot).start()

        for half in range(2):
            fetch(r, half, slot).wait()
            for p in range(16 * half, 16 * half + 16):
                for m in range(3):
                    wb[m, pl.ds(16 * p, 16), :] = buf[slot, p, pl.ds(16 * m, 16), :].astype(BF16)

        @pl.when(r == 0)
        def _():
            for copy in ins:
                copy.wait()

        for t in range(4):
            rows = pl.ds(256 * t, 256)
            n2, dy = n2_ref[rows, :], dy_ref[rows, :]
            a, b, c = ffn_math(nt(n2, wb[0]), nt(n2, wb[1]), nt(dy, wb[2]))
            f_ref[rows, :] = f_ref[rows, :] + nn(a, wb[2])
            dn2_ref[rows, :] = dn2_ref[rows, :] + (nn(b, wb[0]) + nn(c, wb[1]))
        return carry

    lax.fori_loop(0, 3, step, 0)


def ffn_rest(*far, deps=()):
    o = sds((T, D), F32)
    scratch = [pltpu.VMEM((T, D), BF16), pltpu.VMEM((T, D), BF16), pltpu.VMEM((2, 32, 48, D), F32), pltpu.VMEM((3, UN, D), BF16),
               pltpu.SemaphoreType.DMA((2, 2)), pltpu.SemaphoreType.DMA((2,))]
    return call(ffn_rest_body, (o, o), 0, 0, scratch, 12 * T * D * 1536, 2e7, 26)(far=far, deps=deps)


def dh_body(h_ref, own_ref, rest_ref, dy_ref, gain_ref, dh_ref, dhb_ref, gg_ref):
    gg = jnp.zeros((8, D), F32)
    for t in range(4):
        rows = pl.ds(256 * t, 256)
        h = h_ref[rows, :]
        r = lax.rsqrt(jnp.mean(h * h, axis=-1, keepdims=True) + EPS)
        b = h * r
        dn2 = own_ref[rows, :] + rest_ref[rows, :]
        gg = gg + jnp.sum((dn2 * b).reshape(32, 8, D), axis=0)
        e = dn2 * gain_ref[...].reshape(1, D)
        dh = dy_ref[rows, :].astype(F32) + r * (e - b * jnp.mean(e * b, axis=-1, keepdims=True))
        dh_ref[rows, :] = dh
        dhb_ref[rows, :] = dh.astype(BF16)
    gg_ref[...] = jnp.broadcast_to(jnp.sum(gg, axis=0, keepdims=True), (8, D))


def dh_call(h, own, rest, dy, gain, deps=()):
    return call(dh_body, (sds((T, D), F32), sds((T, D), BF16), sds((8, D), F32)), 5, 0, (), 2e7, 1.2e7)(
        h, own, rest, dy, gain, deps=deps)


def unrotate(start, buf, out_ref, dtype):
    back = jnp.where(start > 0, T - start, 0)
    buf[pl.ds(T, 264), :] = buf[pl.ds(0, 264), :]
    for t in range(4):
        out_ref[pl.ds(256 * t, 256), :] = window(buf, back + 256 * t).astype(dtype)


def layer_body(len_ref, h_ref, own_ref, rest_ref, out_ref, tick_ref, buf):
    tick_ref[...] = jnp.zeros_like(tick_ref)
    for t in range(4):
        rows = pl.ds(256 * t, 256)
        buf[rows, :] = h_ref[rows, :] + (own_ref[rows, :] + rest_ref[rows, :])
    unrotate(long_start(len_ref), buf, out_ref, BF16)


def layer_call(lengths, h, own, rest, deps=()):
    return call(layer_body, (sds((T, D), BF16), sds((8, 128), F32)), 3, 1, [pltpu.VMEM((T + 264, D), F32)], 2e6, 8e6, near=False)(lengths, h, own, rest, deps=deps)


def token_body(len_ref, x_ref, dh_ref, dn1_ref, gain_ref, out_ref, tick_ref, buf):
    tick_ref[...] = jnp.zeros_like(tick_ref)
    for t in range(4):
        rows = pl.ds(256 * t, 256)
        x = x_ref[rows, :].astype(F32)
        r = lax.rsqrt(jnp.mean(x * x, axis=-1, keepdims=True) + EPS)
        b = x * r
        e = dn1_ref[rows, :] * gain_ref[...].reshape(1, D)
        buf[rows, :] = dh_ref[rows, :] + r * (e - b * jnp.mean(e * b, axis=-1, keepdims=True))
    unrotate(long_start(len_ref), buf, out_ref, F32)


def token_call(lengths, xr, dh, dn1, gain, deps=()):
    return call(token_body, (sds((T, D), F32), sds((8, 128), F32)), 4, 1, [pltpu.VMEM((T + 264, D), F32)], 2e7, 1.2e7, near=False)(lengths, xr, dh, dn1, gain, deps=deps)


RING = 4


def x_shift(v, step):
    return lax.ppermute(v, "tensor", [(i, (i + step) % RING) for i in range(RING)])


def dp_table(move):
    table = []
    for y in range(RING):
        for z in range(RING):
            for c in range(2):
                to_y, to_z, to_c = move(y, z, c)
                table.append(((y * RING + z) * 2 + c, (to_y % RING * RING + to_z % RING) * 2 + to_c))
    return table


def a_shift(v, step):
    return lax.ppermute(v, "dp", dp_table(lambda y, z, c: (y + step * (1 - c), z + step * c, c)))


def b_shift(v, step):
    return lax.ppermute(v, "dp", dp_table(lambda y, z, c: (y + step * c, z + step * (1 - c), c)))


def core_swap(v):
    return lax.ppermute(v, "dp", dp_table(lambda y, z, c: (y, z, 1 - c)))


def local(
    tokens,
    lengths,
    attn_gain,
    query_weight,
    key_weight,
    value_weight,
    output_weight,
    ffn_gain,
    gate_weight,
    up_weight,
    down_weight,
    cotangent,
):
    x = lax.axis_index("tensor").astype(jnp.int32)
    d = lax.axis_index("dp").astype(jnp.int32)
    core, y, z = d % 2, d // 8, d // 2 % 4
    ja, jb = jnp.where(core == 0, y, z), jnp.where(core == 0, z, y)
    pos = jnp.stack([x, core, ja, jb, d])
    wq, wk, wv = query_weight.T, key_weight.T, value_weight.T
    piece, wo_half = pack(pos, output_weight, gate_weight, up_weight, down_weight)
    pieces = [x_shift(piece, 1), x_shift(piece, -1), x_shift(piece, 2)]
    xr, n1, q, k, v, o, ot, lse = front(lengths, tokens, attn_gain, wq, wk, wv, deps=[piece])
    pieces = cat(*pieces, deps=[lse])
    weights = lax.all_gather(pieces, "dp", axis=0, tiled=True).reshape(32, 3, 48, D)
    near = [x_shift(wo_half, 1), x_shift(wo_half, -1), x_shift(wo_half, 2)]
    dyr = turn(lengths, cotangent, deps=[lse])
    wo_mine = cat(*near)
    oa, ob = x_shift(ot, 1), x_shift(ot, -1)
    wo_other = core_swap(wo_mine)
    oc = x_shift(cat_rows(0, 96, oa, deps=[wo_mine]), 1)
    od = x_shift(cat_rows(96, 96, ob, deps=[wo_mine]), -1)
    h, n2, wo_l, wo_r, wo_x = middle(pos, xr, (ot, oa, ob, oc, od), output_weight, wo_mine, wo_other, ffn_gain)
    f, dn2, keep, send = ffn_own(pos, n2, dyr, gate_weight, up_weight, down_weight)
    ffn_keep, ffn_got = keep, core_swap(send)
    half = qkv_half(pos, wq, wk, wv, deps=[send])
    qkv_l, qkv_r = x_shift(half, 1), x_shift(half, -1)
    f_rest, dn2_rest = ffn_rest(n2, dyr, weights, deps=[half])

    own, right, opposite, left = add_split(ffn_keep, ffn_got, deps=[f_rest])
    ffn_got = (a_shift(left, -1), a_shift(right, 1), a_shift(opposite, 2))
    qkv_near = cat(qkv_l, qkv_r, deps=[f_rest])
    qkv_near_other = core_swap(qkv_near)
    qkv_x = x_shift(half, 2)
    dh, dhb, gain_two = dh_call(h, dn2, dn2_rest, dyr, ffn_gain, deps=[own, qkv_near])
    keep, send, dqkv = own_back(lengths, pos, dhb, output_weight, q, k, v, lse, n1, o)

    ffn_part, right, opposite, left = add_split(own, *ffn_got, deps=[keep])
    ffn_got = (b_shift(left, -1), b_shift(right, 1), b_shift(opposite, 2))
    got = core_swap(send)
    w_l, w_r = qkv_shard(pos, qkv_near, qkv_near_other)
    dn1 = rest_back(0, lengths, n1, dhb, w_l, wo_l, dqkv, wq, wk, wv, deps=[ffn_part, qkv_x])
    ffn_sum = add_four(ffn_part, *ffn_got, deps=[dn1])
    ffn_sums = lax.all_gather(ffn_sum, "dp", axis=0, tiled=True)
    own, right, opposite, left = add_split(keep, got, deps=[dn1])
    got = (a_shift(left, -1), a_shift(right, 1), a_shift(opposite, 2))
    qkv_x_other = core_swap(qkv_x)
    dn1 = rest_back(1, lengths, n1, dhb, w_r, wo_r, dn1, deps=[own])
    own, right, opposite, left = add_split(own, *got, deps=[dn1])
    got = (b_shift(left, -1), b_shift(right, 1), b_shift(opposite, 2))
    (w_x,) = qkv_shard(pos, qkv_x, qkv_x_other)
    dn1, gain_one = rest_back(2, lengths, n1, dhb, w_x, wo_x, dn1, xr, deps=[own])
    own = add_four(own, *got, gain_one, gain_two)
    got = (b_shift(own, 1), b_shift(own, -1), b_shift(own, 2))
    token_grad, tick = token_call(lengths, xr, dh, dn1, attn_gain, deps=[own])
    own = cat_sum(own, *got, deps=[tick])
    got = (a_shift(own, 1), a_shift(own, -1), a_shift(own, 2))
    layer_out, tick = layer_call(lengths, h, f, f_rest, deps=[own])
    gate_grad, up_grad, down_grad, tick2 = unpack_ffn(ffn_sums, deps=[tick])
    own = cat_sum(own, *got, deps=[tick2])
    other = core_swap(own)
    query_grad, key_grad, value_grad, output_grad, attn_gain_grad, ffn_gain_grad = unpack_attn(pos, own, other, deps=[tick])
    return (
        layer_out,
        token_grad,
        attn_gain_grad,
        query_grad.T,
        key_grad.T,
        value_grad.T,
        output_grad,
        ffn_gain_grad,
        gate_grad,
        up_grad,
        down_grad,
    )


def solution(mesh):
    placed = (
        P("dp", None),
        P("dp", None),
        P(),
        P(None, "tensor"),
        P(None, "tensor"),
        P(None, "tensor"),
        P("tensor", None),
        P(),
        P(None, "tensor"),
        P(None, "tensor"),
        P("tensor", None),
        P("dp", None),
    )
    return jax.shard_map(
        local,
        mesh=mesh,
        in_specs=placed,
        out_specs=(
            P("dp", None),
            P("dp", None),
            P(),
            P(None, "tensor"),
            P(None, "tensor"),
            P(None, "tensor"),
            P("tensor", None),
            P(),
            P(None, "tensor"),
            P(None, "tensor"),
            P("tensor", None),
        ),
        check_vma=False,
    )
```
